32 devices in a mesh: scen: 1, grp: 16 (over z, y, core), pen: 2 (over x).
Axes of the slice: x: 2, y: 2, z: 4, core: 2. Of those that a mesh axis runs over, the one named last changes fastest.
Arguments:
- prec_state: float32 [1, 128, 128, 128], P('scen', 'grp', 'pen'), may hold values from -6 to 6
- farm_state: float32 [1, 128, 128, 256], P('scen', 'grp', 'pen'), may hold values from -6 to 6
- yaw_angles: float32 [2, 64], replicated, may hold values from -0.6 to 0.6
- plane_source: int32 [16], replicated, may hold values from 0 to 127, as said below
- cell_index: int32 [16, 2, 128], P('grp', 'pen'), may hold values from 0 to 131071, as said below
- cell_turbine: int32 [16, 2, 128], P('grp', 'pen'), may hold values from 0 to 63
Outputs:
- prec_final: float32 [1, 128, 128, 128], P('scen', 'grp', 'pen')
- farm_final: float32 [1, 128, 128, 256], P('scen', 'grp', 'pen')
- sensitivity: float32 [1, 128, 128, 256], P('scen', 'grp', 'pen')
- yaw_grad: float32 [2, 64], replicated
The draws below stay inside these ranges and needn't reach their ends.
Inputs may be any that keep to these rules, and one draw needn't show every extreme that they name: `plane_source`: 16 distinct planes; plane 0 and plane 128 - 1 are always among them. `cell_index`: distinct within each farm device; index (row * 64 + z) * 256 + x of that device's block.
All inputs are finite; a program needn't handle non-finite values.
Results may differ from the reference program's by a relative error of at most 0.00012.
Values sent between devices are 32-bit elements; how exact they have to be, the bound alone decides.
A program may use at most 64 MiB of HBM per device.

```python
import jax
import jax.numpy as jnp
from jax import lax

YD = 8
FZ = 128
FX = 256
NF = 16
CELLS = 128
TURB = 64
STEPS = 2
ZD = 64
FY = 128
PX = 128
SCEN = 1
N_GRP = 16
N_PEN = 2


def draw_plane_source(key, part):
    middle = jax.random.permutation(key, PX - 2)[:NF - 2].astype(jnp.int32) + 1
    ends = jnp.array([0, PX - 1], dtype=jnp.int32)
    joined = jnp.concatenate([ends, middle])
    order = jax.random.permutation(jax.random.fold_in(key, 7), NF)
    return joined[order].astype(jnp.int32)


def draw_cell_index(key, part):
    keys = jax.random.split(key, N_GRP * N_PEN)

    def single(one_key):
        return jax.random.permutation(one_key, YD * ZD * FX)[:CELLS].astype(jnp.int32)
    chosen = jax.vmap(single)(keys)
    return chosen.reshape(N_GRP, N_PEN, CELLS).astype(jnp.int32)


def plant(entries, own_key, smallest, top_value):
    longest = entries.shape.index(max(entries.shape))
    spots = []
    for shift in (0, 1):
        where = [jax.random.randint(jax.random.fold_in(own_key, axis), (), 0, length) for axis, length in enumerate(entries.shape)]
        where[longest] = (where[longest] + shift) % entries.shape[longest]
        spots.append(tuple(where))
    return entries.at[spots[0]].set(smallest).at[spots[1]].set(top_value)


def shard_levels(key, shape, shards, smallest, top_value):
    loudness = 1.0
    for position, parts in shards:
        draws = jax.random.uniform(jax.random.fold_in(jax.random.fold_in(key, 6), position), (parts,), jnp.float32, smallest / len(shards), top_value / len(shards))
        loudness = loudness * jnp.repeat(jnp.exp(draws), shape[position] // parts).reshape((-1,) + (1,) * (len(shape) - 1 - position))
    return loudness


def bell_draw(own_key, shape, width, most, cuts=(), kind=jnp.bfloat16):
    loudness = shard_levels(own_key, shape, cuts, -0.22, 0.18) if cuts else 1.0
    values = jax.random.normal(own_key, shape, jnp.float32) * width * loudness
    return jnp.minimum(jnp.maximum(values, -most), most).astype(kind)


def setup_inputs(seed: int = 0) -> dict:
    key_of = jax.random.split(jax.random.key(seed), 7)
    prec_state = bell_draw(key_of[0], (SCEN, PX, FZ, FY), 1.0, 6.0, ((1, 16), (2, 2)), jnp.float32)
    farm_state = bell_draw(key_of[1], (SCEN, FY, FZ, FX), 1.0, 6.0, ((1, 16), (2, 2)), jnp.float32)
    yaw_angles = jnp.clip(jax.random.uniform(key_of[2], (STEPS, TURB), jnp.float32, -0.6, 0.6), -0.6, 0.6)
    plane_source = draw_plane_source(jax.random.fold_in(key_of[6], 71), 0)
    cell_index = draw_cell_index(jax.random.fold_in(key_of[6], 71), 0)
    cell_turbine = plant(jax.random.randint(key_of[5], (N_GRP, N_PEN, CELLS), 0, TURB), jax.random.fold_in(key_of[5], 1), 0, TURB - 1).astype(jnp.int32)
    return dict(prec_state=prec_state, farm_state=farm_state, yaw_angles=yaw_angles, plane_source=plane_source, cell_index=cell_index, cell_turbine=cell_turbine)


COURANT = 0.3
VISC_BASE = 0.03
VISC_SLOPE = 0.03
SLOPE_EPS = 0.01
FORCE_GAIN = 0.3
POWER_GAIN = 0.002

def precursor_step(field):
    upper_x = jnp.roll(field, -1, 0)
    lower_x = jnp.roll(field, 1, 0)
    upper_z = jnp.roll(field, -1, 1)
    lower_z = jnp.roll(field, 1, 1)
    upper_y = jnp.roll(field, -1, 2)
    lower_y = jnp.roll(field, 1, 2)
    slope_x = 0.5 * (upper_x - lower_x)
    slope_y = 0.5 * (upper_y - lower_y)
    slope_z = 0.5 * (upper_z - lower_z)
    viscosity = VISC_BASE + VISC_SLOPE * jnp.sqrt(slope_x * slope_x + slope_y * slope_y + slope_z * slope_z + SLOPE_EPS)
    laplacian = upper_x + lower_x + upper_y + lower_y + upper_z + lower_z - 6.0 * field
    return field - COURANT * (field - lower_x) + viscosity * laplacian

def farm_core(field, angles, flat_cells, turbine_ids):
    padded = jnp.pad(field, ((1, 1), (1, 1), (0, 0)))
    upper_y = padded[2:, 1:-1]
    lower_y = padded[:-2, 1:-1]
    upper_z = padded[1:-1, 2:]
    lower_z = padded[1:-1, :-2]
    behind = jnp.concatenate([field[..., :1], field[..., :-1]], axis=-1)
    slope_y = 0.5 * (upper_y - lower_y)
    slope_z = 0.5 * (upper_z - lower_z)
    viscosity = VISC_BASE + VISC_SLOPE * jnp.sqrt(slope_y * slope_y + slope_z * slope_z + SLOPE_EPS)
    laplacian = upper_y + lower_y + upper_z + lower_z - 4.0 * field
    moved = field - COURANT * (field - behind) + viscosity * laplacian
    one_hot = (turbine_ids[:, None] == jnp.arange(TURB, dtype=jnp.int32)[None, :]).astype(jnp.float32)
    cosine = jnp.cos(angles)
    square_factor = jnp.dot(one_hot, cosine * cosine, precision=lax.Precision.HIGHEST)
    cube_factor = jnp.dot(one_hot, cosine * cosine * cosine, precision=lax.Precision.HIGHEST)
    cell_values = field.reshape(-1)[flat_cells]
    flattened = moved.reshape(-1).at[flat_cells].add(-FORCE_GAIN * square_factor * cell_values)
    advanced = flattened.reshape(field.shape)
    at_cells = flattened[flat_cells]
    power_sum = POWER_GAIN * jnp.sum(cube_factor * at_cells * at_cells)
    return (advanced, power_sum)

def reference(prec_state, farm_state, yaw_angles, plane_source, cell_index, cell_turbine):
    rows = cell_index // (ZD * FX)
    depth = cell_index // FX % ZD
    along = cell_index % FX
    lateral = jnp.arange(N_GRP, dtype=jnp.int32)[:, None, None] * YD + rows
    vertical = jnp.arange(N_PEN, dtype=jnp.int32)[None, :, None] * ZD + depth
    flat_cells = ((lateral * FZ + vertical) * FX + along).reshape(-1).astype(jnp.int32)
    turbine_ids = cell_turbine.reshape(-1)

    def scenario(pair):
        precursor, farm_start = pair
        inlets = []
        for step in range(STEPS):
            precursor = precursor_step(precursor)
            inlets.append(jnp.transpose(precursor[plane_source], (2, 1, 0)))

        def objective(farm_now, angles):
            total = jnp.float32(0.0)
            for step in range(STEPS):
                fringed = jnp.concatenate([inlets[step], farm_now[..., NF:]], axis=-1)
                farm_now, power_sum = farm_core(fringed, angles[step], flat_cells, turbine_ids)
                total = total + power_sum
            return (total, farm_now)
        total, backward, farm_end = jax.vjp(objective, farm_start, yaw_angles, has_aux=True)
        sens, angle_grad = backward(jnp.ones_like(total))
        return (precursor, farm_end, sens, angle_grad)
    prec_final, farm_final, sensitivity, angle_grads = lax.map(scenario, (prec_state, farm_state))
    return (prec_final, farm_final, sensitivity, lax.optimization_barrier(jnp.sum(angle_grads, axis=0)))
```

```python
import functools

import jax
import jax.numpy as jnp
from jax import lax
from jax.experimental import pallas as pl
from jax.experimental.pallas import tpu as pltpu
from jax.sharding import PartitionSpec as P

NF = 16
TURB = 64
COURANT = 0.3
VISC_BASE = 0.03
VISC_SLOPE = 0.03
SLOPE_EPS = 0.01
FORCE_GAIN = 0.3
POWER_GAIN = 0.002

MESH = pl.DeviceIdType.MESH
VMEM = pl.BlockSpec(memory_space=pltpu.VMEM)
HBM = pl.BlockSpec(memory_space=pltpu.HBM)
SMEM = pl.BlockSpec(memory_space=pltpu.SMEM)
F32 = jnp.float32
BF16 = jnp.bfloat16


def split2(b):
    high = b.astype(BF16)
    return high, (b - high.astype(F32)).astype(BF16)


def dot(a, b):
    return jnp.dot(a, b, preferred_element_type=F32)


def advance_plane(centre, upper_a, lower_a, upper_z, lower_z, upper_l, lower_l, lower_x):
    slope_a = 0.5 * (upper_a - lower_a)
    slope_l = 0.5 * (upper_l - lower_l)
    slope_z = 0.5 * (upper_z - lower_z)
    viscosity = VISC_BASE + VISC_SLOPE * jnp.sqrt(
        slope_a * slope_a + slope_l * slope_l + slope_z * slope_z + SLOPE_EPS
    )
    laplacian = upper_a + lower_a + upper_l + lower_l + upper_z + lower_z - 6.0 * centre
    return centre - COURANT * (centre - lower_x) + viscosity * laplacian


def periodic_row(src, i, lead_is_x):
    centre = src[i]
    depth, lanes = centre.shape
    upper_l = pltpu.roll(centre, lanes - 1, 1)
    lower_l = pltpu.roll(centre, 1, 1)
    upper_z = pltpu.roll(centre, depth - 1, 0)
    lower_z = pltpu.roll(centre, 1, 0)
    upper_a = src[i + 1]
    lower_a = src[i - 1]
    lower_x = lower_a if lead_is_x else lower_l
    return advance_plane(centre, upper_a, lower_a, upper_z, lower_z, upper_l, lower_l, lower_x)


def farm_kernel(
    sizes, v_in, u_in, index_in, turbine_in, yaw_in, ps_ref,
    prec_ref, farm_ref, sens_ref, grad_ref,
    fp_ref, vp_ref, w_ref, cb_ref,
    v_ref, u_ref, cell_ref, index_ref, turbine_ref, yaw_ref, in_sem,
    vedge, uedge, bsend, rbody, wedge,
    v1, vw1, vw2, c0, c1, w0, w1, u1, u2, lam, nu, ry, rz, am, bm, gc0, gc1, total_a, total_b,
    near_send, near_recv, far_send, far_recv, edge_send, edge_recv, a_send, a_recv, b_send, b_recv,
):
    g = lax.axis_index("grp")
    p = lax.axis_index("pen")
    q = 1 - p
    ns, n, m = sizes
    up = lax.rem(g + 1, n)
    down = lax.rem(g + n - 1, n)
    planes, zd, fy = v_ref.shape
    rows, _, fx = u_ref.shape
    depth = zd + 8
    px = w_ref.shape[2]
    scen = lax.axis_index("scen")

    barrier = pltpu.get_barrier_semaphore()

    def peer(d):
        other = lax.rem(g * m + p + d, n * m)
        return {"grp": other // m, "pen": lax.rem(other, m)}

    def line(d):
        return {"scen": lax.rem(scen + d, ns), "grp": g, "pen": p}

    def greet(make):
        def run(d, carry):
            pl.semaphore_signal(barrier, inc=1, device_id=make(d), device_id_type=MESH)
            return carry

        return run

    lax.fori_loop(1, n * m, greet(peer), 0)
    lax.fori_loop(1, ns, greet(line), 0)

    loads = [
        pltpu.make_async_copy(src, dst, in_sem.at[i])
        for i, (src, dst) in enumerate((
            (v_in, v_ref), (index_in, index_ref), (turbine_in, turbine_ref), (u_in, u_ref), (yaw_in, yaw_ref),
        ))
    ]
    for load in loads:
        load.start()
    loads[0].wait()

    vedge[:, 0:4] = v_ref[:, 0:4]
    vedge[:, 4:8] = v_ref[:, zd - 4 : zd]
    for x in range(planes):
        plane = v_ref[x]
        both = jnp.concatenate(
            [pltpu.roll(plane, 4, 1), pltpu.roll(plane, fy - 4, 1)], axis=0
        )
        bsend[:, x, :] = both.T

    for load in loads[1:]:
        load.wait()
    uedge[:, 0:4] = u_ref[:, 0:4]
    uedge[:, 4:8] = u_ref[:, zd - 4 : zd]
    cell_ref[...] = jnp.zeros_like(cell_ref)
    cell_ref[0:1] = index_ref[...]
    cell_ref[1:2] = turbine_ref[...]

    pl.semaphore_wait(barrier, (n * m - 1) + (ns - 1))

    def far(d):
        target = lax.rem(g + d, n)
        return pltpu.make_async_remote_copy(
            src_ref=bsend.at[pl.ds(target * 8, 8)],
            dst_ref=rbody.at[:, pl.ds(g * planes, planes)],
            send_sem=far_send.at[d],
            recv_sem=far_recv.at[d],
            device_id={"grp": target, "pen": p},
            device_id_type=MESH,
        )

    def far_start(d, carry):
        far(d).start()
        return carry


    moves = [
        (u_ref.at[rows - 4 : rows], fp_ref.at[0:4, 0:zd], up, p),
        (u_ref.at[0:4], fp_ref.at[rows + 4 : rows + 8, 0:zd], down, p),
        (uedge, fp_ref.at[4 : rows + 4, zd : zd + 8], g, q),
        (uedge.at[rows - 4 : rows], fp_ref.at[0:4, zd : zd + 8], up, q),
        (uedge.at[0:4], fp_ref.at[rows + 4 : rows + 8, zd : zd + 8], down, q),
        (v_ref.at[planes - 2 : planes], vp_ref.at[0:2, 0:zd], up, p),
        (v_ref.at[0:2], vp_ref.at[planes + 2 : planes + 4, 0:zd], down, p),
        (vedge, vp_ref.at[2 : planes + 2, zd : zd + 8], g, q),
        (vedge.at[planes - 2 : planes], vp_ref.at[0:2, zd : zd + 8], up, q),
        (vedge.at[0:2], vp_ref.at[planes + 2 : planes + 4, zd : zd + 8], down, q),
        (cell_ref, cb_ref.at[1], up, p),
        (cell_ref, cb_ref.at[2], down, p),
        (cell_ref, cb_ref.at[3], g, q),
        (cell_ref, cb_ref.at[4], up, q),
        (cell_ref, cb_ref.at[5], down, q),
    ]
    copies = [
        pltpu.make_async_remote_copy(
            src_ref=src, dst_ref=dst, send_sem=near_send.at[i], recv_sem=near_recv.at[i],
            device_id={"grp": tg, "pen": tp}, device_id_type=MESH,
        )
        for i, (src, dst, tg, tp) in enumerate(moves)
    ]
    upward, downward, aside = (0, 3), (1, 4), (2,)
    for i in range(10, 15):
        copies[i].start()
    lax.fori_loop(1, n, far_start, 0)
    for i in range(5, 10):
        copies[i].start()
    for i in aside:
        copies[i].start()

    @pl.when(g < n - 1)
    def _():
        for i in upward:
            copies[i].start()

    @pl.when(g > 0)
    def _():
        for i in downward:
            copies[i].start()

    fp_ref[4 : rows + 4, 0:zd] = u_ref[...]
    vp_ref[2 : planes + 2, 0:zd] = v_ref[...]
    cb_ref[0] = cell_ref[...]
    rbody[:, pl.ds(g * planes, planes)] = bsend[pl.ds(g * 8, 8)]

    for i in range(10, 15):
        copies[i].wait()

    lane128 = lax.broadcasted_iota(jnp.int32, (1, 128), 1)
    wanted = jnp.full((1, 128), -1, jnp.int32)
    for j in range(NF):
        wanted = jnp.where(lane128 == j, ps_ref[j], wanted)
    pick = (lax.broadcasted_iota(jnp.int32, (px, 128), 0) == wanted).astype(BF16)

    def inlet(row):
        hi, lo = split2(row)
        return dot(lo, pick) + dot(hi, pick)

    cosine = jnp.cos(yaw_ref[...])
    sine = jnp.sin(yaw_ref[...])
    index = [cb_ref[k, 0:1, :] for k in range(6)]
    turned = [cb_ref[k].T for k in range(6)]
    count = index[0].shape[1]
    lane_t = lax.broadcasted_iota(jnp.int32, (count, TURB), 1)

    def at_turbine(k, table):
        return jnp.sum(jnp.where(turned[k][:, 1:2] == lane_t, table, 0.0), axis=1, keepdims=True)

    lane_x = lax.broadcasted_iota(jnp.int32, (count, fx), 1)
    sub_z = lax.broadcasted_iota(jnp.int32, (depth, count), 0)
    along = [lax.rem(turned[k][:, 0:1], fx) for k in range(6)]

    def spread(k, s):
        return jnp.where(along[k] == lane_x, at_turbine(k, cosine[s : s + 1]), 0.0)

    sub_column = lax.broadcasted_iota(jnp.int32, (depth, 1), 0)
    z_global = jnp.where(
        sub_column < zd + 4, p * zd + sub_column, p * zd + sub_column - depth
    )
    z_ok = (z_global >= 0) & (z_global < lax.axis_size("pen") * zd)

    def row_ok(r):
        y = g * rows + (r - 4)
        return z_ok & (y >= 0) & (y < n * rows)

    for body, edge, first, last, offset in (
        (1, 4, 0, 4, rows - 4),
        (0, 3, 4, rows + 4, -4),
        (2, 5, rows + 4, rows + 8, -(rows + 4)),
    ):
        values = [
            split2(jnp.concatenate([spread(body, s), spread(edge, s)], axis=0)) for s in range(2)
        ]
        z_body = lax.rem(index[body] // fx, zd)
        y_body = index[body] // (fx * zd)
        z_edge = lax.rem(index[edge] // fx, zd)
        y_edge = index[edge] // (fx * zd)
        z_edge = jnp.where(z_edge < 4, z_edge + zd, jnp.where(z_edge >= zd - 4, z_edge + 8, -1))
        for r in range(first, last):
            yl = r + offset
            hot_body = (sub_z == z_body) & (y_body == yl)
            hot_edge = (sub_z == z_edge) & (y_edge == yl)
            hot = jnp.concatenate([hot_body.astype(F32), hot_edge.astype(F32)], axis=1).astype(BF16)
            for s, field in ((0, c0), (1, c1)):
                hi, lo = values[s]
                total = dot(hot, lo) + dot(hot, hi)
                field[r] = jnp.where(row_ok(r), total, 0.0)

    def far_wait(d, carry):
        far(d).wait()
        return carry

    lax.fori_loop(1, n, far_wait, 0)

    for i in range(8):
        flipped = rbody[i].T
        for h in range(2):
            part = flipped[h * zd : (h + 1) * zd]
            w_ref[h * 8 + i, 0:zd] = part
            wedge[h * 8 + i, 0:4] = part[0:4]
            wedge[h * 8 + i, 4:8] = part[zd - 4 : zd]
    last = pltpu.make_async_remote_copy(
        src_ref=wedge, dst_ref=w_ref.at[:, zd : zd + 8], send_sem=edge_send, recv_sem=edge_recv,
        device_id={"grp": g, "pen": q}, device_id_type=MESH,
    )
    last.start()

    for i in range(5, 10):
        copies[i].wait()

    for i in range(1, planes + 3):
        v1[i] = periodic_row(vp_ref, i, True)
    for i in range(2, planes + 2):
        prec_ref[i - 2] = periodic_row(v1, i, True)[0:zd]

    for i in aside:
        copies[i].wait()

    @pl.when(g < n - 1)
    def _():
        for i in upward:
            copies[i].wait_send()
        for i in downward:
            copies[i].wait_recv()

    @pl.when(g > 0)
    def _():
        for i in downward:
            copies[i].wait_send()
        for i in upward:
            copies[i].wait_recv()

    last.wait()


    for i in range(1, 15):
        vw1[i] = periodic_row(w_ref, i, False)
    for i in range(2, 14):
        vw2[i] = periodic_row(vw1, i, False)

    lane_f = lax.broadcasted_iota(jnp.int32, (depth, fx), 1)
    in_fringe = lane_f < NF
    blank = jnp.zeros((depth, fx - 128), F32)

    def fringed(planes_in, field):
        wide = jnp.concatenate([inlet(planes_in), blank], axis=1)
        return jnp.where(in_fringe, wide, field)

    for r in range(16):
        field = fringed(vw1[r], fp_ref[r]) if 1 <= r < 15 else jnp.where(in_fringe, 0.0, fp_ref[r])
        w0[r] = jnp.where(row_ok(r), field, 0.0)

    def forward(step, src, r, cos_field):
        field = src[r]
        upper_y = src[r + 1]
        lower_y = src[r - 1]
        upper_z = pltpu.roll(field, depth - 1, 0)
        lower_z = pltpu.roll(field, 1, 0)
        behind = jnp.where(lane_f == 0, field, pltpu.roll(field, 1, 1))
        slope_y = 0.5 * (upper_y - lower_y)
        slope_z = 0.5 * (upper_z - lower_z)
        square = slope_y * slope_y + slope_z * slope_z + SLOPE_EPS
        inverse = lax.rsqrt(square)
        viscosity = VISC_BASE + VISC_SLOPE * (square * inverse)
        laplacian = upper_y + lower_y + upper_z + lower_z - 4.0 * field
        moved = field - COURANT * (field - behind) + viscosity * laplacian
        c = cos_field[r]
        share = (0.5 * VISC_SLOPE) * laplacian * inverse
        nu[step, r] = viscosity
        ry[step, r] = share * slope_y
        rz[step, r] = share * slope_z
        return moved - FORCE_GAIN * (c * c) * field

    for r in range(1, 15):
        new = forward(0, w0, r, c0)
        u1[r] = new
        field = fringed(vw2[r], new) if 2 <= r < 14 else jnp.where(in_fringe, 0.0, new)
        w1[r] = jnp.where(row_ok(r), field, 0.0)
    for r in range(2, 14):
        new = forward(1, w1, r, c1)
        u2[r] = new
        c = c1[r]
        lam[r] = (2.0 * POWER_GAIN) * (c * c * c) * new
    for r in range(4, rows + 4):
        farm_ref[r - 4] = u2[r][0:zd]
        c = c1[r]
        term = c * (2.0 * FORCE_GAIN * w1[r] * lam[r] - 3.0 * POWER_GAIN * c * u2[r] * u2[r])
        gc1[r - 4] = term[0:zd]

    def spread_terms(step, r):
        value = lam[r]
        am[r] = value * nu[step, r]
        bm[r] = value * ry[step, r]

    def backward(step, r, cos_field):
        value = lam[r]
        a = am[r]
        b = value * rz[step, r]
        c = cos_field[r]
        ahead = jnp.where(lane_f == fx - 1, 0.0, pltpu.roll(value, fx - 1, 1))
        total = value * ((1.0 - COURANT) - FORCE_GAIN * (c * c)) + COURANT * ahead - 4.0 * a
        total = total + (am[r - 1] + bm[r - 1]) + (am[r + 1] - bm[r + 1])
        total = total + pltpu.roll(a + b, 1, 0) + pltpu.roll(a - b, depth - 1, 0)
        return jnp.where(in_fringe, 0.0, total)

    for r in range(2, 14):
        spread_terms(1, r)
    for r in range(3, 13):
        c = c0[r]
        value = backward(1, r, c1) + (2.0 * POWER_GAIN) * (c * c * c) * u1[r]
        u2[r] = jnp.where(row_ok(r), value, 0.0)
    for r in range(3, 13):
        lam[r] = u2[r]
    for r in range(4, rows + 4):
        c = c0[r]
        term = c * (2.0 * FORCE_GAIN * w0[r] * lam[r] - 3.0 * POWER_GAIN * c * u1[r] * u1[r])
        gc0[r - 4] = term[0:zd]
    flat = turned[0][:, 0:1] // fx
    take = (flat == lax.broadcasted_iota(jnp.int32, (count, rows * zd), 1)).astype(F32).astype(BF16)
    total_a[g * m + p] = jnp.zeros(total_a.shape[1:], F32)
    mine = total_a.at[g * m + p]
    for s, terms in ((0, gc0), (1, gc1)):
        hi, lo = split2(terms[...].reshape(rows * zd, fx))
        lines = dot(take, lo) + dot(take, hi)
        value = jnp.sum(jnp.where(along[0] == lane_x, lines, 0.0), axis=1, keepdims=True)
        value = value * at_turbine(0, sine[s : s + 1])
        mine[s : s + 1, 0:TURB] = jnp.sum(
            jnp.where(turned[0][:, 1:2] == lane_t, value, 0.0), axis=0, keepdims=True
        )

    def near_copy(d):
        return pltpu.make_async_remote_copy(
            src_ref=total_a.at[g * m + p], dst_ref=total_a.at[g * m + p],
            send_sem=a_send.at[d], recv_sem=a_recv.at[d], device_id=peer(d), device_id_type=MESH,
        )

    def line_copy(d):
        return pltpu.make_async_remote_copy(
            src_ref=total_b.at[scen], dst_ref=total_b.at[scen],
            send_sem=b_send.at[d], recv_sem=b_recv.at[d], device_id=line(d), device_id_type=MESH,
        )

    def start(make):
        def run(d, carry):
            make(d).start()
            return carry

        return run

    def wait(make):
        def run(d, carry):
            make(d).wait()
            return carry

        return run

    lax.fori_loop(1, n * m, start(near_copy), 0)
    for r in range(3, 13):
        spread_terms(0, r)
    for r in range(4, rows + 4):
        sens_ref[r - 4] = backward(0, r, c0)[0:zd]

    lax.fori_loop(1, n * m, wait(near_copy), 0)
    total_b[scen] = jnp.sum(total_a[...], axis=0)
    lax.fori_loop(1, ns, start(line_copy), 0)
    lax.fori_loop(1, ns, wait(line_copy), 0)
    grad_ref[...] = jnp.sum(total_b[...], axis=0)[0 : grad_ref.shape[0], 0 : grad_ref.shape[1]]


def farm_steps(sizes, v, u, index, turbine, yaw, ps):
    planes, zd, fy = v.shape
    rows, _, fx = u.shape
    ns, n, m = sizes
    px = n * planes
    depth = zd + 8
    farm = pltpu.VMEM((16, depth, fx), F32)
    dma = pltpu.SemaphoreType.DMA
    return pl.pallas_call(
        functools.partial(farm_kernel, sizes),
        out_shape=(
            pltpu.VMEM(v.shape, F32),
            pltpu.VMEM(u.shape, F32),
            pltpu.VMEM(u.shape, F32),
            pltpu.VMEM(yaw.shape, F32),
        ),
        in_specs=[HBM] * 5 + [SMEM],
        out_specs=(VMEM,) * 4,
        scratch_shapes=[
            farm,
            pltpu.VMEM((planes + 4, depth, fy), F32),
            pltpu.VMEM((16, depth, px), F32),
            pltpu.VMEM((6, 8, index.shape[1]), jnp.int32),
            pltpu.VMEM(v.shape, F32),
            pltpu.VMEM(u.shape, F32),
            pltpu.VMEM((8, index.shape[1]), jnp.int32),
            pltpu.VMEM(index.shape, jnp.int32),
            pltpu.VMEM(turbine.shape, jnp.int32),
            pltpu.VMEM(yaw.shape, F32),
            dma((5,)),
            pltpu.VMEM((planes, 8, fy), F32),
            pltpu.VMEM((rows, 8, fx), F32),
            pltpu.VMEM((fy, planes, 2 * zd), F32),
            pltpu.VMEM((8, px, 2 * zd), F32),
            pltpu.VMEM((16, 8, px), F32),
            pltpu.VMEM((planes + 4, depth, fy), F32),
            pltpu.VMEM((16, depth, px), F32),
            pltpu.VMEM((16, depth, px), F32),
            farm, farm, farm, farm, farm, farm, farm,
            pltpu.VMEM((2, 16, depth, fx), F32),
            pltpu.VMEM((2, 16, depth, fx), F32),
            pltpu.VMEM((2, 16, depth, fx), F32),
            farm, farm,
            pltpu.VMEM(u.shape, F32),
            pltpu.VMEM(u.shape, F32),
            pltpu.VMEM((n * m, 2, 128), F32),
            pltpu.VMEM((ns, 2, 128), F32),
            dma((15,)), dma((15,)), dma((n,)), dma((n,)), dma, dma,
            dma((n * m,)), dma((n * m,)), dma((ns,)), dma((ns,)),
        ],
        compiler_params=pltpu.CompilerParams(
            collective_id=0, has_side_effects=True, vmem_limit_bytes=56 * 1024 * 1024
        ),
        name="farm_steps",
    )(v, u, index, turbine, yaw, ps)


def finish_kernel(*refs):
    count = (len(refs) - 1) // 2
    sem = refs[-1]
    copies = [pltpu.make_async_copy(refs[i], refs[count + i], sem.at[i]) for i in range(count)]
    for copy in copies:
        copy.start()
    for copy in copies:
        copy.wait()


def finish(*arrays):
    return pl.pallas_call(
        finish_kernel,
        out_shape=tuple(jax.ShapeDtypeStruct(x.shape, F32) for x in arrays),
        in_specs=[VMEM] * len(arrays),
        out_specs=(HBM,) * len(arrays),
        scratch_shapes=[pltpu.SemaphoreType.DMA((len(arrays),))],
        name="finish",
    )(*[pltpu.with_memory_space_constraint(x, pltpu.VMEM) for x in arrays])


def shards(sizes, prec_state, farm_state, yaw_angles, plane_source, cell_index, cell_turbine):
    prec, farm, sens, yaw_grad = farm_steps(
        sizes, prec_state[0], farm_state[0], cell_index[0], cell_turbine[0], yaw_angles,
        plane_source,
    )
    prec, farm, sens, yaw_grad = finish(prec, farm, sens, yaw_grad)
    return (prec[None], farm[None], sens[None], yaw_grad)


def solution(mesh):
    spec = P("scen", "grp", "pen", None)
    in_specs = (spec, spec, P(), P(), P("grp", "pen", None), P("grp", "pen", None))
    out_specs = (spec, spec, spec, P())
    sizes = tuple(mesh.shape[axis] for axis in ("scen", "grp", "pen"))
    return jax.shard_map(
        functools.partial(shards, sizes), mesh=mesh, in_specs=in_specs, out_specs=out_specs,
        check_vma=False,
    )
```

```python
import functools

import jax
import jax.numpy as jnp
from jax import lax
from jax.experimental import pallas as pl
from jax.experimental.pallas import tpu as pltpu
from jax.sharding import PartitionSpec as P

NF = 16
TURB = 64
COURANT = 0.3
VISC_BASE = 0.03
VISC_SLOPE = 0.03
SLOPE_EPS = 0.01
FORCE_GAIN = 0.3
POWER_GAIN = 0.002

MESH = pl.DeviceIdType.MESH
VMEM = pl.BlockSpec(memory_space=pltpu.VMEM)
HBM = pl.BlockSpec(memory_space=pltpu.HBM)
SMEM = pl.BlockSpec(memory_space=pltpu.SMEM)
F32 = jnp.float32
BF16 = jnp.bfloat16


def split2(b):
    high = b.astype(BF16)
    return high, (b - high.astype(F32)).astype(BF16)


def dot(a, b):
    return jnp.dot(a, b, preferred_element_type=F32)


def advance_plane(centre, upper_a, lower_a, upper_z, lower_z, upper_l, lower_l, lower_x):
    slope_a = 0.5 * (upper_a - lower_a)
    slope_l = 0.5 * (upper_l - lower_l)
    slope_z = 0.5 * (upper_z - lower_z)
    viscosity = VISC_BASE + VISC_SLOPE * jnp.sqrt(
        slope_a * slope_a + slope_l * slope_l + slope_z * slope_z + SLOPE_EPS
    )
    laplacian = upper_a + lower_a + upper_l + lower_l + upper_z + lower_z - 6.0 * centre
    return centre - COURANT * (centre - lower_x) + viscosity * laplacian


def periodic_row(src, i, lead_is_x):
    centre = src[i]
    depth, lanes = centre.shape
    upper_l = pltpu.roll(centre, lanes - 1, 1)
    lower_l = pltpu.roll(centre, 1, 1)
    upper_z = pltpu.roll(centre, depth - 1, 0)
    lower_z = pltpu.roll(centre, 1, 0)
    upper_a = src[i + 1]
    lower_a = src[i - 1]
    lower_x = lower_a if lead_is_x else lower_l
    return advance_plane(centre, upper_a, lower_a, upper_z, lower_z, upper_l, lower_l, lower_x)


def farm_kernel(
    sizes, v_in, u_in, index_in, turbine_in, yaw_in, ps_ref,
    prec_ref, farm_ref, sens_ref, grad_ref,
    fp_ref, vp_ref, w_ref, cb_ref,
    v_ref, u_ref, cell_ref, index_ref, turbine_ref, yaw_ref, in_sem,
    vedge, uedge, bsend, rbody, wedge,
    v1, vw1, vw2, c0, c1, w0, w1, u1, u2, lam, nu, ry, rz, am, bm, gc0, gc1, total_a, total_b,
    pick_ref, cp_ref, side_ref, part_ref,
    near_send, near_recv, far_send, far_recv, edge_send, edge_recv, a_send, a_recv, b_send, b_recv,
):
    g = lax.axis_index("grp")
    p = lax.axis_index("pen")
    q = 1 - p
    ns, n, m = sizes
    up = lax.rem(g + 1, n)
    down = lax.rem(g + n - 1, n)
    odd = lax.rem(g, 2)
    planes, zd, fy = v_ref.shape
    rows, _, fx = u_ref.shape
    depth = zd + 8
    px = w_ref.shape[2]
    scen = lax.axis_index("scen")

    barrier = pltpu.get_barrier_semaphore()

    def peer(d):
        other = lax.rem(g * m + p + d, n * m)
        return {"grp": other // m, "pen": lax.rem(other, m)}

    def mate(d):
        return {"grp": lax.rem(g + d, n), "pen": p}

    def line(d):
        return {"scen": lax.rem(scen + d, ns), "grp": g, "pen": p}

    def greet(make):
        def run(d, carry):
            pl.semaphore_signal(barrier, inc=1, device_id=make(d), device_id_type=MESH)
            return carry

        return run

    lax.fori_loop(1, n, greet(mate), 0)
    for target in (g, up, down):
        pl.semaphore_signal(barrier, inc=1, device_id={"grp": target, "pen": q}, device_id_type=MESH)
    lax.fori_loop(1, ns, greet(line), 0)

    loads = [
        pltpu.make_async_copy(src, dst, in_sem.at[i])
        for i, (src, dst) in enumerate((
            (v_in, v_ref), (index_in, index_ref), (turbine_in, turbine_ref), (u_in, u_ref), (yaw_in, yaw_ref),
        ))
    ]
    for load in loads:
        load.start()
    loads[0].wait()

    vedge[:, 0:4] = v_ref[:, 0:4]
    vedge[:, 4:8] = v_ref[:, zd - 4 : zd]
    for x in range(planes):
        plane = v_ref[x]
        both = jnp.concatenate([plane, pltpu.roll(plane, fy - 6, 1)], axis=0).T
        bsend[4 : fy + 4, x, :] = both
        bsend[0:4, x, :] = both[fy - 4 : fy]
        bsend[fy + 4 : fy + 8, x, :] = both[0:4]

    for load in loads[1:]:
        load.wait()
    uedge[:, 0:4] = u_ref[:, 0:4]
    uedge[:, 4:8] = u_ref[:, zd - 4 : zd]
    cell_ref[...] = jnp.zeros_like(cell_ref)
    cell_ref[0:1] = index_ref[...]
    cell_ref[1:2] = turbine_ref[...]

    pl.semaphore_wait(barrier, (n - 1) + 3 + (ns - 1))

    def far(d):
        target = lax.rem(g + d, n)
        return pltpu.make_async_remote_copy(
            src_ref=bsend.at[pl.ds(target * 8 + 4 * lax.rem(target, 2), 6)],
            dst_ref=rbody.at[:, pl.ds(g * planes, planes)],
            send_sem=far_send.at[d],
            recv_sem=far_recv.at[d],
            device_id={"grp": target, "pen": p},
            device_id_type=MESH,
        )

    def far_start(d, carry):
        far(d).start()
        return carry


    moves = [
        (u_ref.at[rows - 4 : rows], fp_ref.at[0:4, 0:zd], up, p),
        (u_ref.at[0:4], fp_ref.at[rows + 4 : rows + 8, 0:zd], down, p),
        (uedge, fp_ref.at[4 : rows + 4, zd : zd + 8], g, q),
        (uedge.at[rows - 4 : rows], fp_ref.at[0:4, zd : zd + 8], up, q),
        (uedge.at[0:4], fp_ref.at[rows + 4 : rows + 8, zd : zd + 8], down, q),
        (v_ref.at[planes - 2 : planes], vp_ref.at[0:2, 0:zd], up, p),
        (v_ref.at[0:2], vp_ref.at[planes + 2 : planes + 4, 0:zd], down, p),
        (vedge, vp_ref.at[2 : planes + 2, zd : zd + 8], g, q),
        (vedge.at[planes - 2 : planes], vp_ref.at[0:2, zd : zd + 8], up, q),
        (vedge.at[0:2], vp_ref.at[planes + 2 : planes + 4, zd : zd + 8], down, q),
        (cell_ref, cb_ref.at[1], up, p),
        (cell_ref, cb_ref.at[2], down, p),
        (cell_ref, cb_ref.at[3], g, q),
        (cell_ref, cb_ref.at[4], up, q),
        (cell_ref, cb_ref.at[5], down, q),
    ]
    copies = [
        pltpu.make_async_remote_copy(
            src_ref=src, dst_ref=dst, send_sem=near_send.at[i], recv_sem=near_recv.at[i],
            device_id={"grp": tg, "pen": tp}, device_id_type=MESH,
        )
        for i, (src, dst, tg, tp) in enumerate(moves)
    ]
    upward, downward, aside = (0, 3), (1, 4), (2,)
    for i in range(10, 15):
        copies[i].start()
    for i in range(5, 10):
        copies[i].start()
    for i in aside:
        copies[i].start()

    @pl.when(g < n - 1)
    def _():
        for i in upward:
            copies[i].start()

    @pl.when(g > 0)
    def _():
        for i in downward:
            copies[i].start()

    lax.fori_loop(1, n, far_start, 0)

    fp_ref[4 : rows + 4, 0:zd] = u_ref[...]
    vp_ref[2 : planes + 2, 0:zd] = v_ref[...]
    cb_ref[0] = cell_ref[...]
    rbody[:, pl.ds(g * planes, planes)] = bsend[pl.ds(g * 8 + 4 * odd, 6)]

    for i in range(10, 15):
        copies[i].wait()

    lane128 = lax.broadcasted_iota(jnp.int32, (1, 128), 1)
    wanted = jnp.full((1, 128), -1, jnp.int32)
    for j in range(NF):
        wanted = jnp.where((lane128 & (NF - 1)) == j, ps_ref[j], wanted)
    sub_x = lax.broadcasted_iota(jnp.int32, (px, 128), 0)
    pick = jnp.concatenate(
        [(sub_x == wanted).astype(F32), (sub_x == ps_ref[NF - 1]).astype(F32)], axis=1
    ).astype(BF16)
    pick_ref[0:px] = pick
    pick_ref[px : 2 * px] = pick

    cosine = jnp.cos(yaw_ref[...])
    sine = jnp.sin(yaw_ref[...])
    index = [cb_ref[k, 0:1, :] for k in range(6)]
    turned = [cb_ref[k].T for k in range(6)]
    count = index[0].shape[1]
    lane_t = lax.broadcasted_iota(jnp.int32, (count, TURB), 1)

    def at_turbine(k, table):
        return jnp.sum(jnp.where(turned[k][:, 1:2] == lane_t, table, 0.0), axis=1, keepdims=True)

    lane_x = lax.broadcasted_iota(jnp.int32, (count, fx), 1)
    sub_z = lax.broadcasted_iota(jnp.int32, (depth, count), 0)
    along = [lax.rem(turned[k][:, 0:1], fx) for k in range(6)]

    turned_cos = [[at_turbine(k, cosine[s : s + 1]) for s in range(2)] for k in range(6)]

    def spread(k, s):
        return jnp.where(along[k] == lane_x, turned_cos[k][s], 0.0)

    sub_column = lax.broadcasted_iota(jnp.int32, (depth, 1), 0)
    z_global = jnp.where(
        sub_column < zd + 4, p * zd + sub_column, p * zd + sub_column - depth
    )
    z_ok = (z_global >= 0) & (z_global < lax.axis_size("pen") * zd)

    def row_ok(r):
        y = g * rows + (r - 4)
        return z_ok & (y >= 0) & (y < n * rows)

    for body, edge, first, last, offset in (
        (1, 4, 0, 4, rows - 4),
        (0, 3, 4, rows + 4, -4),
        (2, 5, rows + 4, rows + 8, -(rows + 4)),
    ):
        values = [
            split2(jnp.concatenate([spread(body, s), spread(edge, s)], axis=0)) for s in range(2)
        ]
        z_body = lax.rem(index[body] // fx, zd)
        y_body = index[body] // (fx * zd)
        z_edge = lax.rem(index[edge] // fx, zd)
        y_edge = index[edge] // (fx * zd)
        z_edge = jnp.where(z_edge < 4, z_edge + zd, jnp.where(z_edge >= zd - 4, z_edge + 8, -1))
        for r in range(first, last):
            yl = r + offset
            hot_body = (sub_z == z_body) & (y_body == yl)
            hot_edge = (sub_z == z_edge) & (y_edge == yl)
            hot = jnp.concatenate([hot_body.astype(F32), hot_edge.astype(F32)], axis=1).astype(BF16)
            for s, field in ((0, c0), (1, c1)):
                hi, lo = values[s]
                total = dot(hot, lo) + dot(hot, hi)
                field[r] = jnp.where(row_ok(r), total, 0.0)

    lane_r = lane128 // 8
    lane_k = lane128 & 7
    y_side = g * rows + lane_r - 4
    side_ok = z_ok & (y_side >= 0) & (y_side < n * rows)
    y_edge = g * rows + jnp.where(lane128 < 64, -1, rows)
    edge_ok = z_ok & (y_edge >= 0) & (y_edge < n * rows)

    hots, packs = [], []
    slots = []
    for k in range(6):
        z_cell = lax.rem(index[k] // fx, zd)
        if k >= 3:
            z_cell = jnp.where(z_cell < 4, z_cell + zd, jnp.where(z_cell >= zd - 4, z_cell + 8, -1))
        hots.append((sub_z == z_cell).astype(F32))
        r_cell = turned[k][:, 0:1] // (fx * zd) - (-4, rows - 4, -(rows + 4))[k % 3]
        in_front = jnp.where(along[k] < NF, (r_cell - 4) * NF + along[k], -1)
        beside = jnp.where((along[k] >= 14) & (along[k] < 22), r_cell * 8 + along[k] - 14, -1)
        slots.append((in_front, beside))
        parts = []
        for s in range(2):
            if k % 3 == 0:
                parts.append(jnp.where(in_front == lane128, turned_cos[k][s], 0.0))
            else:
                parts.append(jnp.zeros((count, 128), F32))
            parts.append(jnp.where(beside == lane128, turned_cos[k][s], 0.0))
        packs.append(jnp.concatenate(parts, axis=1))
    hi, lo = split2(jnp.concatenate(packs, axis=0))
    hot = jnp.concatenate(hots, axis=1).astype(BF16)
    packed = dot(hot, lo) + dot(hot, hi)
    for k in range(4):
        part = packed[:, k * 128 : (k + 1) * 128]
        cp_ref[k] = jnp.where(side_ok if k % 2 else z_ok, part, 0.0)

    def far_wait(d, carry):
        far(d).wait()
        return carry

    for i in range(5, 10):
        copies[i].wait()

    for i in aside:
        copies[i].wait()

    @pl.when(g < n - 1)
    def _():
        for i in upward:
            copies[i].wait_send()
        for i in downward:
            copies[i].wait_recv()

    @pl.when(g > 0)
    def _():
        for i in downward:
            copies[i].wait_send()
        for i in upward:
            copies[i].wait_recv()

    side = jnp.zeros((depth, 128), F32)
    for r in range(16):
        side = jnp.where(lane_r == r, pltpu.roll(fp_ref[r, :, 0:128], (8 * r - 14) % 128, 1), side)
    side_ref[...] = side

    lane_f = lax.broadcasted_iota(jnp.int32, (depth, fx), 1)

    for r in range(16):
        w0[r] = jnp.where(row_ok(r), fp_ref[r], 0.0)

    def advance(field, upper_y, lower_y, behind, c):
        upper_z = pltpu.roll(field, depth - 1, 0)
        lower_z = pltpu.roll(field, 1, 0)
        slope_y = 0.5 * (upper_y - lower_y)
        slope_z = 0.5 * (upper_z - lower_z)
        square = slope_y * slope_y + slope_z * slope_z + SLOPE_EPS
        inverse = lax.rsqrt(square)
        viscosity = VISC_BASE + VISC_SLOPE * (square * inverse)
        laplacian = upper_y + lower_y + upper_z + lower_z - 4.0 * field
        moved = field - COURANT * (field - behind) + viscosity * laplacian
        share = (0.5 * VISC_SLOPE) * laplacian * inverse
        return moved - FORCE_GAIN * (c * c) * field, viscosity, share * slope_y, share * slope_z

    def forward(step, src, r, cos_field):
        field = src[r]
        behind = jnp.where(lane_f == 0, field, pltpu.roll(field, 1, 1))
        new, nu[step, r], ry[step, r], rz[step, r] = advance(
            field, src[r + 1], src[r - 1], behind, cos_field[r]
        )
        return new

    def power_slope(c, field):
        return (2.0 * POWER_GAIN) * (c * c * c) * field

    def yaw_term(c, field, value, new):
        return c * (2.0 * FORCE_GAIN * field * value - 3.0 * POWER_GAIN * c * new * new)

    for r in range(1, 15):
        new = forward(0, w0, r, c0)
        u1[r] = new
        w1[r] = jnp.where(row_ok(r), new, 0.0)
    for r in range(2, 14):
        new = forward(1, w1, r, c1)
        u2[r] = new
        lam[r] = power_slope(c1[r], new)
    for r in range(4, rows + 4):
        farm_ref[r - 4] = u2[r][0:zd]
        gc1[r - 4] = yaw_term(c1[r], w1[r], lam[r], u2[r])[0:zd]

    def spread_terms(step, r):
        value = lam[r]
        am[r] = value * nu[step, r]
        bm[r] = value * ry[step, r]

    def backward(step, r, cos_field):
        value = lam[r]
        a = am[r]
        b = value * rz[step, r]
        c = cos_field[r]
        ahead = jnp.where(lane_f == fx - 1, 0.0, pltpu.roll(value, fx - 1, 1))
        total = value * ((1.0 - COURANT) - FORCE_GAIN * (c * c)) + COURANT * ahead - 4.0 * a
        total = total + (am[r - 1] + bm[r - 1]) + (am[r + 1] - bm[r + 1])
        return total + pltpu.roll(a + b, 1, 0) + pltpu.roll(a - b, depth - 1, 0)

    for r in range(2, 14):
        spread_terms(1, r)
    for r in range(3, 13):
        value = backward(1, r, c1) + power_slope(c0[r], u1[r])
        u2[r] = jnp.where(row_ok(r), value, 0.0)
    for r in range(3, 13):
        lam[r] = u2[r]
    for r in range(4, rows + 4):
        gc0[r - 4] = yaw_term(c0[r], w0[r], lam[r], u1[r])[0:zd]
    for r in range(3, 13):
        spread_terms(0, r)
    for r in range(4, rows + 4):
        sens_ref[r - 4] = backward(0, r, c0)[0:zd]

    flat = turned[0][:, 0:1] // fx
    take = (flat == lax.broadcasted_iota(jnp.int32, (count, rows * zd), 1)).astype(F32).astype(BF16)
    far_along = jnp.where(along[0] >= 18, along[0], -1)
    for s, terms in ((0, gc0), (1, gc1)):
        hi, lo = split2(terms[...].reshape(rows * zd, fx))
        lines = dot(take, lo) + dot(take, hi)
        value = jnp.where(far_along == lane_x, lines, 0.0)
        part_ref[s] = value[:, 0:128] + value[:, 128:256]

    lax.fori_loop(1, n, far_wait, 0)

    base = 4 * odd
    for i in range(6):
        flipped = rbody[i].T
        for h in range(2):
            part = flipped[h * zd : (h + 1) * zd]
            w_ref[base + h * 6 + i, 0:zd] = part
            wedge[base + h * 6 + i, 0:4] = part[0:4]
            wedge[base + h * 6 + i, 4:8] = part[zd - 4 : zd]
    inner, outer = 8 - base, 12 * odd
    mated = g + 1 - 2 * odd
    lasts = [
        pltpu.make_async_remote_copy(
            src_ref=src, dst_ref=dst, send_sem=edge_send.at[i], recv_sem=edge_recv.at[i],
            device_id={"grp": target, "pen": side_pen}, device_id_type=MESH,
        )
        for i, (src, dst, target, side_pen) in enumerate((
            (wedge.at[pl.ds(base, 12)], w_ref.at[pl.ds(base, 12), zd : zd + 8], g, q),
            (wedge.at[pl.ds(inner, 4)], w_ref.at[pl.ds(outer, 4), zd : zd + 8], mated, q),
            (w_ref.at[pl.ds(inner, 4), 0:zd], w_ref.at[pl.ds(outer, 4), 0:zd], mated, p),
        ))
    ]
    for last in lasts:
        last.start()

    for i in range(1, planes + 3):
        v1[i] = periodic_row(vp_ref, i, True)
    for i in range(2, planes + 2):
        prec_ref[i - 2] = periodic_row(v1, i, True)[0:zd]

    for last in lasts:
        last.wait()

    for i in range(1, 15):
        vw1[i] = periodic_row(w_ref, i, False)
    for i in range(2, 14):
        vw2[i] = periodic_row(vw1, i, False)

    def inlets(src, first, stop):
        hi, lo = split2(src[first:stop].reshape((stop - first) * depth, px))
        found = dot(jnp.concatenate([hi, lo], axis=1), pick_ref[...])
        front = jnp.zeros((depth, 128), F32)
        rim = front
        beside = front
        for r in range(first, stop):
            part = found[(r - first) * depth : (r - first + 1) * depth]
            if 4 <= r < 12:
                front = jnp.where(lane128 // NF == r - 4, part[:, 0:128], front)
            elif r == 3:
                rim = jnp.where(lane128 < 64, part[:, 0:128], rim)
            elif r == 12:
                rim = jnp.where(lane128 >= 64, part[:, 0:128], rim)
            beside = jnp.where(lane_r == r, part[:, 128:256], beside)
        return jnp.where(z_ok, front, 0.0), jnp.where(edge_ok, rim, 0.0), beside

    def front_step(field, rim, c):
        upper_y = jnp.where(lane128 >= 112, rim, pltpu.roll(field, 112, 1))
        lower_y = jnp.where(lane128 < 16, rim, pltpu.roll(field, 16, 1))
        behind = jnp.where((lane128 & 15) == 0, field, pltpu.roll(field, 1, 1))
        return advance(field, upper_y, lower_y, behind, c)[0]

    def side_step(field, c):
        return advance(field, pltpu.roll(field, 120, 1), pltpu.roll(field, 8, 1), pltpu.roll(field, 1, 1), c)

    def side_back(value, c, scale, slope_y, slope_z):
        a = value * scale
        b = value * slope_y
        d = value * slope_z
        total = value * ((1.0 - COURANT) - FORCE_GAIN * (c * c)) - 4.0 * a
        total = total + COURANT * pltpu.roll(value, 127, 1)
        total = total + pltpu.roll(a + b, 8, 1) + pltpu.roll(a - b, 120, 1)
        return total + pltpu.roll(a + d, 1, 0) + pltpu.roll(a - d, depth - 1, 0)

    front0, rim0, beside0 = inlets(vw1, 1, 15)
    front1, rim1, beside1 = inlets(vw2, 2, 14)
    cf0, cs0, cf1, cs1 = (cp_ref[k] for k in range(4))

    uf1 = front_step(front0, rim0, cf0)
    uf2 = front_step(front1, rim1, cf1)
    tf0 = yaw_term(cf0, front0, power_slope(cf0, uf1), uf1)
    tf1 = yaw_term(cf1, front1, power_slope(cf1, uf2), uf2)

    ws0 = jnp.where(side_ok, jnp.where(lane_k == 1, beside0, side_ref[...]), 0.0)
    us1, *back0 = side_step(ws0, cs0)
    ws1 = jnp.where(side_ok, jnp.where(lane_k == 1, beside1, us1), 0.0)
    us2, *back1 = side_step(ws1, cs1)
    value2 = power_slope(cs1, us2)
    value1 = jnp.where(side_ok, side_back(value2, cs1, *back1) + power_slope(cs0, us1), 0.0)
    ss = side_back(value1, cs0, *back0)
    ts0 = yaw_term(cs0, ws0, value1, us1)
    ts1 = yaw_term(cs1, ws1, value2, us2)

    terms = jnp.concatenate([tf0, ts0, tf1, ts1], axis=1)[0:zd]
    hi, lo = split2(terms)
    z_own = lax.rem(turned[0][:, 0:1] // fx, zd)
    take_z = (z_own == lax.broadcasted_iota(jnp.int32, (count, zd), 1)).astype(F32).astype(BF16)
    lines = dot(take_z, lo) + dot(take_z, hi)
    in_front = slots[0][0]
    beside = jnp.where((along[0] >= 16) & (along[0] < 18), slots[0][1], -1)
    total_a[g * m + p] = jnp.zeros(total_a.shape[1:], F32)
    mine = total_a.at[g * m + p]
    for s in range(2):
        value = part_ref[s] + jnp.where(in_front == lane128, lines[:, s * 256 : s * 256 + 128], 0.0)
        value = value + jnp.where(beside == lane128, lines[:, s * 256 + 128 : s * 256 + 256], 0.0)
        value = jnp.sum(value, axis=1, keepdims=True) * at_turbine(0, sine[s : s + 1])
        mine[s : s + 1, 0:TURB] = jnp.sum(
            jnp.where(turned[0][:, 1:2] == lane_t, value, 0.0), axis=0, keepdims=True
        )

    def near_copy(d):
        return pltpu.make_async_remote_copy(
            src_ref=total_a.at[g * m + p], dst_ref=total_a.at[g * m + p],
            send_sem=a_send.at[d], recv_sem=a_recv.at[d], device_id=peer(d), device_id_type=MESH,
        )

    def line_copy(d):
        return pltpu.make_async_remote_copy(
            src_ref=total_b.at[scen], dst_ref=total_b.at[scen],
            send_sem=b_send.at[d], recv_sem=b_recv.at[d], device_id=line(d), device_id_type=MESH,
        )

    def start(make):
        def run(d, carry):
            make(d).start()
            return carry

        return run

    def wait(make):
        def run(d, carry):
            make(d).wait()
            return carry

        return run

    lax.fori_loop(1, n * m, start(near_copy), 0)

    us2, ss, uf2 = us2[0:zd], ss[0:zd], uf2[0:zd]
    for r in range(rows):
        shift = (-18 - 8 * r) % 128
        farm_ref[r, :, 0:128] = jnp.where(
            lane128 < NF, pltpu.roll(uf2, (-NF * r) % 128, 1),
            jnp.where(lane128 < 18, pltpu.roll(us2, shift, 1), farm_ref[r, :, 0:128]),
        )
        sens_ref[r, :, 0:128] = jnp.where(
            lane128 < NF, 0.0,
            jnp.where(lane128 < 18, pltpu.roll(ss, shift, 1), sens_ref[r, :, 0:128]),
        )

    lax.fori_loop(1, n * m, wait(near_copy), 0)
    total_b[scen] = jnp.sum(total_a[...], axis=0)
    lax.fori_loop(1, ns, start(line_copy), 0)
    lax.fori_loop(1, ns, wait(line_copy), 0)
    grad_ref[...] = jnp.sum(total_b[...], axis=0)[0 : grad_ref.shape[0], 0 : grad_ref.shape[1]]


def farm_steps(sizes, v, u, index, turbine, yaw, ps):
    planes, zd, fy = v.shape
    rows, _, fx = u.shape
    ns, n, m = sizes
    px = n * planes
    depth = zd + 8
    farm = pltpu.VMEM((16, depth, fx), F32)
    dma = pltpu.SemaphoreType.DMA
    return pl.pallas_call(
        functools.partial(farm_kernel, sizes),
        out_shape=(
            pltpu.VMEM(v.shape, F32),
            pltpu.VMEM(u.shape, F32),
            pltpu.VMEM(u.shape, F32),
            pltpu.VMEM(yaw.shape, F32),
        ),
        in_specs=[HBM] * 5 + [SMEM],
        out_specs=(VMEM,) * 4,
        scratch_shapes=[
            farm,
            pltpu.VMEM((planes + 4, depth, fy), F32),
            pltpu.VMEM((16, depth, px), F32),
            pltpu.VMEM((6, 8, index.shape[1]), jnp.int32),
            pltpu.VMEM(v.shape, F32),
            pltpu.VMEM(u.shape, F32),
            pltpu.VMEM((8, index.shape[1]), jnp.int32),
            pltpu.VMEM(index.shape, jnp.int32),
            pltpu.VMEM(turbine.shape, jnp.int32),
            pltpu.VMEM(yaw.shape, F32),
            dma((5,)),
            pltpu.VMEM((planes, 8, fy), F32),
            pltpu.VMEM((rows, 8, fx), F32),
            pltpu.VMEM((fy + 8, planes, 2 * zd), F32),
            pltpu.VMEM((6, px, 2 * zd), F32),
            pltpu.VMEM((16, 8, px), F32),
            pltpu.VMEM((planes + 4, depth, fy), F32),
            pltpu.VMEM((16, depth, px), F32),
            pltpu.VMEM((16, depth, px), F32),
            farm, farm, farm, farm, farm, farm, farm,
            pltpu.VMEM((2, 16, depth, fx), F32),
            pltpu.VMEM((2, 16, depth, fx), F32),
            pltpu.VMEM((2, 16, depth, fx), F32),
            farm, farm,
            pltpu.VMEM(u.shape, F32),
            pltpu.VMEM(u.shape, F32),
            pltpu.VMEM((n * m, 2, 128), F32),
            pltpu.VMEM((ns, 2, 128), F32),
            pltpu.VMEM((2 * px, 256), BF16),
            pltpu.VMEM((4, depth, 128), F32),
            pltpu.VMEM((depth, 128), F32),
            pltpu.VMEM((2, index.shape[1], 128), F32),
            dma((15,)), dma((15,)), dma((n,)), dma((n,)), dma((3,)), dma((3,)),
            dma((n * m,)), dma((n * m,)), dma((ns,)), dma((ns,)),
        ],
        compiler_params=pltpu.CompilerParams(
            collective_id=0, has_side_effects=True, vmem_limit_bytes=56 * 1024 * 1024
        ),
        name="farm_steps",
    )(v, u, index, turbine, yaw, ps)


def finish_kernel(*refs):
    count = (len(refs) - 1) // 2
    sem = refs[-1]
    copies = [pltpu.make_async_copy(refs[i], refs[count + i], sem.at[i]) for i in range(count)]
    for copy in copies:
        copy.start()
    for copy in copies:
        copy.wait()


def finish(*arrays):
    return pl.pallas_call(
        finish_kernel,
        out_shape=tuple(jax.ShapeDtypeStruct(x.shape, F32) for x in arrays),
        in_specs=[VMEM] * len(arrays),
        out_specs=(HBM,) * len(arrays),
        scratch_shapes=[pltpu.SemaphoreType.DMA((len(arrays),))],
        name="finish",
    )(*[pltpu.with_memory_space_constraint(x, pltpu.VMEM) for x in arrays])


def shards(sizes, prec_state, farm_state, yaw_angles, plane_source, cell_index, cell_turbine):
    prec, farm, sens, yaw_grad = farm_steps(
        sizes, prec_state[0], farm_state[0], cell_index[0], cell_turbine[0], yaw_angles,
        plane_source,
    )
    prec, farm, sens, yaw_grad = finish(prec, farm, sens, yaw_grad)
    return (prec[None], farm[None], sens[None], yaw_grad)


def solution(mesh):
    spec = P("scen", "grp", "pen", None)
    in_specs = (spec, spec, P(), P(), P("grp", "pen", None), P("grp", "pen", None))
    out_specs = (spec, spec, spec, P())
    sizes = tuple(mesh.shape[axis] for axis in ("scen", "grp", "pen"))
    return jax.shard_map(
        functools.partial(shards, sizes), mesh=mesh, in_specs=in_specs, out_specs=out_specs,
        check_vma=False,
    )
```

```python
import functools

import jax
import jax.numpy as jnp
from jax import lax
from jax.experimental import pallas as pl
from jax.experimental.pallas import tpu as pltpu
from jax.sharding import PartitionSpec as P

NF = 16
TURB = 64
COURANT = 0.3
VISC_BASE = 0.03
VISC_SLOPE = 0.03
SLOPE_EPS = 0.01
FORCE_GAIN = 0.3
POWER_GAIN = 0.002

MESH = pl.DeviceIdType.MESH
VMEM = pl.BlockSpec(memory_space=pltpu.VMEM)
HBM = pl.BlockSpec(memory_space=pltpu.HBM)
SMEM = pl.BlockSpec(memory_space=pltpu.SMEM)
F32 = jnp.float32
BF16 = jnp.bfloat16


def split2(b):
    high = b.astype(BF16)
    return high, (b - high.astype(F32)).astype(BF16)


def dot(a, b):
    return jnp.dot(a, b, preferred_element_type=F32)


def advance_plane(centre, upper_a, lower_a, upper_z, lower_z, upper_l, lower_l, lower_x):
    slope_a = 0.5 * (upper_a - lower_a)
    slope_l = 0.5 * (upper_l - lower_l)
    slope_z = 0.5 * (upper_z - lower_z)
    viscosity = VISC_BASE + VISC_SLOPE * jnp.sqrt(
        slope_a * slope_a + slope_l * slope_l + slope_z * slope_z + SLOPE_EPS
    )
    laplacian = upper_a + lower_a + upper_l + lower_l + upper_z + lower_z - 6.0 * centre
    return centre - COURANT * (centre - lower_x) + viscosity * laplacian


def periodic_row(src, i, lead_is_x):
    centre = src[i]
    depth, lanes = centre.shape
    upper_l = pltpu.roll(centre, lanes - 1, 1)
    lower_l = pltpu.roll(centre, 1, 1)
    upper_z = pltpu.roll(centre, depth - 1, 0)
    lower_z = pltpu.roll(centre, 1, 0)
    upper_a = src[i + 1]
    lower_a = src[i - 1]
    lower_x = lower_a if lead_is_x else lower_l
    return advance_plane(centre, upper_a, lower_a, upper_z, lower_z, upper_l, lower_l, lower_x)


def farm_kernel(
    sizes, v_in, u_in, index_in, turbine_in, yaw_in, ps_ref,
    prec_ref, farm_ref, sens_ref, grad_ref,
    fp_ref, vp_ref, w_ref, cb_ref,
    v_ref, u_ref, cell_ref, index_ref, turbine_ref, yaw_ref, in_sem,
    vedge, uedge, bsend, rbody, wedge,
    v1, vw1, vw2, c0, c1, w0, w1, u1, u2, lam, nu, ry, rz, am, bm, gc0, gc1, total_a, total_b,
    pick_ref, cp_ref, side_ref, part_ref,
    near_send, near_recv, far_send, far_recv, edge_send, edge_recv, a_send, a_recv, b_send, b_recv,
):
    g = lax.axis_index("grp")
    p = lax.axis_index("pen")
    q = 1 - p
    ns, n, m = sizes
    up = lax.rem(g + 1, n)
    down = lax.rem(g + n - 1, n)
    odd = lax.rem(g, 2)
    planes, zd, fy = v_ref.shape
    rows, _, fx = u_ref.shape
    depth = zd + 8
    px = w_ref.shape[2]
    scen = lax.axis_index("scen")

    barrier = pltpu.get_barrier_semaphore()

    def peer(d):
        other = lax.rem(g * m + p + d, n * m)
        return {"grp": other // m, "pen": lax.rem(other, m)}

    def mate(d):
        return {"grp": lax.rem(g + d, n), "pen": p}

    def line(d):
        return {"scen": lax.rem(scen + d, ns), "grp": g, "pen": p}

    def greet(make):
        def run(d, carry):
            pl.semaphore_signal(barrier, inc=1, device_id=make(d), device_id_type=MESH)
            return carry

        return run

    lax.fori_loop(1, n, greet(mate), 0)
    for target in (g, up, down):
        pl.semaphore_signal(barrier, inc=1, device_id={"grp": target, "pen": q}, device_id_type=MESH)
    lax.fori_loop(1, ns, greet(line), 0)

    loads = [
        pltpu.make_async_copy(src, dst, in_sem.at[i])
        for i, (src, dst) in enumerate((
            (v_in, v_ref), (index_in, index_ref), (turbine_in, turbine_ref), (u_in, u_ref), (yaw_in, yaw_ref),
        ))
    ]
    for load in loads:
        load.start()
    loads[0].wait()

    vedge[:, 0:4] = v_ref[:, 0:4]
    vedge[:, 4:8] = v_ref[:, zd - 4 : zd]
    for x in range(planes):
        plane = v_ref[x]
        both = jnp.concatenate([plane, pltpu.roll(plane, fy - 6, 1)], axis=0).T
        bsend[4 : fy + 4, x, :] = both
        bsend[0:4, x, :] = both[fy - 4 : fy]
        bsend[fy + 4 : fy + 8, x, :] = both[0:4]

    for load in loads[1:]:
        load.wait()
    uedge[:, 0:4] = u_ref[:, 0:4]
    uedge[:, 4:8] = u_ref[:, zd - 4 : zd]
    cell_ref[...] = jnp.zeros_like(cell_ref)
    cell_ref[0:1] = index_ref[...]
    cell_ref[1:2] = turbine_ref[...]

    pl.semaphore_wait(barrier, (n - 1) + 3 + (ns - 1))

    def far(d):
        target = lax.rem(g + d, n)
        return pltpu.make_async_remote_copy(
            src_ref=bsend.at[pl.ds(target * 8 + 4 * lax.rem(target, 2), 6)],
            dst_ref=rbody.at[:, pl.ds(g * planes, planes)],
            send_sem=far_send.at[d],
            recv_sem=far_recv.at[d],
            device_id={"grp": target, "pen": p},
            device_id_type=MESH,
        )

    def far_start(d, carry):
        far(d).start()
        return carry


    moves = [
        (u_ref.at[rows - 4 : rows], fp_ref.at[0:4, 0:zd], up, p),
        (u_ref.at[0:4], fp_ref.at[rows + 4 : rows + 8, 0:zd], down, p),
        (uedge, fp_ref.at[4 : rows + 4, zd : zd + 8], g, q),
        (uedge.at[rows - 4 : rows], fp_ref.at[0:4, zd : zd + 8], up, q),
        (uedge.at[0:4], fp_ref.at[rows + 4 : rows + 8, zd : zd + 8], down, q),
        (v_ref.at[planes - 2 : planes], vp_ref.at[0:2, 0:zd], up, p),
        (v_ref.at[0:2], vp_ref.at[planes + 2 : planes + 4, 0:zd], down, p),
        (vedge, vp_ref.at[2 : planes + 2, zd : zd + 8], g, q),
        (vedge.at[planes - 2 : planes], vp_ref.at[0:2, zd : zd + 8], up, q),
        (vedge.at[0:2], vp_ref.at[planes + 2 : planes + 4, zd : zd + 8], down, q),
        (cell_ref, cb_ref.at[1], up, p),
        (cell_ref, cb_ref.at[2], down, p),
        (cell_ref, cb_ref.at[3], g, q),
        (cell_ref, cb_ref.at[4], up, q),
        (cell_ref, cb_ref.at[5], down, q),
    ]
    copies = [
        pltpu.make_async_remote_copy(
            src_ref=src, dst_ref=dst, send_sem=near_send.at[i], recv_sem=near_recv.at[i],
            device_id={"grp": tg, "pen": tp}, device_id_type=MESH,
        )
        for i, (src, dst, tg, tp) in enumerate(moves)
    ]
    upward, downward, aside = (0, 3), (1, 4), (2,)
    for i in range(10, 15):
        copies[i].start()
    for i in aside:
        copies[i].start()
    lax.fori_loop(1, n, far_start, 0)

    @pl.when(g < n - 1)
    def _():
        for i in upward:
            copies[i].start()

    @pl.when(g > 0)
    def _():
        for i in downward:
            copies[i].start()

    for i in range(5, 10):
        copies[i].start()

    fp_ref[4 : rows + 4, 0:zd] = u_ref[...]
    vp_ref[2 : planes + 2, 0:zd] = v_ref[...]
    cb_ref[0] = cell_ref[...]
    rbody[:, pl.ds(g * planes, planes)] = bsend[pl.ds(g * 8 + 4 * odd, 6)]

    for i in range(10, 15):
        copies[i].wait()

    lane128 = lax.broadcasted_iota(jnp.int32, (1, 128), 1)
    wanted = jnp.full((1, 128), -1, jnp.int32)
    for j in range(NF):
        wanted = jnp.where((lane128 & (NF - 1)) == j, ps_ref[j], wanted)
    sub_x = lax.broadcasted_iota(jnp.int32, (px, 128), 0)
    pick = jnp.concatenate(
        [(sub_x == wanted).astype(F32), (sub_x == ps_ref[NF - 1]).astype(F32)], axis=1
    ).astype(BF16)
    pick_ref[0:px] = pick
    pick_ref[px : 2 * px] = pick

    cosine = jnp.cos(yaw_ref[...])
    sine = jnp.sin(yaw_ref[...])
    index = [cb_ref[k, 0:1, :] for k in range(6)]
    turned = [cb_ref[k].T for k in range(6)]
    count = index[0].shape[1]
    lane_t = lax.broadcasted_iota(jnp.int32, (count, TURB), 1)

    def at_turbine(k, table):
        return jnp.sum(jnp.where(turned[k][:, 1:2] == lane_t, table, 0.0), axis=1, keepdims=True)

    lane_x = lax.broadcasted_iota(jnp.int32, (count, fx), 1)
    sub_z = lax.broadcasted_iota(jnp.int32, (depth, count), 0)
    along = [lax.rem(turned[k][:, 0:1], fx) for k in range(6)]

    turned_cos = [[at_turbine(k, cosine[s : s + 1]) for s in range(2)] for k in range(6)]

    def spread(k, s):
        return jnp.where(along[k] == lane_x, turned_cos[k][s], 0.0)

    sub_column = lax.broadcasted_iota(jnp.int32, (depth, 1), 0)
    z_global = jnp.where(
        sub_column < zd + 4, p * zd + sub_column, p * zd + sub_column - depth
    )
    z_ok = (z_global >= 0) & (z_global < lax.axis_size("pen") * zd)

    def row_ok(r):
        y = g * rows + (r - 4)
        return z_ok & (y >= 0) & (y < n * rows)

    for body, edge, first, last, offset in (
        (1, 4, 0, 4, rows - 4),
        (0, 3, 4, rows + 4, -4),
        (2, 5, rows + 4, rows + 8, -(rows + 4)),
    ):
        values = [
            split2(jnp.concatenate([spread(body, s), spread(edge, s)], axis=0)) for s in range(2)
        ]
        z_body = lax.rem(index[body] // fx, zd)
        y_body = index[body] // (fx * zd)
        z_edge = lax.rem(index[edge] // fx, zd)
        y_edge = index[edge] // (fx * zd)
        z_edge = jnp.where(z_edge < 4, z_edge + zd, jnp.where(z_edge >= zd - 4, z_edge + 8, -1))
        for r in range(first, last):
            yl = r + offset
            hot_body = (sub_z == z_body) & (y_body == yl)
            hot_edge = (sub_z == z_edge) & (y_edge == yl)
            hot = jnp.concatenate([hot_body.astype(F32), hot_edge.astype(F32)], axis=1).astype(BF16)
            for s, field in ((0, c0), (1, c1)):
                hi, lo = values[s]
                total = dot(hot, lo) + dot(hot, hi)
                field[r] = jnp.where(row_ok(r), total, 0.0)

    lane_r = lane128 // 8
    lane_k = lane128 & 7
    y_side = g * rows + lane_r - 4
    side_ok = z_ok & (y_side >= 0) & (y_side < n * rows)
    y_edge = g * rows + jnp.where(lane128 < 64, -1, rows)
    edge_ok = z_ok & (y_edge >= 0) & (y_edge < n * rows)

    hots, packs = [], []
    slots = []
    for k in range(6):
        z_cell = lax.rem(index[k] // fx, zd)
        if k >= 3:
            z_cell = jnp.where(z_cell < 4, z_cell + zd, jnp.where(z_cell >= zd - 4, z_cell + 8, -1))
        hots.append((sub_z == z_cell).astype(F32))
        r_cell = turned[k][:, 0:1] // (fx * zd) - (-4, rows - 4, -(rows + 4))[k % 3]
        in_front = jnp.where(along[k] < NF, (r_cell - 4) * NF + along[k], -1)
        beside = jnp.where((along[k] >= 14) & (along[k] < 22), r_cell * 8 + along[k] - 14, -1)
        slots.append((in_front, beside))
        parts = []
        for s in range(2):
            if k % 3 == 0:
                parts.append(jnp.where(in_front == lane128, turned_cos[k][s], 0.0))
            else:
                parts.append(jnp.zeros((count, 128), F32))
            parts.append(jnp.where(beside == lane128, turned_cos[k][s], 0.0))
        packs.append(jnp.concatenate(parts, axis=1))
    hi, lo = split2(jnp.concatenate(packs, axis=0))
    hot = jnp.concatenate(hots, axis=1).astype(BF16)
    packed = dot(hot, lo) + dot(hot, hi)
    for k in range(4):
        part = packed[:, k * 128 : (k + 1) * 128]
        cp_ref[k] = jnp.where(side_ok if k % 2 else z_ok, part, 0.0)

    def far_wait(d, carry):
        far(d).wait()
        return carry

    for i in aside:
        copies[i].wait()

    lane_f = lax.broadcasted_iota(jnp.int32, (depth, fx), 1)

    for r in range(4, 12):
        w0[r] = jnp.where(z_ok, fp_ref[r], 0.0)

    def advance(field, upper_y, lower_y, behind, c):
        upper_z = pltpu.roll(field, depth - 1, 0)
        lower_z = pltpu.roll(field, 1, 0)
        slope_y = 0.5 * (upper_y - lower_y)
        slope_z = 0.5 * (upper_z - lower_z)
        square = slope_y * slope_y + slope_z * slope_z + SLOPE_EPS
        inverse = lax.rsqrt(square)
        viscosity = VISC_BASE + VISC_SLOPE * (square * inverse)
        laplacian = upper_y + lower_y + upper_z + lower_z - 4.0 * field
        moved = field - COURANT * (field - behind) + viscosity * laplacian
        share = (0.5 * VISC_SLOPE) * laplacian * inverse
        return moved - FORCE_GAIN * (c * c) * field, viscosity, share * slope_y, share * slope_z

    def forward(step, src, r, cos_field):
        field = src[r]
        behind = jnp.where(lane_f == 0, field, pltpu.roll(field, 1, 1))
        new, nu[step, r], ry[step, r], rz[step, r] = advance(
            field, src[r + 1], src[r - 1], behind, cos_field[r]
        )
        return new

    def power_slope(c, field):
        return (2.0 * POWER_GAIN) * (c * c * c) * field

    def yaw_term(c, field, value, new):
        return c * (2.0 * FORCE_GAIN * field * value - 3.0 * POWER_GAIN * c * new * new)

    for r in range(5, 11):
        new = forward(0, w0, r, c0)
        u1[r] = new
        w1[r] = jnp.where(row_ok(r), new, 0.0)
    for r in range(6, 10):
        new = forward(1, w1, r, c1)
        u2[r] = new
        lam[r] = power_slope(c1[r], new)
    lax.fori_loop(1, n, far_wait, 0)

    base = 4 * odd
    for i in range(6):
        flipped = rbody[i].T
        for h in range(2):
            part = flipped[h * zd : (h + 1) * zd]
            w_ref[base + h * 6 + i, 0:zd] = part
            wedge[base + h * 6 + i, 0:4] = part[0:4]
            wedge[base + h * 6 + i, 4:8] = part[zd - 4 : zd]
    inner, outer = 8 - base, 12 * odd
    mated = g + 1 - 2 * odd
    lasts = [
        pltpu.make_async_remote_copy(
            src_ref=src, dst_ref=dst, send_sem=edge_send.at[i], recv_sem=edge_recv.at[i],
            device_id={"grp": target, "pen": side_pen}, device_id_type=MESH,
        )
        for i, (src, dst, target, side_pen) in enumerate((
            (wedge.at[pl.ds(base, 12)], w_ref.at[pl.ds(base, 12), zd : zd + 8], g, q),
            (wedge.at[pl.ds(inner, 4)], w_ref.at[pl.ds(outer, 4), zd : zd + 8], mated, q),
            (w_ref.at[pl.ds(inner, 4), 0:zd], w_ref.at[pl.ds(outer, 4), 0:zd], mated, p),
        ))
    ]
    for last in lasts:
        last.start()

    for last in lasts:
        last.wait()


    for i in range(1, 15):
        vw1[i] = periodic_row(w_ref, i, False)
    for i in range(2, 14):
        vw2[i] = periodic_row(vw1, i, False)

    def inlets(src, first, stop):
        hi, lo = split2(src[first:stop].reshape((stop - first) * depth, px))
        found = dot(jnp.concatenate([hi, lo], axis=1), pick_ref[...])
        front = jnp.zeros((depth, 128), F32)
        rim = front
        beside = front
        for r in range(first, stop):
            part = found[(r - first) * depth : (r - first + 1) * depth]
            if 4 <= r < 12:
                front = jnp.where(lane128 // NF == r - 4, part[:, 0:128], front)
            elif r == 3:
                rim = jnp.where(lane128 < 64, part[:, 0:128], rim)
            elif r == 12:
                rim = jnp.where(lane128 >= 64, part[:, 0:128], rim)
            beside = jnp.where(lane_r == r, part[:, 128:256], beside)
        return jnp.where(z_ok, front, 0.0), jnp.where(edge_ok, rim, 0.0), beside

    def front_step(field, rim, c):
        upper_y = jnp.where(lane128 >= 112, rim, pltpu.roll(field, 112, 1))
        lower_y = jnp.where(lane128 < 16, rim, pltpu.roll(field, 16, 1))
        behind = jnp.where((lane128 & 15) == 0, field, pltpu.roll(field, 1, 1))
        return advance(field, upper_y, lower_y, behind, c)[0]

    def side_step(field, c):
        return advance(field, pltpu.roll(field, 120, 1), pltpu.roll(field, 8, 1), pltpu.roll(field, 1, 1), c)

    def side_back(value, c, scale, slope_y, slope_z):
        a = value * scale
        b = value * slope_y
        d = value * slope_z
        total = value * ((1.0 - COURANT) - FORCE_GAIN * (c * c)) - 4.0 * a
        total = total + COURANT * pltpu.roll(value, 127, 1)
        total = total + pltpu.roll(a + b, 8, 1) + pltpu.roll(a - b, 120, 1)
        return total + pltpu.roll(a + d, 1, 0) + pltpu.roll(a - d, depth - 1, 0)

    front0, rim0, beside0 = inlets(vw1, 1, 15)
    front1, rim1, beside1 = inlets(vw2, 2, 14)
    cf0, cs0, cf1, cs1 = (cp_ref[k] for k in range(4))

    uf1 = front_step(front0, rim0, cf0)
    uf2 = front_step(front1, rim1, cf1)
    tf0 = yaw_term(cf0, front0, power_slope(cf0, uf1), uf1)
    tf1 = yaw_term(cf1, front1, power_slope(cf1, uf2), uf2)

    @pl.when(g < n - 1)
    def _():
        for i in upward:
            copies[i].wait_send()
        for i in downward:
            copies[i].wait_recv()

    @pl.when(g > 0)
    def _():
        for i in downward:
            copies[i].wait_send()
        for i in upward:
            copies[i].wait_recv()

    side = jnp.zeros((depth, 128), F32)
    for r in range(16):
        side = jnp.where(lane_r == r, pltpu.roll(fp_ref[r, :, 0:128], (8 * r - 14) % 128, 1), side)
    side_ref[...] = side

    def spread_terms(step, r):
        value = lam[r]
        am[r] = value * nu[step, r]
        bm[r] = value * ry[step, r]

    def backward(step, r, cos_field):
        value = lam[r]
        a = am[r]
        b = value * rz[step, r]
        c = cos_field[r]
        ahead = jnp.where(lane_f == fx - 1, 0.0, pltpu.roll(value, fx - 1, 1))
        total = value * ((1.0 - COURANT) - FORCE_GAIN * (c * c)) + COURANT * ahead - 4.0 * a
        total = total + (am[r - 1] + bm[r - 1]) + (am[r + 1] - bm[r + 1])
        return total + pltpu.roll(a + b, 1, 0) + pltpu.roll(a - b, depth - 1, 0)

    for r in (0, 1, 2, 3, 12, 13, 14, 15):
        w0[r] = jnp.where(row_ok(r), fp_ref[r], 0.0)
    for r in (1, 2, 3, 4, 11, 12, 13, 14):
        new = forward(0, w0, r, c0)
        u1[r] = new
        w1[r] = jnp.where(row_ok(r), new, 0.0)
    for r in (2, 3, 4, 5, 10, 11, 12, 13):
        new = forward(1, w1, r, c1)
        u2[r] = new
        lam[r] = power_slope(c1[r], new)
    for r in range(4, rows + 4):
        gc1[r - 4] = yaw_term(c1[r], w1[r], lam[r], u2[r])[0:zd]
        farm_ref[r - 4] = u2[r][0:zd]
    for r in range(2, 14):
        spread_terms(1, r)
    for r in range(3, 13):
        value = backward(1, r, c1) + power_slope(c0[r], u1[r])
        u2[r] = jnp.where(row_ok(r), value, 0.0)
    for r in range(3, 13):
        lam[r] = u2[r]
    for r in range(4, rows + 4):
        gc0[r - 4] = yaw_term(c0[r], w0[r], lam[r], u1[r])[0:zd]
    ws0 = jnp.where(side_ok, jnp.where(lane_k == 1, beside0, side_ref[...]), 0.0)
    us1, *back0 = side_step(ws0, cs0)
    ws1 = jnp.where(side_ok, jnp.where(lane_k == 1, beside1, us1), 0.0)
    us2, *back1 = side_step(ws1, cs1)
    value2 = power_slope(cs1, us2)
    value1 = jnp.where(side_ok, side_back(value2, cs1, *back1) + power_slope(cs0, us1), 0.0)
    ts0 = yaw_term(cs0, ws0, value1, us1)
    ts1 = yaw_term(cs1, ws1, value2, us2)

    flat = turned[0][:, 0:1] // fx
    take = (flat == lax.broadcasted_iota(jnp.int32, (count, rows * zd), 1)).astype(F32).astype(BF16)
    far_along = jnp.where(along[0] >= 18, along[0], -1)
    for s, terms in ((0, gc0), (1, gc1)):
        hi, lo = split2(terms[...].reshape(rows * zd, fx))
        lines = dot(take, lo) + dot(take, hi)
        value = jnp.where(far_along == lane_x, lines, 0.0)
        part_ref[s] = value[:, 0:128] + value[:, 128:256]

    terms = jnp.concatenate([tf0, ts0, tf1, ts1], axis=1)[0:zd]
    hi, lo = split2(terms)
    z_own = lax.rem(turned[0][:, 0:1] // fx, zd)
    take_z = (z_own == lax.broadcasted_iota(jnp.int32, (count, zd), 1)).astype(F32).astype(BF16)
    lines = dot(take_z, lo) + dot(take_z, hi)
    in_front = slots[0][0]
    beside = jnp.where((along[0] >= 16) & (along[0] < 18), slots[0][1], -1)
    total_a[g * m + p] = jnp.zeros(total_a.shape[1:], F32)
    mine = total_a.at[g * m + p]
    for s in range(2):
        value = part_ref[s] + jnp.where(in_front == lane128, lines[:, s * 256 : s * 256 + 128], 0.0)
        value = value + jnp.where(beside == lane128, lines[:, s * 256 + 128 : s * 256 + 256], 0.0)
        value = jnp.sum(value, axis=1, keepdims=True) * at_turbine(0, sine[s : s + 1])
        mine[s : s + 1, 0:TURB] = jnp.sum(
            jnp.where(turned[0][:, 1:2] == lane_t, value, 0.0), axis=0, keepdims=True
        )

    def near_copy(d):
        return pltpu.make_async_remote_copy(
            src_ref=total_a.at[g * m + p], dst_ref=total_a.at[g * m + p],
            send_sem=a_send.at[d], recv_sem=a_recv.at[d], device_id=peer(d), device_id_type=MESH,
        )

    def line_copy(d):
        return pltpu.make_async_remote_copy(
            src_ref=total_b.at[scen], dst_ref=total_b.at[scen],
            send_sem=b_send.at[d], recv_sem=b_recv.at[d], device_id=line(d), device_id_type=MESH,
        )

    def start(make):
        def run(d, carry):
            make(d).start()
            return carry

        return run

    def wait(make):
        def run(d, carry):
            make(d).wait()
            return carry

        return run

    lax.fori_loop(1, n * m, start(near_copy), 0)

    for r in range(3, 13):
        spread_terms(0, r)
    for r in range(4, rows + 4):
        sens_ref[r - 4] = backward(0, r, c0)[0:zd]

    ss = side_back(value1, cs0, *back0)

    us2, ss, uf2 = us2[0:zd], ss[0:zd], uf2[0:zd]
    for r in range(rows):
        shift = (-18 - 8 * r) % 128
        farm_ref[r, :, 0:128] = jnp.where(
            lane128 < NF, pltpu.roll(uf2, (-NF * r) % 128, 1),
            jnp.where(lane128 < 18, pltpu.roll(us2, shift, 1), farm_ref[r, :, 0:128]),
        )
        sens_ref[r, :, 0:128] = jnp.where(
            lane128 < NF, 0.0,
            jnp.where(lane128 < 18, pltpu.roll(ss, shift, 1), sens_ref[r, :, 0:128]),
        )

    for i in range(5, 10):
        copies[i].wait()

    for i in range(1, planes + 3):
        v1[i] = periodic_row(vp_ref, i, True)
    for i in range(2, planes + 2):
        prec_ref[i - 2] = periodic_row(v1, i, True)[0:zd]

    lax.fori_loop(1, n * m, wait(near_copy), 0)
    total_b[scen] = jnp.sum(total_a[...], axis=0)
    lax.fori_loop(1, ns, start(line_copy), 0)
    lax.fori_loop(1, ns, wait(line_copy), 0)
    grad_ref[...] = jnp.sum(total_b[...], axis=0)[0 : grad_ref.shape[0], 0 : grad_ref.shape[1]]


def farm_steps(sizes, v, u, index, turbine, yaw, ps):
    planes, zd, fy = v.shape
    rows, _, fx = u.shape
    ns, n, m = sizes
    px = n * planes
    depth = zd + 8
    farm = pltpu.VMEM((16, depth, fx), F32)
    dma = pltpu.SemaphoreType.DMA
    return pl.pallas_call(
        functools.partial(farm_kernel, sizes),
        out_shape=(
            pltpu.VMEM(v.shape, F32),
            pltpu.VMEM(u.shape, F32),
            pltpu.VMEM(u.shape, F32),
            pltpu.VMEM(yaw.shape, F32),
        ),
        in_specs=[HBM] * 5 + [SMEM],
        out_specs=(VMEM,) * 4,
        scratch_shapes=[
            farm,
            pltpu.VMEM((planes + 4, depth, fy), F32),
            pltpu.VMEM((16, depth, px), F32),
            pltpu.VMEM((6, 8, index.shape[1]), jnp.int32),
            pltpu.VMEM(v.shape, F32),
            pltpu.VMEM(u.shape, F32),
            pltpu.VMEM((8, index.shape[1]), jnp.int32),
            pltpu.VMEM(index.shape, jnp.int32),
            pltpu.VMEM(turbine.shape, jnp.int32),
            pltpu.VMEM(yaw.shape, F32),
            dma((5,)),
            pltpu.VMEM((planes, 8, fy), F32),
            pltpu.VMEM((rows, 8, fx), F32),
            pltpu.VMEM((fy + 8, planes, 2 * zd), F32),
            pltpu.VMEM((6, px, 2 * zd), F32),
            pltpu.VMEM((16, 8, px), F32),
            pltpu.VMEM((planes + 4, depth, fy), F32),
            pltpu.VMEM((16, depth, px), F32),
            pltpu.VMEM((16, depth, px), F32),
            farm, farm, farm, farm, farm, farm, farm,
            pltpu.VMEM((2, 16, depth, fx), F32),
            pltpu.VMEM((2, 16, depth, fx), F32),
            pltpu.VMEM((2, 16, depth, fx), F32),
            farm, farm,
            pltpu.VMEM(u.shape, F32),
            pltpu.VMEM(u.shape, F32),
            pltpu.VMEM((n * m, 2, 128), F32),
            pltpu.VMEM((ns, 2, 128), F32),
            pltpu.VMEM((2 * px, 256), BF16),
            pltpu.VMEM((4, depth, 128), F32),
            pltpu.VMEM((depth, 128), F32),
            pltpu.VMEM((2, index.shape[1], 128), F32),
            dma((15,)), dma((15,)), dma((n,)), dma((n,)), dma((3,)), dma((3,)),
            dma((n * m,)), dma((n * m,)), dma((ns,)), dma((ns,)),
        ],
        compiler_params=pltpu.CompilerParams(
            collective_id=0, has_side_effects=True, vmem_limit_bytes=56 * 1024 * 1024
        ),
        name="farm_steps",
    )(v, u, index, turbine, yaw, ps)


def finish_kernel(*refs):
    count = (len(refs) - 1) // 2
    sem = refs[-1]
    copies = [pltpu.make_async_copy(refs[i], refs[count + i], sem.at[i]) for i in range(count)]
    for copy in copies:
        copy.start()
    for copy in copies:
        copy.wait()


def finish(*arrays):
    return pl.pallas_call(
        finish_kernel,
        out_shape=tuple(jax.ShapeDtypeStruct(x.shape, F32) for x in arrays),
        in_specs=[VMEM] * len(arrays),
        out_specs=(HBM,) * len(arrays),
        scratch_shapes=[pltpu.SemaphoreType.DMA((len(arrays),))],
        name="finish",
    )(*[pltpu.with_memory_space_constraint(x, pltpu.VMEM) for x in arrays])


def shards(sizes, prec_state, farm_state, yaw_angles, plane_source, cell_index, cell_turbine):
    prec, farm, sens, yaw_grad = farm_steps(
        sizes, prec_state[0], farm_state[0], cell_index[0], cell_turbine[0], yaw_angles,
        plane_source,
    )
    prec, farm, sens, yaw_grad = finish(prec, farm, sens, yaw_grad)
    return (prec[None], farm[None], sens[None], yaw_grad)


def solution(mesh):
    spec = P("scen", "grp", "pen", None)
    in_specs = (spec, spec, P(), P(), P("grp", "pen", None), P("grp", "pen", None))
    out_specs = (spec, spec, spec, P())
    sizes = tuple(mesh.shape[axis] for axis in ("scen", "grp", "pen"))
    return jax.shard_map(
        functools.partial(shards, sizes), mesh=mesh, in_specs=in_specs, out_specs=out_specs,
        check_vma=False,
    )
```

```python
import functools

import jax
import jax.numpy as jnp
from jax import lax
from jax.experimental import pallas as pl
from jax.experimental.pallas import tpu as pltpu
from jax.sharding import PartitionSpec as P

NF = 16
TURB = 64
COURANT = 0.3
VISC_BASE = 0.03
VISC_SLOPE = 0.03
SLOPE_EPS = 0.01
FORCE_GAIN = 0.3
POWER_GAIN = 0.002

MESH = pl.DeviceIdType.MESH
VMEM = pl.BlockSpec(memory_space=pltpu.VMEM)
HBM = pl.BlockSpec(memory_space=pltpu.HBM)
SMEM = pl.BlockSpec(memory_space=pltpu.SMEM)
F32 = jnp.float32
BF16 = jnp.bfloat16


def split2(b):
    high = b.astype(BF16)
    return high, (b - high.astype(F32)).astype(BF16)


def dot(a, b):
    return jnp.dot(a, b, preferred_element_type=F32)


def advance_plane(centre, upper_a, lower_a, upper_z, lower_z, upper_l, lower_l, lower_x):
    slope_a = 0.5 * (upper_a - lower_a)
    slope_l = 0.5 * (upper_l - lower_l)
    slope_z = 0.5 * (upper_z - lower_z)
    viscosity = VISC_BASE + VISC_SLOPE * jnp.sqrt(
        slope_a * slope_a + slope_l * slope_l + slope_z * slope_z + SLOPE_EPS
    )
    laplacian = upper_a + lower_a + upper_l + lower_l + upper_z + lower_z - 6.0 * centre
    return centre - COURANT * (centre - lower_x) + viscosity * laplacian


def periodic_row(src, i, lead_is_x):
    centre = src[i]
    depth, lanes = centre.shape
    upper_l = pltpu.roll(centre, lanes - 1, 1)
    lower_l = pltpu.roll(centre, 1, 1)
    upper_z = pltpu.roll(centre, depth - 1, 0)
    lower_z = pltpu.roll(centre, 1, 0)
    upper_a = src[i + 1]
    lower_a = src[i - 1]
    lower_x = lower_a if lead_is_x else lower_l
    return advance_plane(centre, upper_a, lower_a, upper_z, lower_z, upper_l, lower_l, lower_x)


def farm_kernel(
    sizes, v_in, u_in, index_in, turbine_in, yaw_in, ps_ref,
    prec_ref, farm_ref, sens_ref, grad_ref,
    fp_ref, vp_ref, w_ref, cb_ref,
    v_ref, u_ref, cell_ref, index_ref, turbine_ref, yaw_ref, in_sem,
    vedge, uedge, bsend, rbody, esend, ebody,
    v1, vw1, vw2, c0, c1, w0, w1, u1, u2, lam, nu, ry, rz, am, bm, gc0, gc1, total_a, total_b,
    pick_ref, cp_ref, side_ref, part_ref,
    near_send, near_recv, far_send, far_recv, rim_send, rim_recv, edge_send, edge_recv, a_send, a_recv, b_send, b_recv,
):
    g = lax.axis_index("grp")
    p = lax.axis_index("pen")
    q = 1 - p
    ns, n, m = sizes
    up = lax.rem(g + 1, n)
    down = lax.rem(g + n - 1, n)
    odd = lax.rem(g, 2)
    planes, zd, fy = v_ref.shape
    rows, _, fx = u_ref.shape
    depth = zd + 8
    px = w_ref.shape[2]
    scen = lax.axis_index("scen")

    barrier = pltpu.get_barrier_semaphore()

    def peer(d):
        other = lax.rem(g * m + p + d, n * m)
        return {"grp": other // m, "pen": lax.rem(other, m)}

    def mate(d):
        return {"grp": lax.rem(g + d, n), "pen": p}

    def line(d):
        return {"scen": lax.rem(scen + d, ns), "grp": g, "pen": p}

    def greet(make):
        def run(d, carry):
            pl.semaphore_signal(barrier, inc=1, device_id=make(d), device_id_type=MESH)
            return carry

        return run

    lax.fori_loop(1, n, greet(mate), 0)
    for target in (g, up, down):
        pl.semaphore_signal(barrier, inc=1, device_id={"grp": target, "pen": q}, device_id_type=MESH)
    lax.fori_loop(1, ns, greet(line), 0)

    loads = [
        pltpu.make_async_copy(src, dst, in_sem.at[i])
        for i, (src, dst) in enumerate((
            (v_in, v_ref), (index_in, index_ref), (turbine_in, turbine_ref), (u_in, u_ref), (yaw_in, yaw_ref),
        ))
    ]
    for load in loads:
        load.start()
    loads[0].wait()

    vedge[:, 0:4] = v_ref[:, 0:4]
    vedge[:, 4:8] = v_ref[:, zd - 4 : zd]
    for x in range(planes):
        plane = v_ref[x]
        both = jnp.concatenate([plane, pltpu.roll(plane, fy - 6, 1)], axis=0).T
        bsend[4 : fy + 4, x, :] = both
        bsend[0:4, x, :] = both[fy - 4 : fy]
        bsend[fy + 4 : fy + 8, x, :] = both[0:4]

    for load in loads[1:]:
        load.wait()
    uedge[:, 0:4] = u_ref[:, 0:4]
    uedge[:, 4:8] = u_ref[:, zd - 4 : zd]
    cell_ref[...] = jnp.zeros_like(cell_ref)
    cell_ref[0:1] = index_ref[...]
    cell_ref[1:2] = turbine_ref[...]

    pl.semaphore_wait(barrier, (n - 1) + 3 + (ns - 1))

    def far(d):
        target = lax.rem(g + d, n)
        return pltpu.make_async_remote_copy(
            src_ref=bsend.at[pl.ds(target * 8 + 4 * lax.rem(target, 2), 6)],
            dst_ref=rbody.at[:, pl.ds(g * planes, planes)],
            send_sem=far_send.at[d],
            recv_sem=far_recv.at[d],
            device_id={"grp": target, "pen": p},
            device_id_type=MESH,
        )

    def far_start(d, carry):
        far(d).start()
        return carry


    moves = [
        (u_ref.at[rows - 4 : rows], fp_ref.at[0:4, 0:zd], up, p),
        (u_ref.at[0:4], fp_ref.at[rows + 4 : rows + 8, 0:zd], down, p),
        (uedge, fp_ref.at[4 : rows + 4, zd : zd + 8], g, q),
        (uedge.at[rows - 4 : rows], fp_ref.at[0:4, zd : zd + 8], up, q),
        (uedge.at[0:4], fp_ref.at[rows + 4 : rows + 8, zd : zd + 8], down, q),
        (v_ref.at[planes - 2 : planes], vp_ref.at[0:2, 0:zd], up, p),
        (v_ref.at[0:2], vp_ref.at[planes + 2 : planes + 4, 0:zd], down, p),
        (vedge, vp_ref.at[2 : planes + 2, zd : zd + 8], g, q),
        (vedge.at[planes - 2 : planes], vp_ref.at[0:2, zd : zd + 8], up, q),
        (vedge.at[0:2], vp_ref.at[planes + 2 : planes + 4, zd : zd + 8], down, q),
        (cell_ref, cb_ref.at[1], up, p),
        (cell_ref, cb_ref.at[2], down, p),
        (cell_ref, cb_ref.at[3], g, q),
        (cell_ref, cb_ref.at[4], up, q),
        (cell_ref, cb_ref.at[5], down, q),
    ]
    copies = [
        pltpu.make_async_remote_copy(
            src_ref=src, dst_ref=dst, send_sem=near_send.at[i], recv_sem=near_recv.at[i],
            device_id={"grp": tg, "pen": tp}, device_id_type=MESH,
        )
        for i, (src, dst, tg, tp) in enumerate(moves)
    ]
    upward, downward, aside = (0, 3), (1, 4), (2,)
    copies[7].start()
    for i in range(10, 15):
        copies[i].start()
    for i in aside:
        copies[i].start()
    @pl.when(g < n - 1)
    def _():
        for i in upward:
            copies[i].start()

    @pl.when(g > 0)
    def _():
        for i in downward:
            copies[i].start()

    lax.fori_loop(n // 2 - 2, n // 2 + 3, far_start, 0)

    def rim_copy(d):
        target = lax.rem(g + d, n)
        return pltpu.make_async_remote_copy(
            src_ref=esend.at[target], dst_ref=ebody.at[pl.ds(g * planes, planes)],
            send_sem=rim_send.at[d], recv_sem=rim_recv.at[d],
            device_id={"grp": target, "pen": p}, device_id_type=MESH,
        )

    def rim_start(d, carry):
        rim_copy(d).start()
        return carry

    def rim_wait(d, carry):
        rim_copy(d).wait()
        return carry

    copies[7].wait()
    for x in range(planes):
        edge = vp_ref[x + 2, zd : zd + 8]
        tall = jnp.concatenate(
            [edge if i == 4 else pltpu.roll(edge, (4 - i) % fy, 1) for i in range(16)], axis=0
        ).T
        esend[:, x, :] = tall.reshape(n, rows, 128)[:, 0]
    lax.fori_loop(1, n, rim_start, 0)
    lax.fori_loop(n // 2 + 3, n, far_start, 0)
    lax.fori_loop(1, n // 2 - 2, far_start, 0)

    for i in (5, 6, 8, 9):
        copies[i].start()

    ebody[pl.ds(g * planes, planes)] = esend[g]
    fp_ref[4 : rows + 4, 0:zd] = u_ref[...]
    vp_ref[2 : planes + 2, 0:zd] = v_ref[...]
    cb_ref[0] = cell_ref[...]
    rbody[:, pl.ds(g * planes, planes)] = bsend[pl.ds(g * 8 + 4 * odd, 6)]

    for i in range(10, 15):
        copies[i].wait()

    lane128 = lax.broadcasted_iota(jnp.int32, (1, 128), 1)
    wanted = jnp.full((1, 128), -1, jnp.int32)
    for j in range(NF):
        wanted = jnp.where((lane128 & (NF - 1)) == j, ps_ref[j], wanted)
    sub_x = lax.broadcasted_iota(jnp.int32, (px, 128), 0)
    pick = jnp.concatenate(
        [(sub_x == wanted).astype(F32), (sub_x == ps_ref[NF - 1]).astype(F32)], axis=1
    ).astype(BF16)
    pick_ref[0:px] = pick
    pick_ref[px : 2 * px] = pick

    cosine = jnp.cos(yaw_ref[...])
    sine = jnp.sin(yaw_ref[...])
    index = [cb_ref[k, 0:1, :] for k in range(6)]
    turned = [cb_ref[k].T for k in range(6)]
    count = index[0].shape[1]
    lane_t = lax.broadcasted_iota(jnp.int32, (count, TURB), 1)

    def at_turbine(k, table):
        return jnp.sum(jnp.where(turned[k][:, 1:2] == lane_t, table, 0.0), axis=1, keepdims=True)

    lane_x = lax.broadcasted_iota(jnp.int32, (count, fx), 1)
    sub_z = lax.broadcasted_iota(jnp.int32, (depth, count), 0)
    along = [lax.rem(turned[k][:, 0:1], fx) for k in range(6)]

    turned_cos = [[at_turbine(k, cosine[s : s + 1]) for s in range(2)] for k in range(6)]

    def spread(k, s):
        return jnp.where(along[k] == lane_x, turned_cos[k][s], 0.0)

    sub_column = lax.broadcasted_iota(jnp.int32, (depth, 1), 0)
    z_global = jnp.where(
        sub_column < zd + 4, p * zd + sub_column, p * zd + sub_column - depth
    )
    z_ok = (z_global >= 0) & (z_global < lax.axis_size("pen") * zd)

    def row_ok(r):
        y = g * rows + (r - 4)
        return z_ok & (y >= 0) & (y < n * rows)

    for body, edge, first, last, offset in (
        (1, 4, 0, 4, rows - 4),
        (0, 3, 4, rows + 4, -4),
        (2, 5, rows + 4, rows + 8, -(rows + 4)),
    ):
        values = [
            split2(jnp.concatenate([spread(body, s), spread(edge, s)], axis=0)) for s in range(2)
        ]
        z_body = lax.rem(index[body] // fx, zd)
        y_body = index[body] // (fx * zd)
        z_edge = lax.rem(index[edge] // fx, zd)
        y_edge = index[edge] // (fx * zd)
        z_edge = jnp.where(z_edge < 4, z_edge + zd, jnp.where(z_edge >= zd - 4, z_edge + 8, -1))
        for r in range(first, last):
            yl = r + offset
            hot_body = (sub_z == z_body) & (y_body == yl)
            hot_edge = (sub_z == z_edge) & (y_edge == yl)
            hot = jnp.concatenate([hot_body.astype(F32), hot_edge.astype(F32)], axis=1).astype(BF16)
            for s, field in ((0, c0), (1, c1)):
                hi, lo = values[s]
                total = dot(hot, lo) + dot(hot, hi)
                field[r] = jnp.where(row_ok(r), total, 0.0)

    lane_r = lane128 // 8
    lane_k = lane128 & 7
    y_side = g * rows + lane_r - 4
    side_ok = z_ok & (y_side >= 0) & (y_side < n * rows)
    y_edge = g * rows + jnp.where(lane128 < 64, -1, rows)
    edge_ok = z_ok & (y_edge >= 0) & (y_edge < n * rows)

    hots, packs = [], []
    slots = []
    for k in range(6):
        z_cell = lax.rem(index[k] // fx, zd)
        if k >= 3:
            z_cell = jnp.where(z_cell < 4, z_cell + zd, jnp.where(z_cell >= zd - 4, z_cell + 8, -1))
        hots.append((sub_z == z_cell).astype(F32))
        r_cell = turned[k][:, 0:1] // (fx * zd) - (-4, rows - 4, -(rows + 4))[k % 3]
        in_front = jnp.where(along[k] < NF, (r_cell - 4) * NF + along[k], -1)
        beside = jnp.where((along[k] >= 14) & (along[k] < 22), r_cell * 8 + along[k] - 14, -1)
        slots.append((in_front, beside))
        parts = []
        for s in range(2):
            if k % 3 == 0:
                parts.append(jnp.where(in_front == lane128, turned_cos[k][s], 0.0))
            else:
                parts.append(jnp.zeros((count, 128), F32))
            parts.append(jnp.where(beside == lane128, turned_cos[k][s], 0.0))
        packs.append(jnp.concatenate(parts, axis=1))
    hi, lo = split2(jnp.concatenate(packs, axis=0))
    hot = jnp.concatenate(hots, axis=1).astype(BF16)
    packed = dot(hot, lo) + dot(hot, hi)
    for k in range(4):
        part = packed[:, k * 128 : (k + 1) * 128]
        cp_ref[k] = jnp.where(side_ok if k % 2 else z_ok, part, 0.0)

    def far_wait(d, carry):
        far(d).wait()
        return carry

    for i in aside:
        copies[i].wait()

    lane_f = lax.broadcasted_iota(jnp.int32, (depth, fx), 1)

    for r in range(4, 12):
        w0[r] = jnp.where(z_ok, fp_ref[r], 0.0)

    def advance(field, upper_y, lower_y, behind, c):
        upper_z = pltpu.roll(field, depth - 1, 0)
        lower_z = pltpu.roll(field, 1, 0)
        slope_y = 0.5 * (upper_y - lower_y)
        slope_z = 0.5 * (upper_z - lower_z)
        square = slope_y * slope_y + slope_z * slope_z + SLOPE_EPS
        inverse = lax.rsqrt(square)
        viscosity = VISC_BASE + VISC_SLOPE * (square * inverse)
        laplacian = upper_y + lower_y + upper_z + lower_z - 4.0 * field
        moved = field - COURANT * (field - behind) + viscosity * laplacian
        share = (0.5 * VISC_SLOPE) * laplacian * inverse
        return moved - FORCE_GAIN * (c * c) * field, viscosity, share * slope_y, share * slope_z

    def forward(step, src, r, cos_field):
        field = src[r]
        behind = jnp.where(lane_f == 0, field, pltpu.roll(field, 1, 1))
        new, nu[step, r], ry[step, r], rz[step, r] = advance(
            field, src[r + 1], src[r - 1], behind, cos_field[r]
        )
        return new

    def power_slope(c, field):
        return (2.0 * POWER_GAIN) * (c * c * c) * field

    def yaw_term(c, field, value, new):
        return c * (2.0 * FORCE_GAIN * field * value - 3.0 * POWER_GAIN * c * new * new)

    for r in range(5, 11):
        new = forward(0, w0, r, c0)
        u1[r] = new
        w1[r] = jnp.where(row_ok(r), new, 0.0)
    for r in range(6, 10):
        new = forward(1, w1, r, c1)
        u2[r] = new
        lam[r] = power_slope(c1[r], new)
    @pl.when(g < n - 1)
    def _():
        for i in upward:
            copies[i].wait_send()
        for i in downward:
            copies[i].wait_recv()

    @pl.when(g > 0)
    def _():
        for i in downward:
            copies[i].wait_send()
        for i in upward:
            copies[i].wait_recv()

    side = jnp.zeros((depth, 128), F32)
    for r in range(16):
        side = jnp.where(lane_r == r, pltpu.roll(fp_ref[r, :, 0:128], (8 * r - 14) % 128, 1), side)
    side_ref[...] = side

    def spread_terms(step, r):
        value = lam[r]
        am[r] = value * nu[step, r]
        bm[r] = value * ry[step, r]

    def backward(step, r, cos_field):
        value = lam[r]
        a = am[r]
        b = value * rz[step, r]
        c = cos_field[r]
        ahead = jnp.where(lane_f == fx - 1, 0.0, pltpu.roll(value, fx - 1, 1))
        total = value * ((1.0 - COURANT) - FORCE_GAIN * (c * c)) + COURANT * ahead - 4.0 * a
        total = total + (am[r - 1] + bm[r - 1]) + (am[r + 1] - bm[r + 1])
        return total + pltpu.roll(a + b, 1, 0) + pltpu.roll(a - b, depth - 1, 0)

    for r in (0, 1, 2, 3, 12, 13, 14, 15):
        w0[r] = jnp.where(row_ok(r), fp_ref[r], 0.0)
    for r in (1, 2, 3, 4, 11, 12, 13, 14):
        new = forward(0, w0, r, c0)
        u1[r] = new
        w1[r] = jnp.where(row_ok(r), new, 0.0)
    for r in (2, 3, 4, 5, 10, 11, 12, 13):
        new = forward(1, w1, r, c1)
        u2[r] = new
        lam[r] = power_slope(c1[r], new)
    for r in range(4, rows + 4):
        gc1[r - 4] = yaw_term(c1[r], w1[r], lam[r], u2[r])[0:zd]
        farm_ref[r - 4] = u2[r][0:zd]
    for r in range(2, 14):
        spread_terms(1, r)
    for r in range(3, 13):
        value = backward(1, r, c1) + power_slope(c0[r], u1[r])
        u2[r] = jnp.where(row_ok(r), value, 0.0)
    for r in range(3, 13):
        lam[r] = u2[r]
    for r in range(4, rows + 4):
        gc0[r - 4] = yaw_term(c0[r], w0[r], lam[r], u1[r])[0:zd]
    flat = turned[0][:, 0:1] // fx
    take = (flat == lax.broadcasted_iota(jnp.int32, (count, rows * zd), 1)).astype(F32).astype(BF16)
    far_along = jnp.where(along[0] >= 18, along[0], -1)
    for s, terms in ((0, gc0), (1, gc1)):
        hi, lo = split2(terms[...].reshape(rows * zd, fx))
        lines = dot(take, lo) + dot(take, hi)
        value = jnp.where(far_along == lane_x, lines, 0.0)
        part_ref[s] = value[:, 0:128] + value[:, 128:256]

    lax.fori_loop(1, n, far_wait, 0)

    lax.fori_loop(1, n, rim_wait, 0)

    for i in range(6):
        flipped = rbody[i].T
        for h in range(2):
            k = h * 6 + i
            w_ref[k + odd * (11 - 2 * k), 0:zd] = flipped[h * zd : (h + 1) * zd]
    mated = g + 1 - 2 * odd
    lasts = [
        pltpu.make_async_remote_copy(
            src_ref=w_ref.at[8 + k, 0:zd], dst_ref=w_ref.at[15 - k, 0:zd],
            send_sem=edge_send.at[k], recv_sem=edge_recv.at[k],
            device_id={"grp": mated, "pen": p}, device_id_type=MESH,
        )
        for k in range(4)
    ]
    for last in lasts:
        last.start()
    rims = ebody[...].T
    for r in range(16):
        w_ref[r + odd * (15 - 2 * r), zd : zd + 8] = rims[8 * r : 8 * r + 8]

    for i in range(1, 11):
        vw1[i] = periodic_row(w_ref, i, False)
    for i in range(2, 10):
        vw2[i] = periodic_row(vw1, i, False)

    for last in lasts:
        last.wait()


    for i in range(11, 15):
        vw1[i] = periodic_row(w_ref, i, False)
    for i in range(10, 14):
        vw2[i] = periodic_row(vw1, i, False)

    def inlets(src, first, stop):
        hi, lo = split2(src[first:stop].reshape((stop - first) * depth, px))
        found = dot(jnp.concatenate([hi, lo], axis=1), pick_ref[...])
        front = jnp.zeros((depth, 128), F32)
        rim = front
        beside = front
        for r in range(first, stop):
            part = found[(r - first) * depth : (r - first + 1) * depth]
            row = r + odd * (15 - 2 * r)
            if 4 <= r < 12:
                front = jnp.where(lane128 // NF == row - 4, part[:, 0:128], front)
            elif r == 3:
                rim = jnp.where(lane128 // 64 == odd, part[:, 0:128], rim)
            elif r == 12:
                rim = jnp.where(lane128 // 64 == 1 - odd, part[:, 0:128], rim)
            beside = jnp.where(lane_r == row, part[:, 128:256], beside)
        return jnp.where(z_ok, front, 0.0), jnp.where(edge_ok, rim, 0.0), beside

    def front_step(field, rim, c):
        upper_y = jnp.where(lane128 >= 112, rim, pltpu.roll(field, 112, 1))
        lower_y = jnp.where(lane128 < 16, rim, pltpu.roll(field, 16, 1))
        behind = jnp.where((lane128 & 15) == 0, field, pltpu.roll(field, 1, 1))
        return advance(field, upper_y, lower_y, behind, c)[0]

    def side_step(field, c):
        return advance(field, pltpu.roll(field, 120, 1), pltpu.roll(field, 8, 1), pltpu.roll(field, 1, 1), c)

    def side_back(value, c, scale, slope_y, slope_z):
        a = value * scale
        b = value * slope_y
        d = value * slope_z
        total = value * ((1.0 - COURANT) - FORCE_GAIN * (c * c)) - 4.0 * a
        total = total + COURANT * pltpu.roll(value, 127, 1)
        total = total + pltpu.roll(a + b, 8, 1) + pltpu.roll(a - b, 120, 1)
        return total + pltpu.roll(a + d, 1, 0) + pltpu.roll(a - d, depth - 1, 0)

    front0, rim0, beside0 = inlets(vw1, 1, 15)
    front1, rim1, beside1 = inlets(vw2, 2, 14)
    cf0, cs0, cf1, cs1 = (cp_ref[k] for k in range(4))

    uf1 = front_step(front0, rim0, cf0)
    uf2 = front_step(front1, rim1, cf1)
    tf0 = yaw_term(cf0, front0, power_slope(cf0, uf1), uf1)
    tf1 = yaw_term(cf1, front1, power_slope(cf1, uf2), uf2)

    ws0 = jnp.where(side_ok, jnp.where(lane_k == 1, beside0, side_ref[...]), 0.0)
    us1, *back0 = side_step(ws0, cs0)
    ws1 = jnp.where(side_ok, jnp.where(lane_k == 1, beside1, us1), 0.0)
    us2, *back1 = side_step(ws1, cs1)
    value2 = power_slope(cs1, us2)
    value1 = jnp.where(side_ok, side_back(value2, cs1, *back1) + power_slope(cs0, us1), 0.0)
    ts0 = yaw_term(cs0, ws0, value1, us1)
    ts1 = yaw_term(cs1, ws1, value2, us2)

    terms = jnp.concatenate([tf0, ts0, tf1, ts1], axis=1)[0:zd]
    hi, lo = split2(terms)
    z_own = lax.rem(turned[0][:, 0:1] // fx, zd)
    take_z = (z_own == lax.broadcasted_iota(jnp.int32, (count, zd), 1)).astype(F32).astype(BF16)
    lines = dot(take_z, lo) + dot(take_z, hi)
    in_front = slots[0][0]
    beside = jnp.where((along[0] >= 16) & (along[0] < 18), slots[0][1], -1)
    total_a[g * m + p] = jnp.zeros(total_a.shape[1:], F32)
    mine = total_a.at[g * m + p]
    for s in range(2):
        value = part_ref[s] + jnp.where(in_front == lane128, lines[:, s * 256 : s * 256 + 128], 0.0)
        value = value + jnp.where(beside == lane128, lines[:, s * 256 + 128 : s * 256 + 256], 0.0)
        value = jnp.sum(value, axis=1, keepdims=True) * at_turbine(0, sine[s : s + 1])
        mine[s : s + 1, 0:TURB] = jnp.sum(
            jnp.where(turned[0][:, 1:2] == lane_t, value, 0.0), axis=0, keepdims=True
        )

    def near_copy(d):
        return pltpu.make_async_remote_copy(
            src_ref=total_a.at[g * m + p], dst_ref=total_a.at[g * m + p],
            send_sem=a_send.at[d], recv_sem=a_recv.at[d], device_id=peer(d), device_id_type=MESH,
        )

    def line_copy(d):
        return pltpu.make_async_remote_copy(
            src_ref=total_b.at[scen], dst_ref=total_b.at[scen],
            send_sem=b_send.at[d], recv_sem=b_recv.at[d], device_id=line(d), device_id_type=MESH,
        )

    def start(make):
        def run(d, carry):
            make(d).start()
            return carry

        return run

    def wait(make):
        def run(d, carry):
            make(d).wait()
            return carry

        return run

    lax.fori_loop(1, n * m, start(near_copy), 0)

    for r in range(3, 13):
        spread_terms(0, r)
    for r in range(4, rows + 4):
        sens_ref[r - 4] = backward(0, r, c0)[0:zd]

    ss = side_back(value1, cs0, *back0)

    us2, ss, uf2 = us2[0:zd], ss[0:zd], uf2[0:zd]
    for r in range(rows):
        shift = (-18 - 8 * r) % 128
        farm_ref[r, :, 0:128] = jnp.where(
            lane128 < NF, pltpu.roll(uf2, (-NF * r) % 128, 1),
            jnp.where(lane128 < 18, pltpu.roll(us2, shift, 1), farm_ref[r, :, 0:128]),
        )
        sens_ref[r, :, 0:128] = jnp.where(
            lane128 < NF, 0.0,
            jnp.where(lane128 < 18, pltpu.roll(ss, shift, 1), sens_ref[r, :, 0:128]),
        )

    for i in (5, 6, 8, 9):
        copies[i].wait()

    for i in range(1, planes + 3):
        v1[i] = periodic_row(vp_ref, i, True)
    for i in range(2, planes + 2):
        prec_ref[i - 2] = periodic_row(v1, i, True)[0:zd]

    lax.fori_loop(1, n * m, wait(near_copy), 0)
    total_b[scen] = jnp.sum(total_a[...], axis=0)
    lax.fori_loop(1, ns, start(line_copy), 0)
    lax.fori_loop(1, ns, wait(line_copy), 0)
    grad_ref[...] = jnp.sum(total_b[...], axis=0)[0 : grad_ref.shape[0], 0 : grad_ref.shape[1]]


def farm_steps(sizes, v, u, index, turbine, yaw, ps):
    planes, zd, fy = v.shape
    rows, _, fx = u.shape
    ns, n, m = sizes
    px = n * planes
    depth = zd + 8
    farm = pltpu.VMEM((16, depth, fx), F32)
    dma = pltpu.SemaphoreType.DMA
    return pl.pallas_call(
        functools.partial(farm_kernel, sizes),
        out_shape=(
            pltpu.VMEM(v.shape, F32),
            pltpu.VMEM(u.shape, F32),
            pltpu.VMEM(u.shape, F32),
            pltpu.VMEM(yaw.shape, F32),
        ),
        in_specs=[HBM] * 5 + [SMEM],
        out_specs=(VMEM,) * 4,
        scratch_shapes=[
            farm,
            pltpu.VMEM((planes + 4, depth, fy), F32),
            pltpu.VMEM((16, depth, px), F32),
            pltpu.VMEM((6, 8, index.shape[1]), jnp.int32),
            pltpu.VMEM(v.shape, F32),
            pltpu.VMEM(u.shape, F32),
            pltpu.VMEM((8, index.shape[1]), jnp.int32),
            pltpu.VMEM(index.shape, jnp.int32),
            pltpu.VMEM(turbine.shape, jnp.int32),
            pltpu.VMEM(yaw.shape, F32),
            dma((5,)),
            pltpu.VMEM((planes, 8, fy), F32),
            pltpu.VMEM((rows, 8, fx), F32),
            pltpu.VMEM((fy + 8, planes, 2 * zd), F32),
            pltpu.VMEM((6, px, 2 * zd), F32),
            pltpu.VMEM((n, planes, 128), F32),
            pltpu.VMEM((px, 128), F32),
            pltpu.VMEM((planes + 4, depth, fy), F32),
            pltpu.VMEM((16, depth, px), F32),
            pltpu.VMEM((16, depth, px), F32),
            farm, farm, farm, farm, farm, farm, farm,
            pltpu.VMEM((2, 16, depth, fx), F32),
            pltpu.VMEM((2, 16, depth, fx), F32),
            pltpu.VMEM((2, 16, depth, fx), F32),
            farm, farm,
            pltpu.VMEM(u.shape, F32),
            pltpu.VMEM(u.shape, F32),
            pltpu.VMEM((n * m, 2, 128), F32),
            pltpu.VMEM((ns, 2, 128), F32),
            pltpu.VMEM((2 * px, 256), BF16),
            pltpu.VMEM((4, depth, 128), F32),
            pltpu.VMEM((depth, 128), F32),
            pltpu.VMEM((2, index.shape[1], 128), F32),
            dma((15,)), dma((15,)), dma((n,)), dma((n,)), dma((n,)), dma((n,)), dma((4,)), dma((4,)),
            dma((n * m,)), dma((n * m,)), dma((ns,)), dma((ns,)),
        ],
        compiler_params=pltpu.CompilerParams(
            collective_id=0, has_side_effects=True, vmem_limit_bytes=56 * 1024 * 1024
        ),
        name="farm_steps",
    )(v, u, index, turbine, yaw, ps)


def finish_kernel(*refs):
    count = (len(refs) - 1) // 2
    sem = refs[-1]
    copies = [pltpu.make_async_copy(refs[i], refs[count + i], sem.at[i]) for i in range(count)]
    for copy in copies:
        copy.start()
    for copy in copies:
        copy.wait()


def finish(*arrays):
    return pl.pallas_call(
        finish_kernel,
        out_shape=tuple(jax.ShapeDtypeStruct(x.shape, F32) for x in arrays),
        in_specs=[VMEM] * len(arrays),
        out_specs=(HBM,) * len(arrays),
        scratch_shapes=[pltpu.SemaphoreType.DMA((len(arrays),))],
        name="finish",
    )(*[pltpu.with_memory_space_constraint(x, pltpu.VMEM) for x in arrays])


def shards(sizes, prec_state, farm_state, yaw_angles, plane_source, cell_index, cell_turbine):
    prec, farm, sens, yaw_grad = farm_steps(
        sizes, prec_state[0], farm_state[0], cell_index[0], cell_turbine[0], yaw_angles,
        plane_source,
    )
    prec, farm, sens, yaw_grad = finish(prec, farm, sens, yaw_grad)
    return (prec[None], farm[None], sens[None], yaw_grad)


def solution(mesh):
    spec = P("scen", "grp", "pen", None)
    in_specs = (spec, spec, P(), P(), P("grp", "pen", None), P("grp", "pen", None))
    out_specs = (spec, spec, spec, P())
    sizes = tuple(mesh.shape[axis] for axis in ("scen", "grp", "pen"))
    return jax.shard_map(
        functools.partial(shards, sizes), mesh=mesh, in_specs=in_specs, out_specs=out_specs,
        check_vma=False,
    )
```

```python
import functools

import jax
import jax.numpy as jnp
from jax import lax
from jax.experimental import pallas as pl
from jax.experimental.pallas import tpu as pltpu
from jax.sharding import PartitionSpec as P

NF = 16
TURB = 64
COURANT = 0.3
VISC_BASE = 0.03
VISC_SLOPE = 0.03
SLOPE_EPS = 0.01
FORCE_GAIN = 0.3
POWER_GAIN = 0.002

MESH = pl.DeviceIdType.MESH
VMEM = pl.BlockSpec(memory_space=pltpu.VMEM)
HBM = pl.BlockSpec(memory_space=pltpu.HBM)
SMEM = pl.BlockSpec(memory_space=pltpu.SMEM)
F32 = jnp.float32
BF16 = jnp.bfloat16


def split2(b):
    high = b.astype(BF16)
    return high, (b - high.astype(F32)).astype(BF16)


def dot(a, b):
    return jnp.dot(a, b, preferred_element_type=F32)


def advance_plane(centre, upper_a, lower_a, upper_z, lower_z, upper_l, lower_l, lower_x):
    slope_a = 0.5 * (upper_a - lower_a)
    slope_l = 0.5 * (upper_l - lower_l)
    slope_z = 0.5 * (upper_z - lower_z)
    viscosity = VISC_BASE + VISC_SLOPE * jnp.sqrt(
        slope_a * slope_a + slope_l * slope_l + slope_z * slope_z + SLOPE_EPS
    )
    laplacian = upper_a + lower_a + upper_l + lower_l + upper_z + lower_z - 6.0 * centre
    return centre - COURANT * (centre - lower_x) + viscosity * laplacian


def periodic_row(src, i, lead_is_x):
    centre = src[i]
    depth, lanes = centre.shape
    upper_l = pltpu.roll(centre, lanes - 1, 1)
    lower_l = pltpu.roll(centre, 1, 1)
    upper_z = pltpu.roll(centre, depth - 1, 0)
    lower_z = pltpu.roll(centre, 1, 0)
    upper_a = src[i + 1]
    lower_a = src[i - 1]
    lower_x = lower_a if lead_is_x else lower_l
    return advance_plane(centre, upper_a, lower_a, upper_z, lower_z, upper_l, lower_l, lower_x)


def farm_kernel(
    sizes, v_in, u_in, index_in, turbine_in, yaw_in, ps_ref,
    prec_ref, farm_ref, sens_ref, grad_ref,
    fp_ref, vp_ref, w_ref, cb_ref,
    v_ref, u_ref, cell_ref, index_ref, turbine_ref, yaw_ref, in_sem,
    vedge, uedge, bsend, rbody, esend, ebody,
    v1, vw1, vw2, c0, c1, w0, w1, u1, u2, lam, nu, ry, rz, am, bm, gc0, gc1, total_a, total_b,
    pick_ref, cp_ref, side_ref, part_ref,
    near_send, near_recv, far_send, far_recv, rim_send, rim_recv, edge_send, edge_recv, a_send, a_recv, b_send, b_recv,
):
    g = lax.axis_index("grp")
    p = lax.axis_index("pen")
    q = 1 - p
    ns, n, m = sizes
    up = lax.rem(g + 1, n)
    down = lax.rem(g + n - 1, n)
    odd = lax.rem(g, 2)
    planes, zd, fy = v_ref.shape
    rows, _, fx = u_ref.shape
    depth = zd + 8
    px = w_ref.shape[2]
    scen = lax.axis_index("scen")

    barrier = pltpu.get_barrier_semaphore()

    def peer(d):
        other = lax.rem(g * m + p + d, n * m)
        return {"grp": other // m, "pen": lax.rem(other, m)}

    def mate(d):
        return {"grp": lax.rem(g + d, n), "pen": p}

    def line(d):
        return {"scen": lax.rem(scen + d, ns), "grp": g, "pen": p}

    def greet(make):
        def run(d, carry):
            pl.semaphore_signal(barrier, inc=1, device_id=make(d), device_id_type=MESH)
            return carry

        return run

    lax.fori_loop(1, n, greet(mate), 0)
    for target in (g, up, down):
        pl.semaphore_signal(barrier, inc=1, device_id={"grp": target, "pen": q}, device_id_type=MESH)
    lax.fori_loop(1, ns, greet(line), 0)

    loads = [
        pltpu.make_async_copy(src, dst, in_sem.at[i])
        for i, (src, dst) in enumerate((
            (v_in, v_ref), (index_in, index_ref), (turbine_in, turbine_ref), (u_in, u_ref), (yaw_in, yaw_ref),
        ))
    ]
    for load in loads:
        load.start()
    loads[0].wait()

    vedge[:, 0:4] = v_ref[:, 0:4]
    vedge[:, 4:8] = v_ref[:, zd - 4 : zd]
    for x in range(planes):
        plane = v_ref[x]
        both = jnp.concatenate([plane, pltpu.roll(plane, fy - 6, 1)], axis=0).T
        bsend[4 : fy + 4, x, :] = both
        bsend[0:4, x, :] = both[fy - 4 : fy]
        bsend[fy + 4 : fy + 8, x, :] = both[0:4]

    for load in loads[1:]:
        load.wait()
    uedge[:, 0:4] = u_ref[:, 0:4]
    uedge[:, 4:8] = u_ref[:, zd - 4 : zd]
    cell_ref[...] = jnp.zeros_like(cell_ref)
    cell_ref[0:1] = index_ref[...]
    cell_ref[1:2] = turbine_ref[...]

    pl.semaphore_wait(barrier, (n - 1) + 3 + (ns - 1))

    def far(d):
        target = lax.rem(g + d, n)
        return pltpu.make_async_remote_copy(
            src_ref=bsend.at[pl.ds(target * 8 + 4 * lax.rem(target, 2), 6)],
            dst_ref=rbody.at[:, pl.ds(g * planes, planes)],
            send_sem=far_send.at[d],
            recv_sem=far_recv.at[d],
            device_id={"grp": target, "pen": p},
            device_id_type=MESH,
        )

    def far_start(d, carry):
        far(d).start()
        return carry


    moves = [
        (u_ref.at[rows - 4 : rows], fp_ref.at[0:4, 0:zd], up, p),
        (u_ref.at[0:4], fp_ref.at[rows + 4 : rows + 8, 0:zd], down, p),
        (uedge, fp_ref.at[4 : rows + 4, zd : zd + 8], g, q),
        (uedge.at[rows - 4 : rows], fp_ref.at[0:4, zd : zd + 8], up, q),
        (uedge.at[0:4], fp_ref.at[rows + 4 : rows + 8, zd : zd + 8], down, q),
        (v_ref.at[planes - 2 : planes], vp_ref.at[0:2, 0:zd], up, p),
        (v_ref.at[0:2], vp_ref.at[planes + 2 : planes + 4, 0:zd], down, p),
        (vedge, vp_ref.at[2 : planes + 2, zd : zd + 8], g, q),
        (vedge.at[planes - 2 : planes], vp_ref.at[0:2, zd : zd + 8], up, q),
        (vedge.at[0:2], vp_ref.at[planes + 2 : planes + 4, zd : zd + 8], down, q),
        (cell_ref, cb_ref.at[1], up, p),
        (cell_ref, cb_ref.at[2], down, p),
        (cell_ref, cb_ref.at[3], g, q),
        (cell_ref, cb_ref.at[4], up, q),
        (cell_ref, cb_ref.at[5], down, q),
    ]
    copies = [
        pltpu.make_async_remote_copy(
            src_ref=src, dst_ref=dst, send_sem=near_send.at[i], recv_sem=near_recv.at[i],
            device_id={"grp": tg, "pen": tp}, device_id_type=MESH,
        )
        for i, (src, dst, tg, tp) in enumerate(moves)
    ]
    upward, downward, aside = (0, 3), (1, 4), (2,)
    copies[7].start()
    for i in range(10, 15):
        copies[i].start()
    for i in aside:
        copies[i].start()
    @pl.when(g < n - 1)
    def _():
        for i in upward:
            copies[i].start()

    @pl.when(g > 0)
    def _():
        for i in downward:
            copies[i].start()

    lax.fori_loop(n // 4, n - n // 4 + 1, far_start, 0)

    def rim_copy(d):
        target = lax.rem(g + d, n)
        return pltpu.make_async_remote_copy(
            src_ref=esend.at[target], dst_ref=ebody.at[pl.ds(g * planes, planes)],
            send_sem=rim_send.at[d], recv_sem=rim_recv.at[d],
            device_id={"grp": target, "pen": p}, device_id_type=MESH,
        )

    def rim_start(d, carry):
        rim_copy(d).start()
        return carry

    def rim_wait(d, carry):
        rim_copy(d).wait()
        return carry

    copies[7].wait()
    for x in range(planes):
        edge = vp_ref[x + 2, zd : zd + 8]
        tall = jnp.concatenate(
            [edge if i == 4 else pltpu.roll(edge, (4 - i) % fy, 1) for i in range(16)], axis=0
        ).T
        esend[:, x, :] = tall.reshape(n, rows, 128)[:, 0]
    lax.fori_loop(1, n, rim_start, 0)
    lax.fori_loop(n - n // 4 + 1, n, far_start, 0)
    lax.fori_loop(1, n // 4, far_start, 0)

    ebody[pl.ds(g * planes, planes)] = esend[g]
    fp_ref[4 : rows + 4, 0:zd] = u_ref[...]
    vp_ref[2 : planes + 2, 0:zd] = v_ref[...]
    cb_ref[0] = cell_ref[...]
    rbody[:, pl.ds(g * planes, planes)] = bsend[pl.ds(g * 8 + 4 * odd, 6)]

    for i in range(10, 15):
        copies[i].wait()

    lane128 = lax.broadcasted_iota(jnp.int32, (1, 128), 1)
    wanted = jnp.full((1, 128), -1, jnp.int32)
    for j in range(NF):
        wanted = jnp.where((lane128 & (NF - 1)) == j, ps_ref[j], wanted)
    sub_x = lax.broadcasted_iota(jnp.int32, (px, 128), 0)
    pick = jnp.concatenate(
        [(sub_x == wanted).astype(F32), (sub_x == ps_ref[NF - 1]).astype(F32)], axis=1
    ).astype(BF16)
    pick_ref[0:px] = pick
    pick_ref[px : 2 * px] = pick

    cosine = jnp.cos(yaw_ref[...])
    sine = jnp.sin(yaw_ref[...])
    index = [cb_ref[k, 0:1, :] for k in range(6)]
    turned = [cb_ref[k].T for k in range(6)]
    count = index[0].shape[1]
    lane_t = lax.broadcasted_iota(jnp.int32, (count, TURB), 1)

    def at_turbine(k, table):
        return jnp.sum(jnp.where(turned[k][:, 1:2] == lane_t, table, 0.0), axis=1, keepdims=True)

    lane_x = lax.broadcasted_iota(jnp.int32, (count, fx), 1)
    sub_z = lax.broadcasted_iota(jnp.int32, (depth, count), 0)
    along = [lax.rem(turned[k][:, 0:1], fx) for k in range(6)]

    turned_cos = [[at_turbine(k, cosine[s : s + 1]) for s in range(2)] for k in range(6)]

    def spread(k, s):
        return jnp.where(along[k] == lane_x, turned_cos[k][s], 0.0)

    sub_column = lax.broadcasted_iota(jnp.int32, (depth, 1), 0)
    z_global = jnp.where(
        sub_column < zd + 4, p * zd + sub_column, p * zd + sub_column - depth
    )
    z_ok = (z_global >= 0) & (z_global < lax.axis_size("pen") * zd)

    def row_ok(r):
        y = g * rows + (r - 4)
        return z_ok & (y >= 0) & (y < n * rows)

    for body, edge, first, last, offset in (
        (1, 4, 0, 4, rows - 4),
        (0, 3, 4, rows + 4, -4),
        (2, 5, rows + 4, rows + 8, -(rows + 4)),
    ):
        values = [
            split2(jnp.concatenate([spread(body, s), spread(edge, s)], axis=0)) for s in range(2)
        ]
        z_body = lax.rem(index[body] // fx, zd)
        y_body = index[body] // (fx * zd)
        z_edge = lax.rem(index[edge] // fx, zd)
        y_edge = index[edge] // (fx * zd)
        z_edge = jnp.where(z_edge < 4, z_edge + zd, jnp.where(z_edge >= zd - 4, z_edge + 8, -1))
        for r in range(first, last):
            yl = r + offset
            hot_body = (sub_z == z_body) & (y_body == yl)
            hot_edge = (sub_z == z_edge) & (y_edge == yl)
            hot = jnp.concatenate([hot_body.astype(F32), hot_edge.astype(F32)], axis=1).astype(BF16)
            for s, field in ((0, c0), (1, c1)):
                hi, lo = values[s]
                total = dot(hot, lo) + dot(hot, hi)
                field[r] = jnp.where(row_ok(r), total, 0.0)

    lane_r = lane128 // 8
    lane_k = lane128 & 7
    y_side = g * rows + lane_r - 4
    side_ok = z_ok & (y_side >= 0) & (y_side < n * rows)
    y_edge = g * rows + jnp.where(lane128 < 64, -1, rows)
    edge_ok = z_ok & (y_edge >= 0) & (y_edge < n * rows)

    hots, packs = [], []
    slots = []
    for k in range(6):
        z_cell = lax.rem(index[k] // fx, zd)
        if k >= 3:
            z_cell = jnp.where(z_cell < 4, z_cell + zd, jnp.where(z_cell >= zd - 4, z_cell + 8, -1))
        hots.append((sub_z == z_cell).astype(F32))
        r_cell = turned[k][:, 0:1] // (fx * zd) - (-4, rows - 4, -(rows + 4))[k % 3]
        in_front = jnp.where(along[k] < NF, (r_cell - 4) * NF + along[k], -1)
        beside = jnp.where((along[k] >= 14) & (along[k] < 22), r_cell * 8 + along[k] - 14, -1)
        slots.append((in_front, beside))
        parts = []
        for s in range(2):
            if k % 3 == 0:
                parts.append(jnp.where(in_front == lane128, turned_cos[k][s], 0.0))
            else:
                parts.append(jnp.zeros((count, 128), F32))
            parts.append(jnp.where(beside == lane128, turned_cos[k][s], 0.0))
        packs.append(jnp.concatenate(parts, axis=1))
    hi, lo = split2(jnp.concatenate(packs, axis=0))
    hot = jnp.concatenate(hots, axis=1).astype(BF16)
    packed = dot(hot, lo) + dot(hot, hi)
    for k in range(4):
        part = packed[:, k * 128 : (k + 1) * 128]
        cp_ref[k] = jnp.where(side_ok if k % 2 else z_ok, part, 0.0)

    def far_wait(d, carry):
        far(d).wait()
        return carry

    for i in aside:
        copies[i].wait()

    lane_f = lax.broadcasted_iota(jnp.int32, (depth, fx), 1)

    for r in range(4, 12):
        w0[r] = jnp.where(z_ok, fp_ref[r], 0.0)

    def advance(field, upper_y, lower_y, behind, c):
        upper_z = pltpu.roll(field, depth - 1, 0)
        lower_z = pltpu.roll(field, 1, 0)
        slope_y = 0.5 * (upper_y - lower_y)
        slope_z = 0.5 * (upper_z - lower_z)
        square = slope_y * slope_y + slope_z * slope_z + SLOPE_EPS
        inverse = lax.rsqrt(square)
        viscosity = VISC_BASE + VISC_SLOPE * (square * inverse)
        laplacian = upper_y + lower_y + upper_z + lower_z - 4.0 * field
        moved = field - COURANT * (field - behind) + viscosity * laplacian
        share = (0.5 * VISC_SLOPE) * laplacian * inverse
        return moved - FORCE_GAIN * (c * c) * field, viscosity, share * slope_y, share * slope_z

    def forward(step, src, r, cos_field):
        field = src[r]
        behind = jnp.where(lane_f == 0, field, pltpu.roll(field, 1, 1))
        new, nu[step, r], ry[step, r], rz[step, r] = advance(
            field, src[r + 1], src[r - 1], behind, cos_field[r]
        )
        return new

    def power_slope(c, field):
        return (2.0 * POWER_GAIN) * (c * c * c) * field

    def yaw_term(c, field, value, new):
        return c * (2.0 * FORCE_GAIN * field * value - 3.0 * POWER_GAIN * c * new * new)

    for r in range(5, 11):
        new = forward(0, w0, r, c0)
        u1[r] = new
        w1[r] = jnp.where(row_ok(r), new, 0.0)
    for r in range(6, 10):
        new = forward(1, w1, r, c1)
        u2[r] = new
        lam[r] = power_slope(c1[r], new)
    @pl.when(g < n - 1)
    def _():
        for i in upward:
            copies[i].wait_send()
        for i in downward:
            copies[i].wait_recv()

    @pl.when(g > 0)
    def _():
        for i in downward:
            copies[i].wait_send()
        for i in upward:
            copies[i].wait_recv()

    side = jnp.zeros((depth, 128), F32)
    for r in range(16):
        side = jnp.where(lane_r == r, pltpu.roll(fp_ref[r, :, 0:128], (8 * r - 14) % 128, 1), side)
    side_ref[...] = side

    def spread_terms(step, r):
        value = lam[r]
        am[r] = value * nu[step, r]
        bm[r] = value * ry[step, r]

    def backward(step, r, cos_field):
        value = lam[r]
        a = am[r]
        b = value * rz[step, r]
        c = cos_field[r]
        ahead = jnp.where(lane_f == fx - 1, 0.0, pltpu.roll(value, fx - 1, 1))
        total = value * ((1.0 - COURANT) - FORCE_GAIN * (c * c)) + COURANT * ahead - 4.0 * a
        total = total + (am[r - 1] + bm[r - 1]) + (am[r + 1] - bm[r + 1])
        return total + pltpu.roll(a + b, 1, 0) + pltpu.roll(a - b, depth - 1, 0)

    for r in (0, 1, 2, 3, 12, 13, 14, 15):
        w0[r] = jnp.where(row_ok(r), fp_ref[r], 0.0)
    for r in (1, 2, 3, 4, 11, 12, 13, 14):
        new = forward(0, w0, r, c0)
        u1[r] = new
        w1[r] = jnp.where(row_ok(r), new, 0.0)
    for r in (2, 3, 4, 5, 10, 11, 12, 13):
        new = forward(1, w1, r, c1)
        u2[r] = new
        lam[r] = power_slope(c1[r], new)
    for r in range(4, rows + 4):
        gc1[r - 4] = yaw_term(c1[r], w1[r], lam[r], u2[r])[0:zd]
        farm_ref[r - 4] = u2[r][0:zd]
    for r in range(2, 14):
        spread_terms(1, r)
    for r in range(3, 13):
        value = backward(1, r, c1) + power_slope(c0[r], u1[r])
        u2[r] = jnp.where(row_ok(r), value, 0.0)
    for r in range(3, 13):
        lam[r] = u2[r]
    for r in range(4, rows + 4):
        gc0[r - 4] = yaw_term(c0[r], w0[r], lam[r], u1[r])[0:zd]
    flat = turned[0][:, 0:1] // fx
    take = (flat == lax.broadcasted_iota(jnp.int32, (count, rows * zd), 1)).astype(F32).astype(BF16)
    far_along = jnp.where(along[0] >= 18, along[0], -1)
    for s, terms in ((0, gc0), (1, gc1)):
        hi, lo = split2(terms[...].reshape(rows * zd, fx))
        lines = dot(take, lo) + dot(take, hi)
        value = jnp.where(far_along == lane_x, lines, 0.0)
        part_ref[s] = value[:, 0:128] + value[:, 128:256]

    lax.fori_loop(1, n, far_wait, 0)

    lax.fori_loop(1, n, rim_wait, 0)

    for i in range(6):
        flipped = rbody[i].T
        for h in range(2):
            k = h * 6 + i
            w_ref[k + odd * (11 - 2 * k), 0:zd] = flipped[h * zd : (h + 1) * zd]
    mated = g + 1 - 2 * odd
    lasts = [
        pltpu.make_async_remote_copy(
            src_ref=w_ref.at[8 + k, 0:zd], dst_ref=w_ref.at[15 - k, 0:zd],
            send_sem=edge_send.at[k], recv_sem=edge_recv.at[k],
            device_id={"grp": mated, "pen": p}, device_id_type=MESH,
        )
        for k in range(4)
    ]
    for last in lasts:
        last.start()
    for i in (5, 6, 8, 9):
        copies[i].start()

    rims = ebody[...].T
    for r in range(16):
        w_ref[r + odd * (15 - 2 * r), zd : zd + 8] = rims[8 * r : 8 * r + 8]

    for i in range(1, 11):
        vw1[i] = periodic_row(w_ref, i, False)
    for i in range(2, 10):
        vw2[i] = periodic_row(vw1, i, False)

    for last in lasts:
        last.wait()


    for i in range(11, 15):
        vw1[i] = periodic_row(w_ref, i, False)
    for i in range(10, 14):
        vw2[i] = periodic_row(vw1, i, False)

    def inlets(src, first, stop):
        hi, lo = split2(src[first:stop].reshape((stop - first) * depth, px))
        found = dot(jnp.concatenate([hi, lo], axis=1), pick_ref[...])
        front = jnp.zeros((depth, 128), F32)
        rim = front
        beside = front
        for r in range(first, stop):
            part = found[(r - first) * depth : (r - first + 1) * depth]
            row = r + odd * (15 - 2 * r)
            if 4 <= r < 12:
                front = jnp.where(lane128 // NF == row - 4, part[:, 0:128], front)
            elif r == 3:
                rim = jnp.where(lane128 // 64 == odd, part[:, 0:128], rim)
            elif r == 12:
                rim = jnp.where(lane128 // 64 == 1 - odd, part[:, 0:128], rim)
            beside = jnp.where(lane_r == row, part[:, 128:256], beside)
        return jnp.where(z_ok, front, 0.0), jnp.where(edge_ok, rim, 0.0), beside

    def front_step(field, rim, c):
        upper_y = jnp.where(lane128 >= 112, rim, pltpu.roll(field, 112, 1))
        lower_y = jnp.where(lane128 < 16, rim, pltpu.roll(field, 16, 1))
        behind = jnp.where((lane128 & 15) == 0, field, pltpu.roll(field, 1, 1))
        return advance(field, upper_y, lower_y, behind, c)[0]

    def side_step(field, c):
        return advance(field, pltpu.roll(field, 120, 1), pltpu.roll(field, 8, 1), pltpu.roll(field, 1, 1), c)

    def side_back(value, c, scale, slope_y, slope_z):
        a = value * scale
        b = value * slope_y
        d = value * slope_z
        total = value * ((1.0 - COURANT) - FORCE_GAIN * (c * c)) - 4.0 * a
        total = total + COURANT * pltpu.roll(value, 127, 1)
        total = total + pltpu.roll(a + b, 8, 1) + pltpu.roll(a - b, 120, 1)
        return total + pltpu.roll(a + d, 1, 0) + pltpu.roll(a - d, depth - 1, 0)

    front0, rim0, beside0 = inlets(vw1, 1, 15)
    front1, rim1, beside1 = inlets(vw2, 2, 14)
    cf0, cs0, cf1, cs1 = (cp_ref[k] for k in range(4))

    uf1 = front_step(front0, rim0, cf0)
    uf2 = front_step(front1, rim1, cf1)
    tf0 = yaw_term(cf0, front0, power_slope(cf0, uf1), uf1)
    tf1 = yaw_term(cf1, front1, power_slope(cf1, uf2), uf2)

    ws0 = jnp.where(side_ok, jnp.where(lane_k == 1, beside0, side_ref[...]), 0.0)
    us1, *back0 = side_step(ws0, cs0)
    ws1 = jnp.where(side_ok, jnp.where(lane_k == 1, beside1, us1), 0.0)
    us2, *back1 = side_step(ws1, cs1)
    value2 = power_slope(cs1, us2)
    value1 = jnp.where(side_ok, side_back(value2, cs1, *back1) + power_slope(cs0, us1), 0.0)
    ts0 = yaw_term(cs0, ws0, value1, us1)
    ts1 = yaw_term(cs1, ws1, value2, us2)

    terms = jnp.concatenate([tf0, ts0, tf1, ts1], axis=1)[0:zd]
    hi, lo = split2(terms)
    z_own = lax.rem(turned[0][:, 0:1] // fx, zd)
    take_z = (z_own == lax.broadcasted_iota(jnp.int32, (count, zd), 1)).astype(F32).astype(BF16)
    lines = dot(take_z, lo) + dot(take_z, hi)
    in_front = slots[0][0]
    beside = jnp.where((along[0] >= 16) & (along[0] < 18), slots[0][1], -1)
    total_a[g * m + p] = jnp.zeros(total_a.shape[1:], F32)
    mine = total_a.at[g * m + p]
    for s in range(2):
        value = part_ref[s] + jnp.where(in_front == lane128, lines[:, s * 256 : s * 256 + 128], 0.0)
        value = value + jnp.where(beside == lane128, lines[:, s * 256 + 128 : s * 256 + 256], 0.0)
        value = jnp.sum(value, axis=1, keepdims=True) * at_turbine(0, sine[s : s + 1])
        mine[s : s + 1, 0:TURB] = jnp.sum(
            jnp.where(turned[0][:, 1:2] == lane_t, value, 0.0), axis=0, keepdims=True
        )

    def near_copy(d):
        return pltpu.make_async_remote_copy(
            src_ref=total_a.at[g * m + p], dst_ref=total_a.at[g * m + p],
            send_sem=a_send.at[d], recv_sem=a_recv.at[d], device_id=peer(d), device_id_type=MESH,
        )

    def line_copy(d):
        return pltpu.make_async_remote_copy(
            src_ref=total_b.at[scen], dst_ref=total_b.at[scen],
            send_sem=b_send.at[d], recv_sem=b_recv.at[d], device_id=line(d), device_id_type=MESH,
        )

    def start(make):
        def run(d, carry):
            make(d).start()
            return carry

        return run

    def wait(make):
        def run(d, carry):
            make(d).wait()
            return carry

        return run

    lax.fori_loop(1, n * m, start(near_copy), 0)

    for r in range(3, 13):
        spread_terms(0, r)
    for r in range(4, rows + 4):
        sens_ref[r - 4] = backward(0, r, c0)[0:zd]

    ss = side_back(value1, cs0, *back0)

    us2, ss, uf2 = us2[0:zd], ss[0:zd], uf2[0:zd]
    for r in range(rows):
        shift = (-18 - 8 * r) % 128
        farm_ref[r, :, 0:128] = jnp.where(
            lane128 < NF, pltpu.roll(uf2, (-NF * r) % 128, 1),
            jnp.where(lane128 < 18, pltpu.roll(us2, shift, 1), farm_ref[r, :, 0:128]),
        )
        sens_ref[r, :, 0:128] = jnp.where(
            lane128 < NF, 0.0,
            jnp.where(lane128 < 18, pltpu.roll(ss, shift, 1), sens_ref[r, :, 0:128]),
        )

    for i in (5, 6, 8, 9):
        copies[i].wait()

    for i in range(1, planes + 3):
        v1[i] = periodic_row(vp_ref, i, True)
    for i in range(2, planes + 2):
        prec_ref[i - 2] = periodic_row(v1, i, True)[0:zd]

    lax.fori_loop(1, n * m, wait(near_copy), 0)
    total_b[scen] = jnp.sum(total_a[...], axis=0)
    lax.fori_loop(1, ns, start(line_copy), 0)
    lax.fori_loop(1, ns, wait(line_copy), 0)
    grad_ref[...] = jnp.sum(total_b[...], axis=0)[0 : grad_ref.shape[0], 0 : grad_ref.shape[1]]


def farm_steps(sizes, v, u, index, turbine, yaw, ps):
    planes, zd, fy = v.shape
    rows, _, fx = u.shape
    ns, n, m = sizes
    px = n * planes
    depth = zd + 8
    farm = pltpu.VMEM((16, depth, fx), F32)
    dma = pltpu.SemaphoreType.DMA
    return pl.pallas_call(
        functools.partial(farm_kernel, sizes),
        out_shape=(
            pltpu.VMEM(v.shape, F32),
            pltpu.VMEM(u.shape, F32),
            pltpu.VMEM(u.shape, F32),
            pltpu.VMEM(yaw.shape, F32),
        ),
        in_specs=[HBM] * 5 + [SMEM],
        out_specs=(VMEM,) * 4,
        scratch_shapes=[
            farm,
            pltpu.VMEM((planes + 4, depth, fy), F32),
            pltpu.VMEM((16, depth, px), F32),
            pltpu.VMEM((6, 8, index.shape[1]), jnp.int32),
            pltpu.VMEM(v.shape, F32),
            pltpu.VMEM(u.shape, F32),
            pltpu.VMEM((8, index.shape[1]), jnp.int32),
            pltpu.VMEM(index.shape, jnp.int32),
            pltpu.VMEM(turbine.shape, jnp.int32),
            pltpu.VMEM(yaw.shape, F32),
            dma((5,)),
            pltpu.VMEM((planes, 8, fy), F32),
            pltpu.VMEM((rows, 8, fx), F32),
            pltpu.VMEM((fy + 8, planes, 2 * zd), F32),
            pltpu.VMEM((6, px, 2 * zd), F32),
            pltpu.VMEM((n, planes, 128), F32),
            pltpu.VMEM((px, 128), F32),
            pltpu.VMEM((planes + 4, depth, fy), F32),
            pltpu.VMEM((16, depth, px), F32),
            pltpu.VMEM((16, depth, px), F32),
            farm, farm, farm, farm, farm, farm, farm,
            pltpu.VMEM((2, 16, depth, fx), F32),
            pltpu.VMEM((2, 16, depth, fx), F32),
            pltpu.VMEM((2, 16, depth, fx), F32),
            farm, farm,
            pltpu.VMEM(u.shape, F32),
            pltpu.VMEM(u.shape, F32),
            pltpu.VMEM((n * m, 2, 128), F32),
            pltpu.VMEM((ns, 2, 128), F32),
            pltpu.VMEM((2 * px, 256), BF16),
            pltpu.VMEM((4, depth, 128), F32),
            pltpu.VMEM((depth, 128), F32),
            pltpu.VMEM((2, index.shape[1], 128), F32),
            dma((15,)), dma((15,)), dma((n,)), dma((n,)), dma((n,)), dma((n,)), dma((4,)), dma((4,)),
            dma((n * m,)), dma((n * m,)), dma((ns,)), dma((ns,)),
        ],
        compiler_params=pltpu.CompilerParams(
            collective_id=0, has_side_effects=True, vmem_limit_bytes=56 * 1024 * 1024
        ),
        name="farm_steps",
    )(v, u, index, turbine, yaw, ps)


def finish_kernel(*refs):
    count = (len(refs) - 1) // 2
    sem = refs[-1]
    copies = [pltpu.make_async_copy(refs[i], refs[count + i], sem.at[i]) for i in range(count)]
    for copy in copies:
        copy.start()
    for copy in copies:
        copy.wait()


def finish(*arrays):
    return pl.pallas_call(
        finish_kernel,
        out_shape=tuple(jax.ShapeDtypeStruct(x.shape, F32) for x in arrays),
        in_specs=[VMEM] * len(arrays),
        out_specs=(HBM,) * len(arrays),
        scratch_shapes=[pltpu.SemaphoreType.DMA((len(arrays),))],
        name="finish",
    )(*[pltpu.with_memory_space_constraint(x, pltpu.VMEM) for x in arrays])


def shards(sizes, prec_state, farm_state, yaw_angles, plane_source, cell_index, cell_turbine):
    prec, farm, sens, yaw_grad = farm_steps(
        sizes, prec_state[0], farm_state[0], cell_index[0], cell_turbine[0], yaw_angles,
        plane_source,
    )
    prec, farm, sens, yaw_grad = finish(prec, farm, sens, yaw_grad)
    return (prec[None], farm[None], sens[None], yaw_grad)


def solution(mesh):
    spec = P("scen", "grp", "pen", None)
    in_specs = (spec, spec, P(), P(), P("grp", "pen", None), P("grp", "pen", None))
    out_specs = (spec, spec, spec, P())
    sizes = tuple(mesh.shape[axis] for axis in ("scen", "grp", "pen"))
    return jax.shard_map(
        functools.partial(shards, sizes), mesh=mesh, in_specs=in_specs, out_specs=out_specs,
        check_vma=False,
    )
```

```python
import functools

import jax
import jax.numpy as jnp
from jax import lax
from jax.experimental import pallas as pl
from jax.experimental.pallas import tpu as pltpu
from jax.sharding import PartitionSpec as P

NF = 16
TURB = 64
COURANT = 0.3
VISC_BASE = 0.03
VISC_SLOPE = 0.03
SLOPE_EPS = 0.01
FORCE_GAIN = 0.3
POWER_GAIN = 0.002

MESH = pl.DeviceIdType.MESH
VMEM = pl.BlockSpec(memory_space=pltpu.VMEM)
HBM = pl.BlockSpec(memory_space=pltpu.HBM)
SMEM = pl.BlockSpec(memory_space=pltpu.SMEM)
F32 = jnp.float32
BF16 = jnp.bfloat16


def split2(b):
    high = b.astype(BF16)
    return high, (b - high.astype(F32)).astype(BF16)


def dot(a, b):
    return jnp.dot(a, b, preferred_element_type=F32)


def advance_plane(centre, upper_a, lower_a, upper_z, lower_z, upper_l, lower_l, lower_x):
    slope_a = 0.5 * (upper_a - lower_a)
    slope_l = 0.5 * (upper_l - lower_l)
    slope_z = 0.5 * (upper_z - lower_z)
    viscosity = VISC_BASE + VISC_SLOPE * jnp.sqrt(
        slope_a * slope_a + slope_l * slope_l + slope_z * slope_z + SLOPE_EPS
    )
    laplacian = upper_a + lower_a + upper_l + lower_l + upper_z + lower_z - 6.0 * centre
    return centre - COURANT * (centre - lower_x) + viscosity * laplacian


def periodic_row(src, i, lead_is_x):
    centre = src[i]
    depth, lanes = centre.shape
    upper_l = pltpu.roll(centre, lanes - 1, 1)
    lower_l = pltpu.roll(centre, 1, 1)
    upper_z = pltpu.roll(centre, depth - 1, 0)
    lower_z = pltpu.roll(centre, 1, 0)
    upper_a = src[i + 1]
    lower_a = src[i - 1]
    lower_x = lower_a if lead_is_x else lower_l
    return advance_plane(centre, upper_a, lower_a, upper_z, lower_z, upper_l, lower_l, lower_x)


def farm_kernel(
    sizes, v_in, u_in, index_in, turbine_in, yaw_in, ps_ref,
    prec_ref, farm_ref, sens_ref, grad_ref,
    fp_ref, vp_ref, w_ref, cb_ref,
    v_ref, u_ref, cell_ref, index_ref, turbine_ref, yaw_ref, in_sem,
    vedge, uedge, bsend, rbody, esend, ebody,
    v1, vw1, vw2, c0, c1, w0, w1, u1, u2, lam, nu, ry, rz, am, bm, gc0, gc1, total_a, total_b,
    pick_ref, cp_ref, side_ref, part_ref,
    near_send, near_recv, far_send, far_recv, rim_send, rim_recv, edge_send, edge_recv, a_send, a_recv, b_send, b_recv,
):
    g = lax.axis_index("grp")
    p = lax.axis_index("pen")
    q = 1 - p
    ns, n, m = sizes
    up = lax.rem(g + 1, n)
    down = lax.rem(g + n - 1, n)
    odd = lax.rem(g, 2)
    planes, zd, fy = v_ref.shape
    rows, _, fx = u_ref.shape
    depth = zd + 8
    px = w_ref.shape[2]
    scen = lax.axis_index("scen")

    barrier = pltpu.get_barrier_semaphore()

    def peer(d):
        other = lax.rem(g * m + p + d, n * m)
        return {"grp": other // m, "pen": lax.rem(other, m)}

    def mate(d):
        return {"grp": lax.rem(g + d, n), "pen": p}

    def line(d):
        return {"scen": lax.rem(scen + d, ns), "grp": g, "pen": p}

    def greet(make):
        def run(d, carry):
            pl.semaphore_signal(barrier, inc=1, device_id=make(d), device_id_type=MESH)
            return carry

        return run

    lax.fori_loop(1, n, greet(mate), 0)
    for target in (g, up, down):
        pl.semaphore_signal(barrier, inc=1, device_id={"grp": target, "pen": q}, device_id_type=MESH)
    lax.fori_loop(1, ns, greet(line), 0)

    loads = [
        pltpu.make_async_copy(src, dst, in_sem.at[i])
        for i, (src, dst) in enumerate((
            (v_in, v_ref), (index_in, index_ref), (turbine_in, turbine_ref), (u_in, u_ref), (yaw_in, yaw_ref),
        ))
    ]
    for load in loads:
        load.start()
    loads[0].wait()

    vedge[:, 0:4] = v_ref[:, 0:4]
    vedge[:, 4:8] = v_ref[:, zd - 4 : zd]
    for x in range(planes):
        plane = v_ref[x]
        both = jnp.concatenate([plane, pltpu.roll(plane, fy - 6, 1)], axis=0).T
        bsend[4 : fy + 4, x, :] = both
        bsend[0:4, x, :] = both[fy - 4 : fy]
        bsend[fy + 4 : fy + 8, x, :] = both[0:4]

    for load in loads[1:]:
        load.wait()
    uedge[:, 0:4] = u_ref[:, 0:4]
    uedge[:, 4:8] = u_ref[:, zd - 4 : zd]
    cell_ref[...] = jnp.zeros_like(cell_ref)
    cell_ref[0:1] = index_ref[...]
    cell_ref[1:2] = turbine_ref[...]

    pl.semaphore_wait(barrier, (n - 1) + 3 + (ns - 1))

    def far(d):
        target = lax.rem(g + d, n)
        return pltpu.make_async_remote_copy(
            src_ref=bsend.at[pl.ds(target * 8 + 4 * lax.rem(target, 2), 6)],
            dst_ref=rbody.at[:, pl.ds(g * planes, planes)],
            send_sem=far_send,
            recv_sem=far_recv,
            device_id={"grp": target, "pen": p},
            device_id_type=MESH,
        )

    def far_start(d, carry):
        far(d).start()
        return carry


    moves = [
        (u_ref.at[rows - 4 : rows], fp_ref.at[0:4, 0:zd], up, p),
        (u_ref.at[0:4], fp_ref.at[rows + 4 : rows + 8, 0:zd], down, p),
        (uedge, fp_ref.at[4 : rows + 4, zd : zd + 8], g, q),
        (uedge.at[rows - 4 : rows], fp_ref.at[0:4, zd : zd + 8], up, q),
        (uedge.at[0:4], fp_ref.at[rows + 4 : rows + 8, zd : zd + 8], down, q),
        (v_ref.at[planes - 2 : planes], vp_ref.at[0:2, 0:zd], up, p),
        (v_ref.at[0:2], vp_ref.at[planes + 2 : planes + 4, 0:zd], down, p),
        (vedge, vp_ref.at[2 : planes + 2, zd : zd + 8], g, q),
        (vedge.at[planes - 2 : planes], vp_ref.at[0:2, zd : zd + 8], up, q),
        (vedge.at[0:2], vp_ref.at[planes + 2 : planes + 4, zd : zd + 8], down, q),
        (cell_ref, cb_ref.at[1], up, p),
        (cell_ref, cb_ref.at[2], down, p),
        (cell_ref, cb_ref.at[3], g, q),
        (cell_ref, cb_ref.at[4], up, q),
        (cell_ref, cb_ref.at[5], down, q),
    ]
    copies = [
        pltpu.make_async_remote_copy(
            src_ref=src, dst_ref=dst, send_sem=near_send.at[i], recv_sem=near_recv.at[i],
            device_id={"grp": tg, "pen": tp}, device_id_type=MESH,
        )
        for i, (src, dst, tg, tp) in enumerate(moves)
    ]
    upward, downward, aside = (0, 3), (1, 4), (2,)
    copies[7].start()
    for i in range(10, 15):
        copies[i].start()
    for i in aside:
        copies[i].start()
    @pl.when(g < n - 1)
    def _():
        for i in upward:
            copies[i].start()

    @pl.when(g > 0)
    def _():
        for i in downward:
            copies[i].start()

    lax.fori_loop(n // 4, n - n // 4 + 1, far_start, 0)

    def rim_copy(d):
        target = lax.rem(g + d, n)
        return pltpu.make_async_remote_copy(
            src_ref=esend.at[target], dst_ref=ebody.at[pl.ds(g * planes, planes)],
            send_sem=rim_send, recv_sem=rim_recv,
            device_id={"grp": target, "pen": p}, device_id_type=MESH,
        )

    def rim_start(d, carry):
        rim_copy(d).start()
        return carry

    def bulk_wait(landed, send_sem, recv_sem):
        pltpu.make_async_remote_copy(
            src_ref=landed, dst_ref=landed, send_sem=send_sem, recv_sem=recv_sem,
            device_id={"grp": up, "pen": p}, device_id_type=MESH,
        ).wait()

    copies[7].wait()
    for x in range(planes):
        edge = vp_ref[x + 2, zd : zd + 8]
        tall = jnp.concatenate(
            [edge if i == 4 else pltpu.roll(edge, (4 - i) % fy, 1) for i in range(16)], axis=0
        ).T
        esend[:, x, :] = tall.reshape(n, rows, 128)[:, 0]
    lax.fori_loop(1, n, rim_start, 0)
    lax.fori_loop(n - n // 4 + 1, n, far_start, 0)
    lax.fori_loop(1, n // 4, far_start, 0)

    ebody[pl.ds(g * planes, planes)] = esend[g]
    fp_ref[4 : rows + 4, 0:zd] = u_ref[...]
    vp_ref[2 : planes + 2, 0:zd] = v_ref[...]
    cb_ref[0] = cell_ref[...]
    rbody[:, pl.ds(g * planes, planes)] = bsend[pl.ds(g * 8 + 4 * odd, 6)]

    for i in range(10, 15):
        copies[i].wait()

    lane128 = lax.broadcasted_iota(jnp.int32, (1, 128), 1)
    wanted = jnp.full((1, 128), -1, jnp.int32)
    for j in range(NF):
        wanted = jnp.where((lane128 & (NF - 1)) == j, ps_ref[j], wanted)
    sub_x = lax.broadcasted_iota(jnp.int32, (px, 128), 0)
    pick = jnp.concatenate(
        [(sub_x == wanted).astype(F32), (sub_x == ps_ref[NF - 1]).astype(F32)], axis=1
    ).astype(BF16)
    pick_ref[0:px] = pick
    pick_ref[px : 2 * px] = pick

    cosine = jnp.cos(yaw_ref[...])
    sine = jnp.sin(yaw_ref[...])
    index = [cb_ref[k, 0:1, :] for k in range(6)]
    turned = [cb_ref[k].T for k in range(6)]
    count = index[0].shape[1]
    lane_t = lax.broadcasted_iota(jnp.int32, (count, TURB), 1)

    def at_turbine(k, table):
        return jnp.sum(jnp.where(turned[k][:, 1:2] == lane_t, table, 0.0), axis=1, keepdims=True)

    lane_x = lax.broadcasted_iota(jnp.int32, (count, fx), 1)
    sub_z = lax.broadcasted_iota(jnp.int32, (depth, count), 0)
    along = [lax.rem(turned[k][:, 0:1], fx) for k in range(6)]

    turned_cos = [[at_turbine(k, cosine[s : s + 1]) for s in range(2)] for k in range(6)]

    def spread(k, s):
        return jnp.where(along[k] == lane_x, turned_cos[k][s], 0.0)

    sub_column = lax.broadcasted_iota(jnp.int32, (depth, 1), 0)
    z_global = jnp.where(
        sub_column < zd + 4, p * zd + sub_column, p * zd + sub_column - depth
    )
    z_ok = (z_global >= 0) & (z_global < lax.axis_size("pen") * zd)

    def row_ok(r):
        y = g * rows + (r - 4)
        return z_ok & (y >= 0) & (y < n * rows)

    for body, edge, first, last, offset in (
        (1, 4, 0, 4, rows - 4),
        (0, 3, 4, rows + 4, -4),
        (2, 5, rows + 4, rows + 8, -(rows + 4)),
    ):
        values = [
            split2(jnp.concatenate([spread(body, s), spread(edge, s)], axis=0)) for s in range(2)
        ]
        z_body = lax.rem(index[body] // fx, zd)
        y_body = index[body] // (fx * zd)
        z_edge = lax.rem(index[edge] // fx, zd)
        y_edge = index[edge] // (fx * zd)
        z_edge = jnp.where(z_edge < 4, z_edge + zd, jnp.where(z_edge >= zd - 4, z_edge + 8, -1))
        for r in range(first, last):
            yl = r + offset
            hot_body = (sub_z == z_body) & (y_body == yl)
            hot_edge = (sub_z == z_edge) & (y_edge == yl)
            hot = jnp.concatenate([hot_body.astype(F32), hot_edge.astype(F32)], axis=1).astype(BF16)
            for s, field in ((0, c0), (1, c1)):
                hi, lo = values[s]
                total = dot(hot, lo) + dot(hot, hi)
                field[r] = jnp.where(row_ok(r), total, 0.0)

    lane_r = lane128 // 8
    lane_k = lane128 & 7
    y_side = g * rows + lane_r - 4
    side_ok = z_ok & (y_side >= 0) & (y_side < n * rows)
    y_edge = g * rows + jnp.where(lane128 < 64, -1, rows)
    edge_ok = z_ok & (y_edge >= 0) & (y_edge < n * rows)

    hots, packs = [], []
    slots = []
    for k in range(6):
        z_cell = lax.rem(index[k] // fx, zd)
        if k >= 3:
            z_cell = jnp.where(z_cell < 4, z_cell + zd, jnp.where(z_cell >= zd - 4, z_cell + 8, -1))
        hots.append((sub_z == z_cell).astype(F32))
        r_cell = turned[k][:, 0:1] // (fx * zd) - (-4, rows - 4, -(rows + 4))[k % 3]
        in_front = jnp.where(along[k] < NF, (r_cell - 4) * NF + along[k], -1)
        beside = jnp.where((along[k] >= 14) & (along[k] < 22), r_cell * 8 + along[k] - 14, -1)
        slots.append((in_front, beside))
        parts = []
        for s in range(2):
            if k % 3 == 0:
                parts.append(jnp.where(in_front == lane128, turned_cos[k][s], 0.0))
            else:
                parts.append(jnp.zeros((count, 128), F32))
            parts.append(jnp.where(beside == lane128, turned_cos[k][s], 0.0))
        packs.append(jnp.concatenate(parts, axis=1))
    hi, lo = split2(jnp.concatenate(packs, axis=0))
    hot = jnp.concatenate(hots, axis=1).astype(BF16)
    packed = dot(hot, lo) + dot(hot, hi)
    for k in range(4):
        part = packed[:, k * 128 : (k + 1) * 128]
        cp_ref[k] = jnp.where(side_ok if k % 2 else z_ok, part, 0.0)

    for i in aside:
        copies[i].wait()

    lane_f = lax.broadcasted_iota(jnp.int32, (depth, fx), 1)

    for r in range(4, 12):
        w0[r] = jnp.where(z_ok, fp_ref[r], 0.0)

    def advance(field, upper_y, lower_y, behind, c):
        upper_z = pltpu.roll(field, depth - 1, 0)
        lower_z = pltpu.roll(field, 1, 0)
        slope_y = 0.5 * (upper_y - lower_y)
        slope_z = 0.5 * (upper_z - lower_z)
        square = slope_y * slope_y + slope_z * slope_z + SLOPE_EPS
        inverse = lax.rsqrt(square)
        viscosity = VISC_BASE + VISC_SLOPE * (square * inverse)
        laplacian = upper_y + lower_y + upper_z + lower_z - 4.0 * field
        moved = field - COURANT * (field - behind) + viscosity * laplacian
        share = (0.5 * VISC_SLOPE) * laplacian * inverse
        return moved - FORCE_GAIN * (c * c) * field, viscosity, share * slope_y, share * slope_z

    def forward(step, src, r, cos_field):
        field = src[r]
        behind = jnp.where(lane_f == 0, field, pltpu.roll(field, 1, 1))
        new, nu[step, r], ry[step, r], rz[step, r] = advance(
            field, src[r + 1], src[r - 1], behind, cos_field[r]
        )
        return new

    def power_slope(c, field):
        return (2.0 * POWER_GAIN) * (c * c * c) * field

    def yaw_term(c, field, value, new):
        return c * (2.0 * FORCE_GAIN * field * value - 3.0 * POWER_GAIN * c * new * new)

    for r in range(5, 11):
        new = forward(0, w0, r, c0)
        u1[r] = new
        w1[r] = jnp.where(row_ok(r), new, 0.0)
    for r in range(6, 10):
        new = forward(1, w1, r, c1)
        u2[r] = new
        lam[r] = power_slope(c1[r], new)
    @pl.when(g < n - 1)
    def _():
        for i in upward:
            copies[i].wait_send()
        for i in downward:
            copies[i].wait_recv()

    @pl.when(g > 0)
    def _():
        for i in downward:
            copies[i].wait_send()
        for i in upward:
            copies[i].wait_recv()

    side = jnp.zeros((depth, 128), F32)
    for r in range(16):
        side = jnp.where(lane_r == r, pltpu.roll(fp_ref[r, :, 0:128], (8 * r - 14) % 128, 1), side)
    side_ref[...] = side

    def spread_terms(step, r):
        value = lam[r]
        am[r] = value * nu[step, r]
        bm[r] = value * ry[step, r]

    def backward(step, r, cos_field):
        value = lam[r]
        a = am[r]
        b = value * rz[step, r]
        c = cos_field[r]
        ahead = jnp.where(lane_f == fx - 1, 0.0, pltpu.roll(value, fx - 1, 1))
        total = value * ((1.0 - COURANT) - FORCE_GAIN * (c * c)) + COURANT * ahead - 4.0 * a
        total = total + (am[r - 1] + bm[r - 1]) + (am[r + 1] - bm[r + 1])
        return total + pltpu.roll(a + b, 1, 0) + pltpu.roll(a - b, depth - 1, 0)

    for r in (0, 1, 2, 3, 12, 13, 14, 15):
        w0[r] = jnp.where(row_ok(r), fp_ref[r], 0.0)
    for r in (1, 2, 3, 4, 11, 12, 13, 14):
        new = forward(0, w0, r, c0)
        u1[r] = new
        w1[r] = jnp.where(row_ok(r), new, 0.0)
    for r in (2, 3, 4, 5, 10, 11, 12, 13):
        new = forward(1, w1, r, c1)
        u2[r] = new
        lam[r] = power_slope(c1[r], new)
    for r in range(4, rows + 4):
        gc1[r - 4] = yaw_term(c1[r], w1[r], lam[r], u2[r])[0:zd]
        farm_ref[r - 4] = u2[r][0:zd]
    for r in range(2, 14):
        spread_terms(1, r)
    for r in range(3, 13):
        value = backward(1, r, c1) + power_slope(c0[r], u1[r])
        u2[r] = jnp.where(row_ok(r), value, 0.0)
    for r in range(3, 13):
        lam[r] = u2[r]
    for r in range(4, rows + 4):
        gc0[r - 4] = yaw_term(c0[r], w0[r], lam[r], u1[r])[0:zd]
    flat = turned[0][:, 0:1] // fx
    take = (flat == lax.broadcasted_iota(jnp.int32, (count, rows * zd), 1)).astype(F32).astype(BF16)
    far_along = jnp.where(along[0] >= 18, along[0], -1)
    for s, terms in ((0, gc0), (1, gc1)):
        hi, lo = split2(terms[...].reshape(rows * zd, fx))
        lines = dot(take, lo) + dot(take, hi)
        value = jnp.where(far_along == lane_x, lines, 0.0)
        part_ref[s] = value[:, 0:128] + value[:, 128:256]

    bulk_wait(rbody.at[:, 0 : px - planes], far_send, far_recv)

    bulk_wait(ebody.at[0 : px - planes], rim_send, rim_recv)

    for i in range(6):
        flipped = rbody[i].T
        for h in range(2):
            k = h * 6 + i
            w_ref[k + odd * (11 - 2 * k), 0:zd] = flipped[h * zd : (h + 1) * zd]
    mated = g + 1 - 2 * odd
    lasts = [
        pltpu.make_async_remote_copy(
            src_ref=w_ref.at[8 + k, 0:zd], dst_ref=w_ref.at[15 - k, 0:zd],
            send_sem=edge_send.at[k], recv_sem=edge_recv.at[k],
            device_id={"grp": mated, "pen": p}, device_id_type=MESH,
        )
        for k in range(4)
    ]
    for last in lasts:
        last.start()
    for i in (5, 6, 8, 9):
        copies[i].start()

    rims = ebody[...].T
    for r in range(16):
        w_ref[r + odd * (15 - 2 * r), zd : zd + 8] = rims[8 * r : 8 * r + 8]

    for i in range(1, 11):
        vw1[i] = periodic_row(w_ref, i, False)
    for i in range(2, 10):
        vw2[i] = periodic_row(vw1, i, False)

    for last in lasts:
        last.wait()


    for i in range(11, 15):
        vw1[i] = periodic_row(w_ref, i, False)
    for i in range(10, 14):
        vw2[i] = periodic_row(vw1, i, False)

    def inlets(src, first, stop):
        hi, lo = split2(src[first:stop].reshape((stop - first) * depth, px))
        found = dot(jnp.concatenate([hi, lo], axis=1), pick_ref[...])
        front = jnp.zeros((depth, 128), F32)
        rim = front
        beside = front
        for r in range(first, stop):
            part = found[(r - first) * depth : (r - first + 1) * depth]
            row = r + odd * (15 - 2 * r)
            if 4 <= r < 12:
                front = jnp.where(lane128 // NF == row - 4, part[:, 0:128], front)
            elif r == 3:
                rim = jnp.where(lane128 // 64 == odd, part[:, 0:128], rim)
            elif r == 12:
                rim = jnp.where(lane128 // 64 == 1 - odd, part[:, 0:128], rim)
            beside = jnp.where(lane_r == row, part[:, 128:256], beside)
        return jnp.where(z_ok, front, 0.0), jnp.where(edge_ok, rim, 0.0), beside

    def front_step(field, rim, c):
        upper_y = jnp.where(lane128 >= 112, rim, pltpu.roll(field, 112, 1))
        lower_y = jnp.where(lane128 < 16, rim, pltpu.roll(field, 16, 1))
        behind = jnp.where((lane128 & 15) == 0, field, pltpu.roll(field, 1, 1))
        return advance(field, upper_y, lower_y, behind, c)[0]

    def side_step(field, c):
        return advance(field, pltpu.roll(field, 120, 1), pltpu.roll(field, 8, 1), pltpu.roll(field, 1, 1), c)

    def side_back(value, c, scale, slope_y, slope_z):
        a = value * scale
        b = value * slope_y
        d = value * slope_z
        total = value * ((1.0 - COURANT) - FORCE_GAIN * (c * c)) - 4.0 * a
        total = total + COURANT * pltpu.roll(value, 127, 1)
        total = total + pltpu.roll(a + b, 8, 1) + pltpu.roll(a - b, 120, 1)
        return total + pltpu.roll(a + d, 1, 0) + pltpu.roll(a - d, depth - 1, 0)

    front0, rim0, beside0 = inlets(vw1, 1, 15)
    front1, rim1, beside1 = inlets(vw2, 2, 14)
    cf0, cs0, cf1, cs1 = (cp_ref[k] for k in range(4))

    uf1 = front_step(front0, rim0, cf0)
    uf2 = front_step(front1, rim1, cf1)
    tf0 = yaw_term(cf0, front0, power_slope(cf0, uf1), uf1)
    tf1 = yaw_term(cf1, front1, power_slope(cf1, uf2), uf2)

    ws0 = jnp.where(side_ok, jnp.where(lane_k == 1, beside0, side_ref[...]), 0.0)
    us1, *back0 = side_step(ws0, cs0)
    ws1 = jnp.where(side_ok, jnp.where(lane_k == 1, beside1, us1), 0.0)
    us2, *back1 = side_step(ws1, cs1)
    value2 = power_slope(cs1, us2)
    value1 = jnp.where(side_ok, side_back(value2, cs1, *back1) + power_slope(cs0, us1), 0.0)
    ts0 = yaw_term(cs0, ws0, value1, us1)
    ts1 = yaw_term(cs1, ws1, value2, us2)

    terms = jnp.concatenate([tf0, ts0, tf1, ts1], axis=1)[0:zd]
    hi, lo = split2(terms)
    z_own = lax.rem(turned[0][:, 0:1] // fx, zd)
    take_z = (z_own == lax.broadcasted_iota(jnp.int32, (count, zd), 1)).astype(F32).astype(BF16)
    lines = dot(take_z, lo) + dot(take_z, hi)
    in_front = slots[0][0]
    beside = jnp.where((along[0] >= 16) & (along[0] < 18), slots[0][1], -1)
    total_a[g * m + p] = jnp.zeros(total_a.shape[1:], F32)
    mine = total_a.at[g * m + p]
    for s in range(2):
        value = part_ref[s] + jnp.where(in_front == lane128, lines[:, s * 256 : s * 256 + 128], 0.0)
        value = value + jnp.where(beside == lane128, lines[:, s * 256 + 128 : s * 256 + 256], 0.0)
        value = jnp.sum(value, axis=1, keepdims=True) * at_turbine(0, sine[s : s + 1])
        mine[s : s + 1, 0:TURB] = jnp.sum(
            jnp.where(turned[0][:, 1:2] == lane_t, value, 0.0), axis=0, keepdims=True
        )

    def near_copy(d):
        return pltpu.make_async_remote_copy(
            src_ref=total_a.at[g * m + p], dst_ref=total_a.at[g * m + p],
            send_sem=a_send, recv_sem=a_recv, device_id=peer(d), device_id_type=MESH,
        )

    def line_copy(d):
        return pltpu.make_async_remote_copy(
            src_ref=total_b.at[scen], dst_ref=total_b.at[scen],
            send_sem=b_send.at[d], recv_sem=b_recv.at[d], device_id=line(d), device_id_type=MESH,
        )

    def start(make):
        def run(d, carry):
            make(d).start()
            return carry

        return run

    def wait(make):
        def run(d, carry):
            make(d).wait()
            return carry

        return run

    lax.fori_loop(1, n * m, start(near_copy), 0)

    for r in range(3, 13):
        spread_terms(0, r)
    for r in range(4, rows + 4):
        sens_ref[r - 4] = backward(0, r, c0)[0:zd]

    ss = side_back(value1, cs0, *back0)

    us2, ss, uf2 = us2[0:zd], ss[0:zd], uf2[0:zd]
    for r in range(rows):
        shift = (-18 - 8 * r) % 128
        farm_ref[r, :, 0:128] = jnp.where(
            lane128 < NF, pltpu.roll(uf2, (-NF * r) % 128, 1),
            jnp.where(lane128 < 18, pltpu.roll(us2, shift, 1), farm_ref[r, :, 0:128]),
        )
        sens_ref[r, :, 0:128] = jnp.where(
            lane128 < NF, 0.0,
            jnp.where(lane128 < 18, pltpu.roll(ss, shift, 1), sens_ref[r, :, 0:128]),
        )

    for i in (5, 6, 8, 9):
        copies[i].wait()

    for i in range(1, planes + 3):
        v1[i] = periodic_row(vp_ref, i, True)
    for i in range(2, planes + 2):
        prec_ref[i - 2] = periodic_row(v1, i, True)[0:zd]

    bulk_wait(total_a.at[0 : n * m - 1], a_send, a_recv)
    total_b[scen] = jnp.sum(total_a[...], axis=0)
    lax.fori_loop(1, ns, start(line_copy), 0)
    lax.fori_loop(1, ns, wait(line_copy), 0)
    grad_ref[...] = jnp.sum(total_b[...], axis=0)[0 : grad_ref.shape[0], 0 : grad_ref.shape[1]]


def farm_steps(sizes, v, u, index, turbine, yaw, ps):
    planes, zd, fy = v.shape
    rows, _, fx = u.shape
    ns, n, m = sizes
    px = n * planes
    depth = zd + 8
    farm = pltpu.VMEM((16, depth, fx), F32)
    dma = pltpu.SemaphoreType.DMA
    return pl.pallas_call(
        functools.partial(farm_kernel, sizes),
        out_shape=(
            pltpu.VMEM(v.shape, F32),
            pltpu.VMEM(u.shape, F32),
            pltpu.VMEM(u.shape, F32),
            pltpu.VMEM(yaw.shape, F32),
        ),
        in_specs=[HBM] * 5 + [SMEM],
        out_specs=(VMEM,) * 4,
        scratch_shapes=[
            farm,
            pltpu.VMEM((planes + 4, depth, fy), F32),
            pltpu.VMEM((16, depth, px), F32),
            pltpu.VMEM((6, 8, index.shape[1]), jnp.int32),
            pltpu.VMEM(v.shape, F32),
            pltpu.VMEM(u.shape, F32),
            pltpu.VMEM((8, index.shape[1]), jnp.int32),
            pltpu.VMEM(index.shape, jnp.int32),
            pltpu.VMEM(turbine.shape, jnp.int32),
            pltpu.VMEM(yaw.shape, F32),
            dma((5,)),
            pltpu.VMEM((planes, 8, fy), F32),
            pltpu.VMEM((rows, 8, fx), F32),
            pltpu.VMEM((fy + 8, planes, 2 * zd), F32),
            pltpu.VMEM((6, px, 2 * zd), F32),
            pltpu.VMEM((n, planes, 128), F32),
            pltpu.VMEM((px, 128), F32),
            pltpu.VMEM((planes + 4, depth, fy), F32),
            pltpu.VMEM((16, depth, px), F32),
            pltpu.VMEM((16, depth, px), F32),
            farm, farm, farm, farm, farm, farm, farm,
            pltpu.VMEM((2, 16, depth, fx), F32),
            pltpu.VMEM((2, 16, depth, fx), F32),
            pltpu.VMEM((2, 16, depth, fx), F32),
            farm, farm,
            pltpu.VMEM(u.shape, F32),
            pltpu.VMEM(u.shape, F32),
            pltpu.VMEM((n * m, 2, 128), F32),
            pltpu.VMEM((ns, 2, 128), F32),
            pltpu.VMEM((2 * px, 256), BF16),
            pltpu.VMEM((4, depth, 128), F32),
            pltpu.VMEM((depth, 128), F32),
            pltpu.VMEM((2, index.shape[1], 128), F32),
            dma((15,)), dma((15,)), dma, dma, dma, dma, dma((4,)), dma((4,)),
            dma, dma, dma((ns,)), dma((ns,)),
        ],
        compiler_params=pltpu.CompilerParams(
            collective_id=0, has_side_effects=True, vmem_limit_bytes=56 * 1024 * 1024
        ),
        name="farm_steps",
    )(v, u, index, turbine, yaw, ps)


def finish_kernel(*refs):
    count = (len(refs) - 1) // 2
    sem = refs[-1]
    copies = [pltpu.make_async_copy(refs[i], refs[count + i], sem.at[i]) for i in range(count)]
    for copy in copies:
        copy.start()
    for copy in copies:
        copy.wait()


def finish(*arrays):
    return pl.pallas_call(
        finish_kernel,
        out_shape=tuple(jax.ShapeDtypeStruct(x.shape, F32) for x in arrays),
        in_specs=[VMEM] * len(arrays),
        out_specs=(HBM,) * len(arrays),
        scratch_shapes=[pltpu.SemaphoreType.DMA((len(arrays),))],
        name="finish",
    )(*[pltpu.with_memory_space_constraint(x, pltpu.VMEM) for x in arrays])


def shards(sizes, prec_state, farm_state, yaw_angles, plane_source, cell_index, cell_turbine):
    prec, farm, sens, yaw_grad = farm_steps(
        sizes, prec_state[0], farm_state[0], cell_index[0], cell_turbine[0], yaw_angles,
        plane_source,
    )
    prec, farm, sens, yaw_grad = finish(prec, farm, sens, yaw_grad)
    return (prec[None], farm[None], sens[None], yaw_grad)


def solution(mesh):
    spec = P("scen", "grp", "pen", None)
    in_specs = (spec, spec, P(), P(), P("grp", "pen", None), P("grp", "pen", None))
    out_specs = (spec, spec, spec, P())
    sizes = tuple(mesh.shape[axis] for axis in ("scen", "grp", "pen"))
    return jax.shard_map(
        functools.partial(shards, sizes), mesh=mesh, in_specs=in_specs, out_specs=out_specs,
        check_vma=False,
    )
```

```python
import functools

import jax
import jax.numpy as jnp
from jax import lax
from jax.experimental import pallas as pl
from jax.experimental.pallas import tpu as pltpu
from jax.sharding import PartitionSpec as P

NF = 16
TURB = 64
COURANT = 0.3
VISC_BASE = 0.03
VISC_SLOPE = 0.03
SLOPE_EPS = 0.01
FORCE_GAIN = 0.3
POWER_GAIN = 0.002

MESH = pl.DeviceIdType.MESH
VMEM = pl.BlockSpec(memory_space=pltpu.VMEM)
HBM = pl.BlockSpec(memory_space=pltpu.HBM)
SMEM = pl.BlockSpec(memory_space=pltpu.SMEM)
F32 = jnp.float32
BF16 = jnp.bfloat16


def split2(b):
    high = b.astype(BF16)
    return high, (b - high.astype(F32)).astype(BF16)


def dot(a, b):
    return jnp.dot(a, b, preferred_element_type=F32)


def advance_plane(centre, upper_a, lower_a, upper_z, lower_z, upper_l, lower_l, lower_x):
    slope_a = 0.5 * (upper_a - lower_a)
    slope_l = 0.5 * (upper_l - lower_l)
    slope_z = 0.5 * (upper_z - lower_z)
    viscosity = VISC_BASE + VISC_SLOPE * jnp.sqrt(
        slope_a * slope_a + slope_l * slope_l + slope_z * slope_z + SLOPE_EPS
    )
    laplacian = upper_a + lower_a + upper_l + lower_l + upper_z + lower_z - 6.0 * centre
    return centre - COURANT * (centre - lower_x) + viscosity * laplacian


def periodic_row(src, i, lead_is_x):
    centre = src[i]
    depth, lanes = centre.shape
    upper_l = pltpu.roll(centre, lanes - 1, 1)
    lower_l = pltpu.roll(centre, 1, 1)
    upper_z = pltpu.roll(centre, depth - 1, 0)
    lower_z = pltpu.roll(centre, 1, 0)
    upper_a = src[i + 1]
    lower_a = src[i - 1]
    lower_x = lower_a if lead_is_x else lower_l
    return advance_plane(centre, upper_a, lower_a, upper_z, lower_z, upper_l, lower_l, lower_x)


def farm_kernel(
    sizes, v_in, u_in, index_in, turbine_in, yaw_in, ps_ref,
    prec_ref, farm_ref, sens_ref, grad_ref,
    fp_ref, vp_ref, w_ref, cb_ref,
    v_ref, u_ref, cell_ref, index_ref, turbine_ref, yaw_ref, in_sem,
    vedge, uedge, bsend, rbody, esend, ebody,
    v1, vw1, vw2, c0, c1, w0, w1, u1, u2, lam, nu, ry, rz, am, bm, gc0, gc1, total_a, total_b,
    pick_ref, cp_ref, side_ref, part_ref,
    near_send, near_recv, far_send, far_recv, rim_send, rim_recv, edge_send, edge_recv, a_send, a_recv, b_send, b_recv,
):
    g = lax.axis_index("grp")
    p = lax.axis_index("pen")
    q = 1 - p
    ns, n, m = sizes
    up = lax.rem(g + 1, n)
    down = lax.rem(g + n - 1, n)
    odd = lax.rem(g, 2)
    planes, zd, fy = v_ref.shape
    rows, _, fx = u_ref.shape
    depth = zd + 8
    px = w_ref.shape[2]
    scen = lax.axis_index("scen")

    barrier = pltpu.get_barrier_semaphore()

    def peer(d):
        other = lax.rem(g * m + p + d, n * m)
        return {"grp": other // m, "pen": lax.rem(other, m)}

    def mate(d):
        return {"grp": lax.rem(g + d, n), "pen": p}

    def line(d):
        return {"scen": lax.rem(scen + d, ns), "grp": g, "pen": p}

    def greet(make):
        def run(d, carry):
            pl.semaphore_signal(barrier, inc=1, device_id=make(d), device_id_type=MESH)
            return carry

        return run

    lax.fori_loop(1, n, greet(mate), 0)
    for target in (g, up, down):
        pl.semaphore_signal(barrier, inc=1, device_id={"grp": target, "pen": q}, device_id_type=MESH)
    lax.fori_loop(1, ns, greet(line), 0)

    loads = [
        pltpu.make_async_copy(src, dst, in_sem.at[i])
        for i, (src, dst) in enumerate((
            (v_in, v_ref), (index_in, index_ref), (turbine_in, turbine_ref), (u_in, u_ref), (yaw_in, yaw_ref),
        ))
    ]
    for load in loads:
        load.start()
    loads[0].wait()

    vedge[:, 0:4] = v_ref[:, 0:4]
    vedge[:, 4:8] = v_ref[:, zd - 4 : zd]
    for x in range(planes):
        plane = v_ref[x]
        both = jnp.concatenate([plane, pltpu.roll(plane, fy - 6, 1)], axis=0).T
        bsend[4 : fy + 4, x, :] = both
        bsend[0:4, x, :] = both[fy - 4 : fy]
        bsend[fy + 4 : fy + 8, x, :] = both[0:4]

    for load in loads[1:]:
        load.wait()
    uedge[:, 0:4] = u_ref[:, 0:4]
    uedge[:, 4:8] = u_ref[:, zd - 4 : zd]
    cell_ref[...] = jnp.zeros_like(cell_ref)
    cell_ref[0:1] = index_ref[...]
    cell_ref[1:2] = turbine_ref[...]

    pl.semaphore_wait(barrier, (n - 1) + 3 + (ns - 1))

    def far(d):
        target = lax.rem(g + d, n)
        return pltpu.make_async_remote_copy(
            src_ref=bsend.at[pl.ds(target * 8 + 4 * lax.rem(target, 2), 6)],
            dst_ref=rbody.at[:, pl.ds(g * planes, planes)],
            send_sem=far_send,
            recv_sem=far_recv,
            device_id={"grp": target, "pen": p},
            device_id_type=MESH,
        )

    def far_start(d, carry):
        far(d).start()
        return carry


    moves = [
        (u_ref.at[rows - 4 : rows], fp_ref.at[0:4, 0:zd], up, p),
        (u_ref.at[0:4], fp_ref.at[rows + 4 : rows + 8, 0:zd], down, p),
        (uedge, fp_ref.at[4 : rows + 4, zd : zd + 8], g, q),
        (uedge.at[rows - 4 : rows], fp_ref.at[0:4, zd : zd + 8], up, q),
        (uedge.at[0:4], fp_ref.at[rows + 4 : rows + 8, zd : zd + 8], down, q),
        (v_ref.at[planes - 2 : planes], vp_ref.at[0:2, 0:zd], up, p),
        (v_ref.at[0:2], vp_ref.at[planes + 2 : planes + 4, 0:zd], down, p),
        (vedge, vp_ref.at[2 : planes + 2, zd : zd + 8], g, q),
        (vedge.at[planes - 2 : planes], vp_ref.at[0:2, zd : zd + 8], up, q),
        (vedge.at[0:2], vp_ref.at[planes + 2 : planes + 4, zd : zd + 8], down, q),
        (cell_ref, cb_ref.at[1], up, p),
        (cell_ref, cb_ref.at[2], down, p),
        (cell_ref, cb_ref.at[3], g, q),
        (cell_ref, cb_ref.at[4], up, q),
        (cell_ref, cb_ref.at[5], down, q),
    ]
    copies = [
        pltpu.make_async_remote_copy(
            src_ref=src, dst_ref=dst, send_sem=near_send.at[i], recv_sem=near_recv.at[i],
            device_id={"grp": tg, "pen": tp}, device_id_type=MESH,
        )
        for i, (src, dst, tg, tp) in enumerate(moves)
    ]
    upward, downward, aside = (0, 3), (1, 4), (2,)
    copies[7].start()
    for i in range(10, 15):
        copies[i].start()
    for i in aside:
        copies[i].start()
    @pl.when(g < n - 1)
    def _():
        for i in upward:
            copies[i].start()

    @pl.when(g > 0)
    def _():
        for i in downward:
            copies[i].start()

    lax.fori_loop(n // 4, n - n // 4 + 1, far_start, 0)

    def rim_copy(d):
        target = lax.rem(g + d, n)
        return pltpu.make_async_remote_copy(
            src_ref=esend.at[target], dst_ref=ebody.at[pl.ds(g * planes, planes)],
            send_sem=rim_send, recv_sem=rim_recv,
            device_id={"grp": target, "pen": p}, device_id_type=MESH,
        )

    def rim_start(d, carry):
        rim_copy(d).start()
        return carry

    def bulk(landed, send_sem, recv_sem):
        return pltpu.make_async_remote_copy(
            src_ref=landed, dst_ref=landed, send_sem=send_sem, recv_sem=recv_sem,
            device_id={"grp": up, "pen": p}, device_id_type=MESH,
        )

    whole_far = bulk(rbody.at[:, 0 : px - planes], far_send, far_recv)
    whole_rim = bulk(ebody.at[0 : px - planes], rim_send, rim_recv)
    whole_sum = bulk(total_a.at[0 : n * m - 1], a_send, a_recv)

    copies[7].wait()
    for x in range(planes):
        edge = vp_ref[x + 2, zd : zd + 8]
        tall = jnp.concatenate(
            [edge if i == 4 else pltpu.roll(edge, (4 - i) % fy, 1) for i in range(16)], axis=0
        ).T
        esend[:, x, :] = tall.reshape(n, rows, 128)[:, 0]
    lax.fori_loop(1, n, rim_start, 0)
    lax.fori_loop(n - n // 4 + 1, n, far_start, 0)
    lax.fori_loop(1, n // 4, far_start, 0)

    ebody[pl.ds(g * planes, planes)] = esend[g]
    fp_ref[4 : rows + 4, 0:zd] = u_ref[...]
    vp_ref[2 : planes + 2, 0:zd] = v_ref[...]
    cb_ref[0] = cell_ref[...]
    rbody[:, pl.ds(g * planes, planes)] = bsend[pl.ds(g * 8 + 4 * odd, 6)]

    for i in range(10, 15):
        copies[i].wait()

    lane128 = lax.broadcasted_iota(jnp.int32, (1, 128), 1)
    wanted = jnp.full((1, 128), -1, jnp.int32)
    for j in range(NF):
        wanted = jnp.where((lane128 & (NF - 1)) == j, ps_ref[j], wanted)
    sub_x = lax.broadcasted_iota(jnp.int32, (px, 128), 0)
    pick = jnp.concatenate(
        [(sub_x == wanted).astype(F32), (sub_x == ps_ref[NF - 1]).astype(F32)], axis=1
    ).astype(BF16)
    pick_ref[0:px] = pick
    pick_ref[px : 2 * px] = pick

    cosine = jnp.cos(yaw_ref[...])
    sine = jnp.sin(yaw_ref[...])
    index = [cb_ref[k, 0:1, :] for k in range(6)]
    turned = [cb_ref[k].T for k in range(6)]
    count = index[0].shape[1]
    lane_t = lax.broadcasted_iota(jnp.int32, (count, TURB), 1)

    def at_turbine(k, table):
        return jnp.sum(jnp.where(turned[k][:, 1:2] == lane_t, table, 0.0), axis=1, keepdims=True)

    lane_x = lax.broadcasted_iota(jnp.int32, (count, fx), 1)
    sub_z = lax.broadcasted_iota(jnp.int32, (depth, count), 0)
    along = [lax.rem(turned[k][:, 0:1], fx) for k in range(6)]

    turned_cos = [[at_turbine(k, cosine[s : s + 1]) for s in range(2)] for k in range(6)]

    def spread(k, s):
        return jnp.where(along[k] == lane_x, turned_cos[k][s], 0.0)

    sub_column = lax.broadcasted_iota(jnp.int32, (depth, 1), 0)
    z_global = jnp.where(
        sub_column < zd + 4, p * zd + sub_column, p * zd + sub_column - depth
    )
    z_ok = (z_global >= 0) & (z_global < lax.axis_size("pen") * zd)

    def row_ok(r):
        y = g * rows + (r - 4)
        return z_ok & (y >= 0) & (y < n * rows)

    for body, edge, first, last, offset in (
        (1, 4, 0, 4, rows - 4),
        (0, 3, 4, rows + 4, -4),
        (2, 5, rows + 4, rows + 8, -(rows + 4)),
    ):
        values = [
            split2(jnp.concatenate([spread(body, s), spread(edge, s)], axis=0)) for s in range(2)
        ]
        z_body = lax.rem(index[body] // fx, zd)
        y_body = index[body] // (fx * zd)
        z_edge = lax.rem(index[edge] // fx, zd)
        y_edge = index[edge] // (fx * zd)
        z_edge = jnp.where(z_edge < 4, z_edge + zd, jnp.where(z_edge >= zd - 4, z_edge + 8, -1))
        for r in range(first, last):
            yl = r + offset
            hot_body = (sub_z == z_body) & (y_body == yl)
            hot_edge = (sub_z == z_edge) & (y_edge == yl)
            hot = jnp.concatenate([hot_body.astype(F32), hot_edge.astype(F32)], axis=1).astype(BF16)
            for s, field in ((0, c0), (1, c1)):
                hi, lo = values[s]
                total = dot(hot, lo) + dot(hot, hi)
                field[r] = jnp.where(row_ok(r), total, 0.0)

    lane_r = lane128 // 8
    lane_k = lane128 & 7
    y_side = g * rows + lane_r - 4
    side_ok = z_ok & (y_side >= 0) & (y_side < n * rows)
    y_edge = g * rows + jnp.where(lane128 < 64, -1, rows)
    edge_ok = z_ok & (y_edge >= 0) & (y_edge < n * rows)

    hots, packs = [], []
    slots = []
    for k in range(6):
        z_cell = lax.rem(index[k] // fx, zd)
        if k >= 3:
            z_cell = jnp.where(z_cell < 4, z_cell + zd, jnp.where(z_cell >= zd - 4, z_cell + 8, -1))
        hots.append((sub_z == z_cell).astype(F32))
        r_cell = turned[k][:, 0:1] // (fx * zd) - (-4, rows - 4, -(rows + 4))[k % 3]
        in_front = jnp.where(along[k] < NF, (r_cell - 4) * NF + along[k], -1)
        beside = jnp.where((along[k] >= 14) & (along[k] < 22), r_cell * 8 + along[k] - 14, -1)
        slots.append((in_front, beside))
        parts = []
        for s in range(2):
            if k % 3 == 0:
                parts.append(jnp.where(in_front == lane128, turned_cos[k][s], 0.0))
            else:
                parts.append(jnp.zeros((count, 128), F32))
            parts.append(jnp.where(beside == lane128, turned_cos[k][s], 0.0))
        packs.append(jnp.concatenate(parts, axis=1))
    hi, lo = split2(jnp.concatenate(packs, axis=0))
    hot = jnp.concatenate(hots, axis=1).astype(BF16)
    packed = dot(hot, lo) + dot(hot, hi)
    for k in range(4):
        part = packed[:, k * 128 : (k + 1) * 128]
        cp_ref[k] = jnp.where(side_ok if k % 2 else z_ok, part, 0.0)

    for i in aside:
        copies[i].wait()

    lane_f = lax.broadcasted_iota(jnp.int32, (depth, fx), 1)

    for r in range(4, 12):
        w0[r] = jnp.where(z_ok, fp_ref[r], 0.0)

    def advance(field, upper_y, lower_y, behind, c):
        upper_z = pltpu.roll(field, depth - 1, 0)
        lower_z = pltpu.roll(field, 1, 0)
        slope_y = 0.5 * (upper_y - lower_y)
        slope_z = 0.5 * (upper_z - lower_z)
        square = slope_y * slope_y + slope_z * slope_z + SLOPE_EPS
        inverse = lax.rsqrt(square)
        viscosity = VISC_BASE + VISC_SLOPE * (square * inverse)
        laplacian = upper_y + lower_y + upper_z + lower_z - 4.0 * field
        moved = field - COURANT * (field - behind) + viscosity * laplacian
        share = (0.5 * VISC_SLOPE) * laplacian * inverse
        return moved - FORCE_GAIN * (c * c) * field, viscosity, share * slope_y, share * slope_z

    def forward(step, src, r, cos_field):
        field = src[r]
        behind = jnp.where(lane_f == 0, field, pltpu.roll(field, 1, 1))
        new, nu[step, r], ry[step, r], rz[step, r] = advance(
            field, src[r + 1], src[r - 1], behind, cos_field[r]
        )
        return new

    def power_slope(c, field):
        return (2.0 * POWER_GAIN) * (c * c * c) * field

    def yaw_term(c, field, value, new):
        return c * (2.0 * FORCE_GAIN * field * value - 3.0 * POWER_GAIN * c * new * new)

    for r in range(5, 11):
        new = forward(0, w0, r, c0)
        u1[r] = new
        w1[r] = jnp.where(row_ok(r), new, 0.0)
    for r in range(6, 10):
        new = forward(1, w1, r, c1)
        u2[r] = new
        lam[r] = power_slope(c1[r], new)
    @pl.when(g < n - 1)
    def _():
        for i in upward:
            copies[i].wait_send()
        for i in downward:
            copies[i].wait_recv()

    @pl.when(g > 0)
    def _():
        for i in downward:
            copies[i].wait_send()
        for i in upward:
            copies[i].wait_recv()

    side = jnp.zeros((depth, 128), F32)
    for r in range(16):
        side = jnp.where(lane_r == r, pltpu.roll(fp_ref[r, :, 0:128], (8 * r - 14) % 128, 1), side)
    side_ref[...] = side

    def spread_terms(step, r):
        value = lam[r]
        am[r] = value * nu[step, r]
        bm[r] = value * ry[step, r]

    def backward(step, r, cos_field):
        value = lam[r]
        a = am[r]
        b = value * rz[step, r]
        c = cos_field[r]
        ahead = jnp.where(lane_f == fx - 1, 0.0, pltpu.roll(value, fx - 1, 1))
        total = value * ((1.0 - COURANT) - FORCE_GAIN * (c * c)) + COURANT * ahead - 4.0 * a
        total = total + (am[r - 1] + bm[r - 1]) + (am[r + 1] - bm[r + 1])
        return total + pltpu.roll(a + b, 1, 0) + pltpu.roll(a - b, depth - 1, 0)

    for r in (0, 1, 2, 3, 12, 13, 14, 15):
        w0[r] = jnp.where(row_ok(r), fp_ref[r], 0.0)
    for r in (1, 2, 3, 4, 11, 12, 13, 14):
        new = forward(0, w0, r, c0)
        u1[r] = new
        w1[r] = jnp.where(row_ok(r), new, 0.0)
    for r in (2, 3, 4, 5, 10, 11, 12, 13):
        new = forward(1, w1, r, c1)
        u2[r] = new
        lam[r] = power_slope(c1[r], new)
    for r in range(4, rows + 4):
        gc1[r - 4] = yaw_term(c1[r], w1[r], lam[r], u2[r])[0:zd]
        farm_ref[r - 4] = u2[r][0:zd]
    for r in range(2, 14):
        spread_terms(1, r)
    for r in range(3, 13):
        value = backward(1, r, c1) + power_slope(c0[r], u1[r])
        u2[r] = jnp.where(row_ok(r), value, 0.0)
    for r in range(3, 13):
        lam[r] = u2[r]
    for r in range(4, rows + 4):
        gc0[r - 4] = yaw_term(c0[r], w0[r], lam[r], u1[r])[0:zd]
    flat = turned[0][:, 0:1] // fx
    take = (flat == lax.broadcasted_iota(jnp.int32, (count, rows * zd), 1)).astype(F32).astype(BF16)
    far_along = jnp.where(along[0] >= 18, along[0], -1)
    for s, terms in ((0, gc0), (1, gc1)):
        hi, lo = split2(terms[...].reshape(rows * zd, fx))
        lines = dot(take, lo) + dot(take, hi)
        value = jnp.where(far_along == lane_x, lines, 0.0)
        part_ref[s] = value[:, 0:128] + value[:, 128:256]

    whole_far.wait_recv()

    whole_rim.wait_recv()

    for i in range(6):
        flipped = rbody[i].T
        for h in range(2):
            k = h * 6 + i
            w_ref[k + odd * (11 - 2 * k), 0:zd] = flipped[h * zd : (h + 1) * zd]
    mated = g + 1 - 2 * odd
    lasts = [
        pltpu.make_async_remote_copy(
            src_ref=w_ref.at[8 + k, 0:zd], dst_ref=w_ref.at[15 - k, 0:zd],
            send_sem=edge_send, recv_sem=edge_recv,
            device_id={"grp": mated, "pen": p}, device_id_type=MESH,
        )
        for k in range(4)
    ]
    for last in lasts:
        last.start()
    for i in (5, 6, 8, 9):
        copies[i].start()

    rims = ebody[...].T
    for r in range(16):
        w_ref[r + odd * (15 - 2 * r), zd : zd + 8] = rims[8 * r : 8 * r + 8]

    for i in range(1, 11):
        vw1[i] = periodic_row(w_ref, i, False)
    for i in range(2, 10):
        vw2[i] = periodic_row(vw1, i, False)

    bulk(w_ref.at[8:12, 0:zd], edge_send, edge_recv).wait()


    for i in range(11, 15):
        vw1[i] = periodic_row(w_ref, i, False)
    for i in range(10, 14):
        vw2[i] = periodic_row(vw1, i, False)

    def inlets(src, first, stop):
        hi, lo = split2(src[first:stop].reshape((stop - first) * depth, px))
        found = dot(jnp.concatenate([hi, lo], axis=1), pick_ref[...])
        front = jnp.zeros((depth, 128), F32)
        rim = front
        beside = front
        for r in range(first, stop):
            part = found[(r - first) * depth : (r - first + 1) * depth]
            row = r + odd * (15 - 2 * r)
            if 4 <= r < 12:
                front = jnp.where(lane128 // NF == row - 4, part[:, 0:128], front)
            elif r == 3:
                rim = jnp.where(lane128 // 64 == odd, part[:, 0:128], rim)
            elif r == 12:
                rim = jnp.where(lane128 // 64 == 1 - odd, part[:, 0:128], rim)
            beside = jnp.where(lane_r == row, part[:, 128:256], beside)
        return jnp.where(z_ok, front, 0.0), jnp.where(edge_ok, rim, 0.0), beside

    def front_step(field, rim, c):
        upper_y = jnp.where(lane128 >= 112, rim, pltpu.roll(field, 112, 1))
        lower_y = jnp.where(lane128 < 16, rim, pltpu.roll(field, 16, 1))
        behind = jnp.where((lane128 & 15) == 0, field, pltpu.roll(field, 1, 1))
        return advance(field, upper_y, lower_y, behind, c)[0]

    def side_step(field, c):
        return advance(field, pltpu.roll(field, 120, 1), pltpu.roll(field, 8, 1), pltpu.roll(field, 1, 1), c)

    def side_back(value, c, scale, slope_y, slope_z):
        a = value * scale
        b = value * slope_y
        d = value * slope_z
        total = value * ((1.0 - COURANT) - FORCE_GAIN * (c * c)) - 4.0 * a
        total = total + COURANT * pltpu.roll(value, 127, 1)
        total = total + pltpu.roll(a + b, 8, 1) + pltpu.roll(a - b, 120, 1)
        return total + pltpu.roll(a + d, 1, 0) + pltpu.roll(a - d, depth - 1, 0)

    front0, rim0, beside0 = inlets(vw1, 1, 15)
    front1, rim1, beside1 = inlets(vw2, 2, 14)
    cf0, cs0, cf1, cs1 = (cp_ref[k] for k in range(4))

    uf1 = front_step(front0, rim0, cf0)
    uf2 = front_step(front1, rim1, cf1)
    tf0 = yaw_term(cf0, front0, power_slope(cf0, uf1), uf1)
    tf1 = yaw_term(cf1, front1, power_slope(cf1, uf2), uf2)

    ws0 = jnp.where(side_ok, jnp.where(lane_k == 1, beside0, side_ref[...]), 0.0)
    us1, *back0 = side_step(ws0, cs0)
    ws1 = jnp.where(side_ok, jnp.where(lane_k == 1, beside1, us1), 0.0)
    us2, *back1 = side_step(ws1, cs1)
    value2 = power_slope(cs1, us2)
    value1 = jnp.where(side_ok, side_back(value2, cs1, *back1) + power_slope(cs0, us1), 0.0)
    ts0 = yaw_term(cs0, ws0, value1, us1)
    ts1 = yaw_term(cs1, ws1, value2, us2)

    terms = jnp.concatenate([tf0, ts0, tf1, ts1], axis=1)[0:zd]
    hi, lo = split2(terms)
    z_own = lax.rem(turned[0][:, 0:1] // fx, zd)
    take_z = (z_own == lax.broadcasted_iota(jnp.int32, (count, zd), 1)).astype(F32).astype(BF16)
    lines = dot(take_z, lo) + dot(take_z, hi)
    in_front = slots[0][0]
    beside = jnp.where((along[0] >= 16) & (along[0] < 18), slots[0][1], -1)
    total_a[g * m + p] = jnp.zeros(total_a.shape[1:], F32)
    mine = total_a.at[g * m + p]
    for s in range(2):
        value = part_ref[s] + jnp.where(in_front == lane128, lines[:, s * 256 : s * 256 + 128], 0.0)
        value = value + jnp.where(beside == lane128, lines[:, s * 256 + 128 : s * 256 + 256], 0.0)
        value = jnp.sum(value, axis=1, keepdims=True) * at_turbine(0, sine[s : s + 1])
        mine[s : s + 1, 0:TURB] = jnp.sum(
            jnp.where(turned[0][:, 1:2] == lane_t, value, 0.0), axis=0, keepdims=True
        )

    def near_copy(d):
        return pltpu.make_async_remote_copy(
            src_ref=total_a.at[g * m + p], dst_ref=total_a.at[g * m + p],
            send_sem=a_send, recv_sem=a_recv, device_id=peer(d), device_id_type=MESH,
        )

    def line_copy(d):
        return pltpu.make_async_remote_copy(
            src_ref=total_b.at[scen], dst_ref=total_b.at[scen],
            send_sem=b_send.at[d], recv_sem=b_recv.at[d], device_id=line(d), device_id_type=MESH,
        )

    def start(make):
        def run(d, carry):
            make(d).start()
            return carry

        return run

    def wait(make):
        def run(d, carry):
            make(d).wait()
            return carry

        return run

    lax.fori_loop(1, n * m, start(near_copy), 0)

    for r in range(3, 13):
        spread_terms(0, r)
    for r in range(4, rows + 4):
        sens_ref[r - 4] = backward(0, r, c0)[0:zd]

    ss = side_back(value1, cs0, *back0)

    us2, ss, uf2 = us2[0:zd], ss[0:zd], uf2[0:zd]
    for r in range(rows):
        shift = (-18 - 8 * r) % 128
        farm_ref[r, :, 0:128] = jnp.where(
            lane128 < NF, pltpu.roll(uf2, (-NF * r) % 128, 1),
            jnp.where(lane128 < 18, pltpu.roll(us2, shift, 1), farm_ref[r, :, 0:128]),
        )
        sens_ref[r, :, 0:128] = jnp.where(
            lane128 < NF, 0.0,
            jnp.where(lane128 < 18, pltpu.roll(ss, shift, 1), sens_ref[r, :, 0:128]),
        )

    for i in (5, 6, 8, 9):
        copies[i].wait()

    for i in range(1, planes + 3):
        v1[i] = periodic_row(vp_ref, i, True)
    for i in range(2, planes + 2):
        prec_ref[i - 2] = periodic_row(v1, i, True)[0:zd]

    whole_far.wait_send()
    whole_rim.wait_send()
    whole_sum.wait()
    total_b[scen] = jnp.sum(total_a[...], axis=0)
    lax.fori_loop(1, ns, start(line_copy), 0)
    lax.fori_loop(1, ns, wait(line_copy), 0)
    grad_ref[...] = jnp.sum(total_b[...], axis=0)[0 : grad_ref.shape[0], 0 : grad_ref.shape[1]]


def farm_steps(sizes, v, u, index, turbine, yaw, ps):
    planes, zd, fy = v.shape
    rows, _, fx = u.shape
    ns, n, m = sizes
    px = n * planes
    depth = zd + 8
    farm = pltpu.VMEM((16, depth, fx), F32)
    dma = pltpu.SemaphoreType.DMA
    return pl.pallas_call(
        functools.partial(farm_kernel, sizes),
        out_shape=(
            pltpu.VMEM(v.shape, F32),
            pltpu.VMEM(u.shape, F32),
            pltpu.VMEM(u.shape, F32),
            pltpu.VMEM(yaw.shape, F32),
        ),
        in_specs=[HBM] * 5 + [SMEM],
        out_specs=(VMEM,) * 4,
        scratch_shapes=[
            farm,
            pltpu.VMEM((planes + 4, depth, fy), F32),
            pltpu.VMEM((16, depth, px), F32),
            pltpu.VMEM((6, 8, index.shape[1]), jnp.int32),
            pltpu.VMEM(v.shape, F32),
            pltpu.VMEM(u.shape, F32),
            pltpu.VMEM((8, index.shape[1]), jnp.int32),
            pltpu.VMEM(index.shape, jnp.int32),
            pltpu.VMEM(turbine.shape, jnp.int32),
            pltpu.VMEM(yaw.shape, F32),
            dma((5,)),
            pltpu.VMEM((planes, 8, fy), F32),
            pltpu.VMEM((rows, 8, fx), F32),
            pltpu.VMEM((fy + 8, planes, 2 * zd), F32),
            pltpu.VMEM((6, px, 2 * zd), F32),
            pltpu.VMEM((n, planes, 128), F32),
            pltpu.VMEM((px, 128), F32),
            pltpu.VMEM((planes + 4, depth, fy), F32),
            pltpu.VMEM((16, depth, px), F32),
            pltpu.VMEM((16, depth, px), F32),
            farm, farm, farm, farm, farm, farm, farm,
            pltpu.VMEM((2, 16, depth, fx), F32),
            pltpu.VMEM((2, 16, depth, fx), F32),
            pltpu.VMEM((2, 16, depth, fx), F32),
            farm, farm,
            pltpu.VMEM(u.shape, F32),
            pltpu.VMEM(u.shape, F32),
            pltpu.VMEM((n * m, 2, 128), F32),
            pltpu.VMEM((ns, 2, 128), F32),
            pltpu.VMEM((2 * px, 256), BF16),
            pltpu.VMEM((4, depth, 128), F32),
            pltpu.VMEM((depth, 128), F32),
            pltpu.VMEM((2, index.shape[1], 128), F32),
            dma((15,)), dma((15,)), dma, dma, dma, dma, dma, dma,
            dma, dma, dma((ns,)), dma((ns,)),
        ],
        compiler_params=pltpu.CompilerParams(
            collective_id=0, has_side_effects=True, vmem_limit_bytes=56 * 1024 * 1024
        ),
        name="farm_steps",
    )(v, u, index, turbine, yaw, ps)


def finish_kernel(*refs):
    count = (len(refs) - 1) // 2
    sem = refs[-1]
    copies = [pltpu.make_async_copy(refs[i], refs[count + i], sem.at[i]) for i in range(count)]
    for copy in copies:
        copy.start()
    for copy in copies:
        copy.wait()


def finish(*arrays):
    return pl.pallas_call(
        finish_kernel,
        out_shape=tuple(jax.ShapeDtypeStruct(x.shape, F32) for x in arrays),
        in_specs=[VMEM] * len(arrays),
        out_specs=(HBM,) * len(arrays),
        scratch_shapes=[pltpu.SemaphoreType.DMA((len(arrays),))],
        name="finish",
    )(*[pltpu.with_memory_space_constraint(x, pltpu.VMEM) for x in arrays])


def shards(sizes, prec_state, farm_state, yaw_angles, plane_source, cell_index, cell_turbine):
    prec, farm, sens, yaw_grad = farm_steps(
        sizes, prec_state[0], farm_state[0], cell_index[0], cell_turbine[0], yaw_angles,
        plane_source,
    )
    prec, farm, sens, yaw_grad = finish(prec, farm, sens, yaw_grad)
    return (prec[None], farm[None], sens[None], yaw_grad)


def solution(mesh):
    spec = P("scen", "grp", "pen", None)
    in_specs = (spec, spec, P(), P(), P("grp", "pen", None), P("grp", "pen", None))
    out_specs = (spec, spec, spec, P())
    sizes = tuple(mesh.shape[axis] for axis in ("scen", "grp", "pen"))
    return jax.shard_map(
        functools.partial(shards, sizes), mesh=mesh, in_specs=in_specs, out_specs=out_specs,
        check_vma=False,
    )
```
